32 devices in a mesh: wide: 8 (over y, x, core), narrow: 4 (over z).
Axes of the slice: x: 2, y: 2, z: 4, core: 2. Of those that a mesh axis runs over, the one named last changes fastest.
Arguments:
- inputs: bfloat16 [64, 1024, 512], P('wide', 'narrow'), may hold values from -6 to 6
- positions: int32 [64, 1024], P('wide'), may hold values from 0 to 1023, as said below
- members_index: int32 [1024, 2, 56], P('narrow'), may hold values from 0 to 63, as said below
- members_mask: int32 [1024, 2, 56], P('narrow'), may hold values from 0 to 1, as said below
- gain_attn: float32 [512], replicated, may hold values from 0.5 to 1.5
- input_projection_weight: bfloat16 [512, 3, 512], P(None, None, 'narrow'), may hold values from -0.25 to 0.25
- output_projection_weight: bfloat16 [512, 512], P('narrow'), may hold values from -2 to 2
- gain_mixer: float32 [512], replicated, may hold values from 0.5 to 1.5
- weight_router: bfloat16 [512, 8], replicated, may hold values from -0.1875 to 0.1875
- weight_up: bfloat16 [8, 512, 2048], P(None, None, 'narrow'), may hold values from -1 to 1
- weight_down: bfloat16 [8, 2048, 512], P(None, 'narrow'), may hold values from -3 to 3
- cotangent: bfloat16 [64, 1024, 512], P('wide', 'narrow'), may hold values from -6 to 6
Outputs:
- outputs: bfloat16 [64, 1024, 512], P('wide', 'narrow')
- grad_inputs: float32 [64, 1024, 512], P('wide', 'narrow')
- grad_gain_attn: float32 [512], replicated
- grad_inproj: float32 [512, 3, 512], P(None, None, 'narrow')
- grad_outproj: float32 [512, 512], P('narrow')
- grad_gain_mixer: float32 [512], replicated
- grad_router: float32 [512, 8], replicated
- grad_up: float32 [8, 512, 2048], P(None, None, 'narrow')
- grad_down: float32 [8, 2048, 512], P(None, 'narrow')
The draws below stay inside these ranges and needn't reach their ends.
Inputs may be any that keep to these rules, and one draw needn't show every extreme that they name: `positions`: 0 at a document's first token and one more at each next token; in each block of 8 sequences in a row one sequence, drawn from the seed, holds exactly two documents, the second of which begins between token 896 and token 1023. `members_index`: at each position the live slots of its 2 groups name every sequence exactly once. `members_mask`: each group's row is 1 on its first 8 to 56 slots and 0 after; at each position one group has all 56 slots live.
All inputs are finite; a program needn't handle non-finite values.
Results may differ from the reference program's by a relative error of at most 0.034.
Values may be sent and summed in bfloat16 or wider, within the bound.
A program may use at most 320 MiB of HBM per device.

```python
import jax
import jax.numpy as jnp
from jax import lax

D = 512
HEADS = 8
HEAD_DIM = 64
HIDDEN_SIZE = 2048
EXPERTS = 8
LEN = 1024
GMIN = 8
SEQ_DEV = 8
SEQS = 64
GROUPS = 2
GCAP = 56


def group_table(key):
    split_keys = jax.random.split(jax.random.fold_in(key, 11), LEN)

    def shuffle_one(item_key):
        return jax.random.permutation(item_key, SEQS)
    orders = jax.vmap(shuffle_one)(split_keys)
    full_column = jnp.full((LEN, 1), GCAP, jnp.int32)
    others_count = GROUPS - 1
    remaining = SEQS - GCAP
    base_count = remaining // others_count
    spare_count = remaining % others_count
    others = base_count + (jnp.arange(others_count, dtype=jnp.int32) < spare_count).astype(jnp.int32)
    others = jnp.broadcast_to(others[None, :], (LEN, others_count))
    reach = max(0, min(base_count - GMIN, GCAP - 1 - base_count))
    pair_count = others_count // 2
    if pair_count > 0:
        shifts = jax.random.randint(jax.random.fold_in(key, 12), (LEN, pair_count), -reach, reach + 1)
        paired = jnp.stack([shifts, -shifts], axis=-1).reshape(LEN, 2 * pair_count)
        if others_count > 2 * pair_count:
            paired = jnp.concatenate([paired, jnp.zeros((LEN, 1), jnp.int32)], axis=1)
        others = others + paired.astype(jnp.int32)
    counts = jnp.concatenate([full_column, others.astype(jnp.int32)], axis=1)
    rolls = jax.random.randint(jax.random.fold_in(key, 13), (LEN, 1), 0, GROUPS)
    order_index = (jnp.arange(GROUPS, dtype=jnp.int32)[None, :] - rolls) % GROUPS
    counts = jnp.take_along_axis(counts, order_index, axis=1)
    starts = jnp.cumsum(counts, axis=1) - counts
    slot_index = jnp.arange(GCAP, dtype=jnp.int32)
    live = slot_index[None, None, :] < counts[:, :, None]
    where_at = jnp.where(live, starts[:, :, None] + slot_index[None, None, :], 0)
    index_table = jnp.take_along_axis(orders, where_at.reshape(LEN, GROUPS * GCAP), axis=1).reshape(LEN, GROUPS, GCAP)
    return (index_table.astype(jnp.int32), live.astype(jnp.int32))


def draw_members_index(key, part):
    table = group_table(key)
    return table[0]


def draw_members_mask(key, part):
    table = group_table(key)
    return table[1]


def draw_positions(key, part):
    key = jax.random.fold_in(key, 5)
    marks = jax.random.randint(jax.random.fold_in(key, 1), (SEQS, LEN), 0, 192) == 0
    chosen = jax.random.randint(jax.random.fold_in(key, 2), (SEQS // SEQ_DEV,), 0, SEQ_DEV)
    single = jnp.arange(SEQS) % SEQ_DEV == jnp.repeat(chosen, SEQ_DEV, total_repeat_length=SEQS)
    border = jax.random.randint(jax.random.fold_in(key, 3), (SEQS, 1), LEN - LEN // 8, LEN)
    steps_index = jnp.arange(LEN, dtype=jnp.int32)
    chosen_marks = steps_index[None, :] == border
    marks = jnp.where(single[:, None], chosen_marks, marks) | (steps_index[None, :] == 0)
    starts = lax.cummax(jnp.where(marks, steps_index[None, :], 0), axis=1)
    return (steps_index[None, :] - starts).astype(jnp.int32)


def levels(key, shape, cuts, smallest, top_value):
    loudness, own = 1.0, jax.random.fold_in(key, 6)
    for position, blocks in cuts:
        steps = jnp.exp(jax.random.uniform(jax.random.fold_in(own, position), (blocks,), jnp.float32, smallest / len(cuts), top_value / len(cuts)))
        loudness = loudness * jnp.repeat(steps, shape[position] // blocks).reshape([-1 if axis == position else 1 for axis in range(len(shape))])
    return loudness


def bell_draw(key, dims, deviation, bound, pieces=(), kind=jnp.bfloat16):
    array = jax.random.normal(key, dims, jnp.float32) * deviation
    if len(pieces) > 0:
        array = levels(key, dims, pieces, -0.22, 0.18) * array
    return jnp.clip(array, min=-bound, max=bound).astype(kind)


def setup_inputs(seed: int = 0) -> dict:
    streams_of = jax.random.split(jax.random.key(seed), 13)
    inputs = bell_draw(streams_of[0], (SEQS, LEN, D), 1.0, 6.0, ((0, 8), (1, 4)))
    positions = draw_positions(jax.random.fold_in(streams_of[12], 71), 0)
    members_index = draw_members_index(jax.random.fold_in(streams_of[12], 71), 0)
    members_mask = draw_members_mask(jax.random.fold_in(streams_of[12], 71), 0)
    gain_attn = jnp.clip(1.0 + 0.1 * jax.random.normal(streams_of[4], (D,), jnp.float32), 0.5, 1.5)
    input_projection_weight = bell_draw(streams_of[5], (D, 3, D), D ** -0.5, 0.25, ((2, 4),))
    output_projection_weight = bell_draw(streams_of[6], (D, D), (max(D // 64, 1)) ** -0.5, 2.0, ((0, 4),))
    gain_mixer = jnp.clip(1.0 + 0.1 * jax.random.normal(streams_of[7], (D,), jnp.float32), 0.5, 1.5)
    weight_router = bell_draw(streams_of[8], (D, EXPERTS), (2 * D) ** -0.5, 0.1875)
    weight_up = bell_draw(streams_of[9], (EXPERTS, D, HIDDEN_SIZE), (max(D // 16, 1)) ** -0.5, 1.0, ((2, 4),))
    weight_down = bell_draw(streams_of[10], (EXPERTS, HIDDEN_SIZE, D), (max(HIDDEN_SIZE // 512, 1)) ** -0.5, 3.0, ((1, 4),))
    cotangent = bell_draw(streams_of[11], (SEQS, LEN, D), 1.0, 6.0, ((0, 8), (1, 4)))
    return {"inputs": inputs, "positions": positions, "members_index": members_index, "members_mask": members_mask, "gain_attn": gain_attn, "input_projection_weight": input_projection_weight, "output_projection_weight": output_projection_weight, "gain_mixer": gain_mixer, "weight_router": weight_router, "weight_up": weight_up, "weight_down": weight_down, "cotangent": cotangent}


@jax.custom_vjp
def low(v):
    return lax.optimization_barrier(v.astype(jnp.bfloat16)).astype(jnp.float32)

@jax.custom_vjp
def low_back(v):
    return v

def low_keep(v):
    return (low(v), None)

def low_pass(kept, grad):
    return (grad,)

def back_keep(v):
    return (v, None)

def back_low(kept, grad):
    return (low(grad),)
low.defvjp(low_keep, low_pass)
low_back.defvjp(back_keep, back_low)
epsilon = 1e-06
highest = lax.Precision.HIGHEST

def normalize(values, gain):
    return values * lax.rsqrt(lax.optimization_barrier(jnp.mean(values * values, axis=-1, keepdims=True)) + epsilon) * gain

def reference(inputs, positions, members_index, members_mask, gain_attn, input_projection_weight, output_projection_weight, gain_mixer, weight_router, weight_up, weight_down, cotangent):
    live_slots = members_mask > 0
    selector = ((members_index[..., None] == jnp.arange(SEQS, dtype=jnp.int32)[None, None, None, :]) & live_slots[..., None]).astype(jnp.float32)
    key_order = jnp.arange(LEN, dtype=jnp.int32)
    distance = key_order[:, None] - key_order[None, :]

    def forward(inputs_f, gain_one, inproj, outproj, gain_two, router_w, up_w, down_w):

        def attend_one(pair):
            sequence, position_row = pair
            proj = jnp.einsum('ld,dcf->lcf', sequence, inproj, precision=highest)
            queries = low(low_back(proj[:, 0])).reshape(LEN, HEADS, HEAD_DIM)
            keys_all = low(low_back(proj[:, 1])).reshape(LEN, HEADS, HEAD_DIM)
            values_all = low(low_back(proj[:, 2])).reshape(LEN, HEADS, HEAD_DIM)
            raw_scores = low_back(jnp.einsum('qhd,khd->hqk', queries, keys_all, precision=highest) * HEAD_DIM ** (-0.5))
            allowed = (distance >= 0) & (distance <= position_row[:, None])
            raw_scores = jnp.where(allowed[None], raw_scores, -1e+30)
            probabilities = low(jax.nn.softmax(raw_scores, axis=-1))
            attention_result = jnp.einsum('hqk,khd->qhd', probabilities, values_all, precision=highest).reshape(LEN, D)
            attention_result = low(low_back(attention_result))
            return jnp.dot(attention_result, outproj, precision=highest)
        normed_one = low(low_back(normalize(inputs_f, gain_one)))
        attn_out = low_back(lax.map(jax.checkpoint(attend_one), (normed_one, positions)))
        hidden_one = inputs_f + attn_out
        normed_two = low(low_back(normalize(hidden_one, gain_two)))
        members = jnp.einsum('pgjs,spd->pgjd', selector, normed_two, precision=highest)
        logits = low_back(jnp.einsum('pgjd,de->pgje', members, router_w, precision=highest))
        logits = jnp.where(live_slots[..., None], logits, -1e+30)
        weights = low(jax.nn.softmax(logits, axis=2))
        mixed_tokens = low(low_back(jnp.einsum('pgje,pgjd->pged', weights, members, precision=highest)))
        pre_act = low_back(jnp.einsum('pged,edf->pgef', mixed_tokens, up_w, precision=highest))
        act_low = low(jax.nn.gelu(pre_act))
        expert_out = low_back(jnp.einsum('pgef,efd->pged', act_low, down_w, precision=highest))
        member_out = low(jnp.einsum('pgje,pged->pgjd', weights, expert_out, precision=highest))
        return hidden_one + jnp.einsum('pgjs,pgjd->spd', selector, member_out, precision=highest)
    primals = (inputs.astype(jnp.float32), gain_attn.astype(jnp.float32), input_projection_weight.astype(jnp.float32), output_projection_weight.astype(jnp.float32), gain_mixer.astype(jnp.float32), weight_router.astype(jnp.float32), weight_up.astype(jnp.float32), weight_down.astype(jnp.float32))
    result, backward = jax.vjp(forward, *primals)
    grads = backward(cotangent.astype(jnp.float32))
    return (result.astype(jnp.bfloat16), grads[0], grads[1], grads[2], grads[3], grads[4], grads[5], grads[6], grads[7])
```

```python
import functools

import jax
import jax.numpy as jnp
from jax import lax
from jax.experimental import pallas as pl
from jax.experimental.pallas import tpu as pltpu
from jax.sharding import PartitionSpec as P

MESH = pl.DeviceIdType.MESH
HEAD_DIM = 64
PAIR = 2 * HEAD_DIM
EPS = 1e-06
NEG = -1e30
bf16 = jnp.bfloat16
f32 = jnp.float32
VMEM_LIMIT = 56 << 20


def nn(a, b):
    return lax.dot_general(a, b, (((1,), (0,)), ((), ())), preferred_element_type=f32)


def nt(a, b):
    return lax.dot_general(a, b, (((1,), (1,)), ((), ())), preferred_element_type=f32)


def tn(a, b):
    return lax.dot_general(a, b, (((0,), (0,)), ((), ())), preferred_element_type=f32)


def whole(memory=pltpu.VMEM):
    return pl.BlockSpec(memory_space=memory)


def peers(kind, narrow, wide, cluster):
    w, z = lax.axis_index("wide"), lax.axis_index("narrow")
    if kind == "narrow":
        return z, narrow, lambda j: (w, j)
    if kind == "wide":
        return w, wide, lambda j: (j, z)
    if kind == "cluster":
        first = (w // cluster) * cluster
        return w - first, cluster, lambda j: (first + j, z)
    return w * narrow + z, wide * narrow, lambda j: (j // narrow, lax.rem(j, narrow))


def exchange_body(plans, sizes, *refs):
    count = len(plans)
    sources, targets, sems = refs[:count], refs[count : 2 * count], refs[2 * count :]
    barrier = pltpu.get_barrier_semaphore()
    groups = [peers(kind, *sizes) for kind, _, _, _ in plans]
    greeted = 0
    for kind in dict.fromkeys(kind for kind, _, _, _ in plans):
        me, total, place = peers(kind, *sizes)

        def greet(k, carry, me=me, total=total, place=place):
            pl.semaphore_signal(
                barrier, inc=1, device_id=place(lax.rem(me + k, total)), device_id_type=MESH
            )
            return carry

        lax.fori_loop(1, total, greet, 0)
        greeted += total - 1
    pl.semaphore_wait(barrier, greeted)

    def copy_of(i, k):
        (me, total, place), (_, source_at, target_at, _) = groups[i], plans[i]
        j = lax.rem(me + k, total)
        return pltpu.make_async_remote_copy(
            src_ref=source_at(sources[i], j),
            dst_ref=target_at(targets[i], me),
            send_sem=sems[3 * i].at[k],
            recv_sem=sems[3 * i + 1].at[k],
            device_id=place(j),
            device_id_type=MESH,
        )

    def own_of(i):
        me = groups[i][0]
        return pltpu.make_async_copy(
            plans[i][1](sources[i], me), plans[i][2](targets[i], me), sems[3 * i + 2]
        )

    for i in range(count):

        def begin(k, carry, i=i):
            copy_of(i, k).start()
            return carry

        lax.fori_loop(1, groups[i][1], begin, 0)
        own_of(i).start()
    for i in range(count):

        def finish(k, carry, i=i):
            copy_of(i, k).wait()
            return carry

        lax.fori_loop(1, groups[i][1], finish, 0)
        own_of(i).wait()


def exchange(plans, arrays, sizes, number):
    scratch = []
    for kind, _, _, _ in plans:
        total = {"narrow": sizes[0], "wide": sizes[1], "cluster": sizes[2]}.get(
            kind, sizes[0] * sizes[1]
        )
        scratch += [pltpu.SemaphoreType.DMA((total,))] * 2 + [pltpu.SemaphoreType.DMA]
    return pl.pallas_call(
        functools.partial(exchange_body, plans, sizes),
        out_shape=[jax.ShapeDtypeStruct(p[3], a.dtype) for p, a in zip(plans, arrays)],
        in_specs=[whole(pl.ANY)] * len(plans),
        out_specs=[whole(pl.ANY)] * len(plans),
        scratch_shapes=scratch,
        compiler_params=pltpu.CompilerParams(collective_id=number, has_side_effects=True),
    )(*arrays)


def rows_of(first, count, size):
    return pl.ds(pl.multiple_of(first * size, size), count * size)


def unit_of(values):
    scaling = lax.rsqrt(jnp.mean(values * values, axis=-1, keepdims=True) + EPS)
    return values * scaling, scaling


def unit_back(grad_rows, unit_rows, scaling, gain):
    grad_unit = grad_rows * gain
    inner = jnp.mean(grad_unit * unit_rows, axis=-1, keepdims=True)
    return scaling * (grad_unit - unit_rows * inner)


def attend_body(block, x_ref, start_ref, gain_ref, wall_ref, qkv_ref, att_ref, hid_ref, lse_ref, lse_acc):
    seqs, length, _ = x_ref.shape
    pairs = wall_ref.shape[0]
    lane = lax.broadcasted_iota(jnp.int32, (block, PAIR), 1)
    for s in range(seqs):
        values = x_ref[s].astype(f32)
        normed = (unit_of(values)[0] * gain_ref[...]).astype(bf16)

        def one_pair(n, carry):
            proj = nn(normed, wall_ref[n, :, : 3 * PAIR]).astype(bf16)
            qkv_ref[s, n] = proj
            keys, vals = proj[:, PAIR : 2 * PAIR], proj[:, 2 * PAIR :]
            for i in range(length // block):
                rows = slice(i * block, (i + 1) * block)
                end = (i + 1) * block
                query = proj[rows, :PAIR] * jnp.asarray(HEAD_DIM**-0.5, bf16)
                key_at = lax.broadcasted_iota(jnp.int32, (block, end), 1)
                row_at = i * block + lax.broadcasted_iota(jnp.int32, (block, end), 0)
                allowed = (key_at >= start_ref[s, rows, :]) & (key_at <= row_at)
                got = []
                for j in range(2):
                    own = (lane // HEAD_DIM) == j
                    score = nt(jnp.where(own, query, jnp.zeros_like(query)), keys[:end])
                    score = jnp.where(allowed, score, NEG)
                    peak = jnp.max(score, axis=1, keepdims=True)
                    expo = jnp.exp(score - peak)
                    total = jnp.sum(expo, axis=1, keepdims=True)
                    got.append(nn(expo.astype(bf16), vals[:end]) / total)
                    lse_acc[rows, :] = jnp.where(
                        lane == 2 * n + j, peak + jnp.log(total), lse_acc[rows, :]
                    )
                att_ref[s, n, rows, :] = jnp.where(lane < HEAD_DIM, got[0], got[1]).astype(bf16)
            return carry

        lax.fori_loop(0, pairs, one_pair, 0)
        hidden = values
        for n in range(pairs):
            hidden = hidden + nt(att_ref[s, n], wall_ref[n, :, 3 * PAIR :])
        hid_ref[s] = hidden.astype(bf16)
        lse_ref[s] = jnp.transpose(lse_acc[...])[: 2 * pairs]


def attend(x, start_col, gain, wall):
    seqs, length, features = x.shape
    pairs = wall.shape[0]
    return pl.pallas_call(
        functools.partial(attend_body, min(256, length)),
        out_shape=[
            jax.ShapeDtypeStruct((seqs, pairs, length, 3 * PAIR), bf16),
            jax.ShapeDtypeStruct((seqs, pairs, length, PAIR), bf16),
            jax.ShapeDtypeStruct((seqs, length, features), bf16),
            jax.ShapeDtypeStruct((seqs, 2 * pairs, length), f32),
        ],
        in_specs=[whole()] * 4,
        out_specs=[whole()] * 4,
        scratch_shapes=[pltpu.VMEM((length, PAIR), f32)],
        compiler_params=pltpu.CompilerParams(vmem_limit_bytes=VMEM_LIMIT),
    )(x, start_col, gain, wall)


def attend_back_body(
    block,
    x_ref,
    start_ref,
    gain_ref,
    wall_ref,
    qkv_ref,
    att_ref,
    lse_ref,
    dh_ref,
    gx_ref,
    gwall_ref,
    ggain_ref,
    dq_acc,
    dproj_ref,
    gn_acc,
):
    seqs, length, _ = x_ref.shape
    pairs = wall_ref.shape[0]
    lane = lax.broadcasted_iota(jnp.int32, (length, PAIR), 1)
    scale = jnp.asarray(HEAD_DIM**-0.5, bf16)
    for s in range(seqs):
        values = x_ref[s].astype(f32)
        unit, scaling = unit_of(values)
        normed = (unit * gain_ref[...]).astype(bf16)
        gn_acc[...] = jnp.zeros_like(gn_acc)

        def one_pair(n, carry):
            dh = dh_ref[s]
            d_att = nn(dh, wall_ref[n, :, 3 * PAIR :]).astype(bf16)
            att = att_ref[s, n]
            g_out = tn(dh, att)
            prod = (d_att.astype(f32) * att.astype(f32)).astype(bf16)
            head_row = lax.broadcasted_iota(jnp.int32, (8, PAIR), 0)
            head_lane = lax.broadcasted_iota(jnp.int32, (8, PAIR), 1) // HEAD_DIM
            inner = nt((head_row == head_lane).astype(bf16), prod)
            query = qkv_ref[s, n, :, :PAIR] * scale
            keys, vals = qkv_ref[s, n, :, PAIR : 2 * PAIR], qkv_ref[s, n, :, 2 * PAIR :]
            zero = jnp.zeros_like(query)
            own = [(lane // HEAD_DIM) == j for j in range(2)]
            q_own = [jnp.where(o, query, zero) for o in own]
            k_own = [jnp.where(o, keys, zero) for o in own]
            d_own = [jnp.where(o, d_att, zero) for o in own]
            lse = lse_ref[s]
            head_at = lax.broadcasted_iota(jnp.int32, lse.shape, 0)
            lse_own = [
                jnp.sum(jnp.where(head_at == 2 * n + j, lse, 0.0), axis=0, keepdims=True)
                for j in range(2)
            ]
            dq_acc[...] = jnp.zeros_like(dq_acc)
            for i in range(length // block):
                rows, first = slice(i * block, (i + 1) * block), i * block
                shape = (block, length - first)
                key_at = first + lax.broadcasted_iota(jnp.int32, shape, 0)
                row_at = first + lax.broadcasted_iota(jnp.int32, shape, 1)
                allowed = (key_at >= start_ref[s, :, first:]) & (key_at <= row_at)
                dk = dv = None
                for j in range(2):
                    score = nt(keys[rows], q_own[j][first:])
                    prob = jnp.where(allowed, jnp.exp(score - lse_own[j][:, first:]), 0.0)
                    d_prob = nt(vals[rows], d_own[j][first:])
                    d_score = (prob * (d_prob - inner[j : j + 1, first:])).astype(bf16)
                    dv_part = nn(prob.astype(bf16), d_own[j][first:])
                    dk_part = nn(d_score, q_own[j][first:])
                    dv = dv_part if dv is None else dv + dv_part
                    dk = dk_part if dk is None else dk + dk_part
                    dq_acc[first:, :] += tn(d_score, k_own[j][rows])
                dproj_ref[rows, PAIR : 2 * PAIR] = dk.astype(bf16)
                dproj_ref[rows, 2 * PAIR :] = dv.astype(bf16)
            dproj_ref[:, :PAIR] = (dq_acc[...] * HEAD_DIM**-0.5).astype(bf16)
            d_proj = dproj_ref[...]
            gn_acc[...] += nt(d_proj, wall_ref[n, :, : 3 * PAIR])
            g_in = tn(normed, d_proj)
            if s == 0:
                gwall_ref[n, :, : 3 * PAIR] = g_in
                gwall_ref[n, :, 3 * PAIR :] = g_out
            else:
                gwall_ref[n, :, : 3 * PAIR] += g_in
                gwall_ref[n, :, 3 * PAIR :] += g_out
            return carry

        lax.fori_loop(0, pairs, one_pair, 0)
        grad = gn_acc[...]
        g_gain = jnp.sum(grad * unit, axis=0, keepdims=True)
        if s == 0:
            ggain_ref[...] = g_gain
        else:
            ggain_ref[...] += g_gain
        back = unit_back(grad, unit, scaling, gain_ref[...])
        gx_ref[s] = (dh_ref[s].astype(f32) + back).astype(bf16)


def attend_back(x, start_row, gain, wall, qkv, att, lse, dh):
    seqs, length, features = x.shape
    pairs = wall.shape[0]
    return pl.pallas_call(
        functools.partial(attend_back_body, min(256, length)),
        out_shape=[
            jax.ShapeDtypeStruct((seqs, length, features), bf16),
            jax.ShapeDtypeStruct((pairs, features, 4 * PAIR), f32),
            jax.ShapeDtypeStruct((1, features), f32),
        ],
        in_specs=[whole()] * 8,
        out_specs=[whole()] * 3,
        scratch_shapes=[
            pltpu.VMEM((length, PAIR), f32),
            pltpu.VMEM((length, 3 * PAIR), bf16),
            pltpu.VMEM((length, features), f32),
        ],
        compiler_params=pltpu.CompilerParams(vmem_limit_bytes=VMEM_LIMIT),
    )(x, start_row, gain, wall, qkv, att, lse, dh)


def mix_weights(logits, key_row, experts):
    columns = logits.shape[1]
    cells = 64
    spread = jnp.broadcast_to(logits[:, None, :], (experts, cells, columns)).reshape(
        experts * cells, columns
    )
    row = lax.broadcasted_iota(jnp.int32, (experts * cells, columns), 0)
    spread = jnp.where(lax.rem(row, cells) == key_row, spread, NEG)
    expo = jnp.exp(spread - jnp.max(spread, axis=1, keepdims=True))
    return expo / jnp.sum(expo, axis=1, keepdims=True)


def mix_body(x_ref, g_ref, key_ref, gain_ref, router_ref, mixed_ref, gexp_ref, w_ref):
    experts = router_ref.shape[0]
    values = x_ref[...].astype(f32)
    normed = (unit_of(values)[0] * gain_ref[...]).astype(bf16)
    weights = mix_weights(nt(router_ref[...], normed), key_ref[...], experts)
    w_ref[...] = weights
    low = weights.astype(bf16)
    mixed_ref[...] = nn(low, normed).astype(bf16)
    gexp_ref[...] = nn(low, g_ref[...]).astype(bf16)


def mix(x, g, key_row, gain, router):
    rows = router.shape[0] * 64
    tokens, features = x.shape
    return pl.pallas_call(
        mix_body,
        out_shape=[
            jax.ShapeDtypeStruct((rows, features), bf16),
            jax.ShapeDtypeStruct((rows, features), bf16),
            jax.ShapeDtypeStruct((rows, tokens), f32),
        ],
        in_specs=[whole()] * 5,
        out_specs=[whole()] * 3,
        compiler_params=pltpu.CompilerParams(vmem_limit_bytes=VMEM_LIMIT),
    )(x, g, key_row, gain, router)


def expert_body(m_ref, g_ref, up_ref, down_ref, out_ref, gm_ref, gup_ref, gdown_ref):
    parts = up_ref.shape[0]
    rows, grads = m_ref[...], g_ref[...]
    out = gm = None
    for h in range(parts):
        pre = nn(rows, up_ref[h])
        square = pre * pre
        inner = 0.7978845608028654 * (pre + 0.044715 * pre * square)
        tanh = jnp.tanh(inner)
        act = 0.5 * pre * (1.0 + tanh)
        slope = 0.5 * (1.0 + tanh) + 0.5 * pre * (1.0 - tanh * tanh) * (
            0.7978845608028654 * (1.0 + 3 * 0.044715 * square)
        )
        low = act.astype(bf16)
        g_pre = (nt(grads, down_ref[h]) * slope).astype(bf16)
        out_part, gm_part = nn(low, down_ref[h]), nt(g_pre, up_ref[h])
        out = out_part if out is None else out + out_part
        gm = gm_part if gm is None else gm + gm_part
        gup_ref[h] = tn(rows, g_pre).astype(bf16)
        gdown_ref[h] = tn(low, grads).astype(bf16)
    out_ref[...] = out.astype(bf16)
    gm_ref[...] = gm.astype(bf16)


def expert(rows, grads, up, down):
    return pl.pallas_call(
        expert_body,
        out_shape=[jax.ShapeDtypeStruct(a.shape, bf16) for a in (rows, grads, up, down)],
        in_specs=[whole()] * 4,
        out_specs=[whole()] * 4,
        compiler_params=pltpu.CompilerParams(vmem_limit_bytes=VMEM_LIMIT),
    )(rows, grads, up, down)


def mix_back_body(
    x_ref, g_ref, gain_ref, router_ref, w_ref, eo_ref, gm_ref, out_ref, gh_ref, ggain_ref, grouter_ref
):
    experts = router_ref.shape[0]
    values = x_ref[...].astype(f32)
    unit, scaling = unit_of(values)
    normed = (unit * gain_ref[...]).astype(bf16)
    weights = w_ref[...]
    low = weights.astype(bf16)
    low_t = jnp.transpose(low)
    out_ref[...] = (values + nn(low_t, eo_ref[...])).astype(bf16)
    g_weights = nt(eo_ref[...], g_ref[...]) + nt(gm_ref[...], normed)
    inner = jnp.sum(weights * g_weights, axis=1, keepdims=True)
    g_logits = weights * (g_weights - inner)
    columns = g_logits.shape[1]
    g_logits = jnp.sum(g_logits.reshape(experts, 64, columns), axis=1).astype(bf16)
    g_normed = nn(low_t, gm_ref[...]) + tn(g_logits, router_ref[...])
    grouter_ref[...] = nn(g_logits, normed)
    ggain_ref[...] = jnp.sum(g_normed * unit, axis=0, keepdims=True)
    back = unit_back(g_normed, unit, scaling, gain_ref[...])
    gh_ref[...] = (g_ref[...].astype(f32) + back).astype(bf16)


def mix_back(x, g, gain, router, weights, eo, gm):
    return pl.pallas_call(
        mix_back_body,
        out_shape=[
            jax.ShapeDtypeStruct(x.shape, bf16),
            jax.ShapeDtypeStruct(x.shape, bf16),
            jax.ShapeDtypeStruct((1, x.shape[1]), f32),
            jax.ShapeDtypeStruct(router.shape, f32),
        ],
        in_specs=[whole()] * 7,
        out_specs=[whole()] * 4,
        compiler_params=pltpu.CompilerParams(vmem_limit_bytes=VMEM_LIMIT),
    )(x, g, gain, router, weights, eo, gm)


def per_device(
    inputs,
    positions,
    members_index,
    members_mask,
    gain_attn,
    input_projection_weight,
    output_projection_weight,
    gain_mixer,
    weight_router,
    weight_up,
    weight_down,
    cotangent,
):
    narrow, wide = lax.axis_size("narrow"), lax.axis_size("wide")
    w, z = lax.axis_index("wide"), lax.axis_index("narrow")
    seq_dev, local_len, features = inputs.shape
    length = positions.shape[1]
    groups = members_index.shape[1]
    experts = weight_up.shape[0]
    own_seqs = seq_dev // narrow
    pos_dev = local_len // wide
    seq_total = seq_dev * wide
    sizes = (narrow, wide, experts)

    wall = jnp.concatenate(
        [
            input_projection_weight.reshape(features, -1),
            jnp.transpose(output_projection_weight),
        ],
        axis=1,
    )
    wall = lax.all_gather(wall, "narrow", axis=0, tiled=False)
    e = lax.rem(w, experts)
    up_full = lax.all_gather(
        lax.dynamic_index_in_dim(weight_up, e, 0, keepdims=False), "narrow", axis=0, tiled=False
    )
    down_full = lax.all_gather(
        lax.dynamic_index_in_dim(weight_down, e, 0, keepdims=False), "narrow", axis=0, tiled=False
    )

    row_pos = lax.dynamic_slice_in_dim(positions, z * own_seqs, own_seqs, 0)
    starts = jnp.arange(length, dtype=jnp.int32)[None, :] - row_pos
    offset_rows = w * pos_dev
    index_rows = lax.dynamic_slice_in_dim(members_index, offset_rows, pos_dev, 0)
    live = lax.dynamic_slice_in_dim(members_mask, offset_rows, pos_dev, 0) > 0
    named = (
        index_rows[..., None] == jnp.arange(seq_total, dtype=jnp.int32)[None, None, None, :]
    ) & live[..., None]
    group_of = jnp.max(
        jnp.where(named, jnp.arange(groups, dtype=jnp.int32)[None, :, None, None], 0), axis=(1, 2)
    )
    key_row = group_of + groups * jnp.arange(pos_dev, dtype=jnp.int32)[:, None]
    key_row = jnp.transpose(key_row).reshape(1, seq_total * pos_dev)

    gain_one, gain_two = gain_attn.reshape(1, features), gain_mixer.reshape(1, features)
    router = jnp.transpose(weight_router)

    x_seq, g_mix = exchange(
        [
            (
                "narrow",
                lambda r, j: r.at[pl.ds(j * own_seqs, own_seqs)],
                lambda r, j: r.at[:, rows_of(j, 1, local_len)],
                (own_seqs, length, features),
            ),
            (
                "wide",
                lambda r, j: r.at[:, rows_of(j, 1, pos_dev)],
                lambda r, j: r.at[pl.ds(j * seq_dev, seq_dev)],
                (seq_total, pos_dev, features),
            ),
        ],
        [inputs, cotangent],
        sizes,
        1,
    )
    qkv, att, hidden, lse = attend(x_seq, starts[:, :, None], gain_one, wall)
    (x_mix,) = exchange(
        [
            (
                "all",
                lambda r, j: r.at[:, rows_of(lax.rem(j, narrow) * wide + j // narrow, 1, pos_dev)],
                lambda r, j: r.at[pl.ds(j * own_seqs, own_seqs)],
                (seq_total, pos_dev, features),
            )
        ],
        [hidden],
        sizes,
        2,
    )
    x_mix = x_mix.reshape(seq_total * pos_dev, features)
    g_mix = g_mix.reshape(seq_total * pos_dev, features)
    mixed, g_exp, weights = mix(x_mix, g_mix, key_row, gain_two, router)
    cells = pos_dev * groups

    def swap(a, b, number):
        shape = (experts, cells, features)
        plan = ("cluster", lambda r, j: r.at[j], lambda r, j: r.at[j], shape)
        a, b = exchange([plan, plan], [a.reshape(shape), b.reshape(shape)], sizes, number)
        return a.reshape(-1, features), b.reshape(-1, features)

    rows, row_grads = swap(mixed, g_exp, 3)
    eo, gm, g_up, g_down = expert(rows, row_grads, up_full, down_full)
    eo, gm = swap(eo, gm, 4)
    out_mix, gh_mix, g_gain_two, g_router = mix_back(
        x_mix, g_mix, gain_two, router, weights, eo, gm
    )
    dh, outputs = exchange(
        [
            (
                "all",
                lambda r, j: r.at[pl.ds(j * own_seqs, own_seqs)],
                lambda r, j: r.at[:, rows_of(lax.rem(j, narrow) * wide + j // narrow, 1, pos_dev)],
                (own_seqs, length, features),
            ),
            (
                "wide",
                lambda r, j: r.at[pl.ds(j * seq_dev, seq_dev)],
                lambda r, j: r.at[:, rows_of(j, 1, pos_dev)],
                inputs.shape,
            ),
        ],
        [
            gh_mix.reshape(seq_total, pos_dev, features),
            out_mix.reshape(seq_total, pos_dev, features),
        ],
        sizes,
        5,
    )
    gx, g_wall, g_gain_one = attend_back(
        x_seq, starts[:, None, :], gain_one, wall, qkv, att, lse, dh
    )
    (gx,) = exchange(
        [
            (
                "narrow",
                lambda r, j: r.at[:, rows_of(j, 1, local_len)],
                lambda r, j: r.at[pl.ds(j * own_seqs, own_seqs)],
                inputs.shape,
            )
        ],
        [gx],
        sizes,
        6,
    )
    grad_inputs = gx.astype(f32)

    def expert_grad(part):
        part = lax.psum_scatter(part, "narrow", scatter_dimension=0, tiled=False)
        part = lax.all_gather(part, "wide", axis=0, tiled=False)
        return jnp.sum(
            part.reshape((wide // experts, experts) + part.shape[1:]).astype(f32), axis=0
        )

    grad_up, grad_down = expert_grad(g_up), expert_grad(g_down)
    g_wall = lax.psum_scatter(g_wall.astype(bf16), "narrow", scatter_dimension=0, tiled=False)
    g_wall = lax.psum(g_wall, "wide").astype(f32)
    g_inproj = g_wall[:, : 3 * PAIR].reshape(input_projection_weight.shape)
    g_outproj = jnp.transpose(g_wall[:, 3 * PAIR :])
    g_gain_one, g_gain_two, g_router = lax.psum(
        (g_gain_one, g_gain_two, g_router), ("wide", "narrow")
    )
    return (
        outputs,
        grad_inputs,
        g_gain_one.reshape(features),
        g_inproj,
        g_outproj,
        g_gain_two.reshape(features),
        jnp.transpose(g_router),
        grad_up,
        grad_down,
    )


def solution(mesh):
    in_specs = (
        P("wide", "narrow", None),
        P("wide", None),
        P("narrow", None, None),
        P("narrow", None, None),
        P(),
        P(None, None, "narrow"),
        P("narrow", None),
        P(),
        P(),
        P(None, None, "narrow"),
        P(None, "narrow", None),
        P("wide", "narrow", None),
    )
    out_specs = (
        P("wide", "narrow", None),
        P("wide", "narrow", None),
        P(),
        P(None, None, "narrow"),
        P("narrow", None),
        P(),
        P(),
        P(None, None, "narrow"),
        P(None, "narrow", None),
    )
    return jax.shard_map(
        per_device, mesh=mesh, in_specs=in_specs, out_specs=out_specs, check_vma=False
    )
```

```python
import functools

import jax
import jax.numpy as jnp
from jax import lax
from jax.experimental import pallas as pl
from jax.experimental.pallas import tpu as pltpu
from jax.sharding import PartitionSpec as P

MESH = pl.DeviceIdType.MESH
HEAD_DIM = 64
PAIR = 2 * HEAD_DIM
EPS = 1e-06
NEG = -1e30
bf16 = jnp.bfloat16
f32 = jnp.float32
VMEM_LIMIT = 56 << 20


def nn(a, b):
    return lax.dot_general(a, b, (((1,), (0,)), ((), ())), preferred_element_type=f32)


def nt(a, b):
    return lax.dot_general(a, b, (((1,), (1,)), ((), ())), preferred_element_type=f32)


def tn(a, b):
    return lax.dot_general(a, b, (((0,), (0,)), ((), ())), preferred_element_type=f32)


def whole(memory=pltpu.VMEM):
    return pl.BlockSpec(memory_space=memory)


def peers(kind, narrow, wide, cluster):
    w, z = lax.axis_index("wide"), lax.axis_index("narrow")
    if kind == "narrow":
        return z, narrow, lambda j: (w, j)
    if kind == "wide":
        return w, wide, lambda j: (j, z)
    if kind == "cluster":
        first = (w // cluster) * cluster
        return w - first, cluster, lambda j: (first + j, z)
    return w * narrow + z, wide * narrow, lambda j: (j // narrow, lax.rem(j, narrow))


def exchange_body(plans, sizes, *refs):
    count = len(plans)
    sources, targets, sems = refs[:count], refs[count : 2 * count], refs[2 * count :]
    barrier = pltpu.get_barrier_semaphore()
    groups = [peers(kind, *sizes) for kind, _, _, _ in plans]
    greeted = 0
    for kind in dict.fromkeys(kind for kind, _, _, _ in plans):
        me, total, place = peers(kind, *sizes)

        def greet(k, carry, me=me, total=total, place=place):
            pl.semaphore_signal(
                barrier, inc=1, device_id=place(lax.rem(me + k, total)), device_id_type=MESH
            )
            return carry

        lax.fori_loop(1, total, greet, 0)
        greeted += total - 1
    pl.semaphore_wait(barrier, greeted)

    def copy_of(i, k):
        (me, total, place), (_, source_at, target_at, _) = groups[i], plans[i]
        j = lax.rem(me + k, total)
        return pltpu.make_async_remote_copy(
            src_ref=source_at(sources[i], j),
            dst_ref=target_at(targets[i], me),
            send_sem=sems[3 * i].at[k],
            recv_sem=sems[3 * i + 1].at[k],
            device_id=place(j),
            device_id_type=MESH,
        )

    def own_of(i):
        me = groups[i][0]
        return pltpu.make_async_copy(
            plans[i][1](sources[i], me), plans[i][2](targets[i], me), sems[3 * i + 2]
        )

    for i in range(count):

        def begin(k, carry, i=i):
            copy_of(i, k).start()
            return carry

        lax.fori_loop(1, groups[i][1], begin, 0)
        own_of(i).start()
    for i in range(count):

        def finish(k, carry, i=i):
            copy_of(i, k).wait()
            return carry

        lax.fori_loop(1, groups[i][1], finish, 0)
        own_of(i).wait()


def exchange(plans, arrays, sizes, number):
    scratch = []
    for kind, _, _, _ in plans:
        total = {"narrow": sizes[0], "wide": sizes[1], "cluster": sizes[2]}.get(
            kind, sizes[0] * sizes[1]
        )
        scratch += [pltpu.SemaphoreType.DMA((total,))] * 2 + [pltpu.SemaphoreType.DMA]
    return pl.pallas_call(
        functools.partial(exchange_body, plans, sizes),
        out_shape=[jax.ShapeDtypeStruct(p[3], a.dtype) for p, a in zip(plans, arrays)],
        in_specs=[whole(pl.ANY)] * len(plans),
        out_specs=[whole(pl.ANY)] * len(plans),
        scratch_shapes=scratch,
        compiler_params=pltpu.CompilerParams(collective_id=number, has_side_effects=True),
    )(*arrays)


def rows_of(first, count, size):
    return pl.ds(pl.multiple_of(first * size, size), count * size)


def unit_of(values):
    scaling = lax.rsqrt(jnp.mean(values * values, axis=-1, keepdims=True) + EPS)
    return values * scaling, scaling


def unit_back(grad_rows, unit_rows, scaling, gain):
    grad_unit = grad_rows * gain
    inner = jnp.mean(grad_unit * unit_rows, axis=-1, keepdims=True)
    return scaling * (grad_unit - unit_rows * inner)


def copies(kind, sizes, source_at, target_at, send, recv, own, base=0):
    me, total, place = peers(kind, *sizes)

    def copy_of(k):
        j = lax.rem(me + k, total)
        return pltpu.make_async_remote_copy(
            src_ref=source_at(j),
            dst_ref=target_at(me),
            send_sem=send.at[base + k],
            recv_sem=recv.at[base + k],
            device_id=place(j),
            device_id_type=MESH,
        )

    def each(action):
        def step(k, carry):
            action(copy_of(k))
            return carry

        lax.fori_loop(1, total, step, 0)

    def local():
        return pltpu.make_async_copy(source_at(me), target_at(me), own)

    def start():
        each(lambda c: c.start())
        if own is not None:
            local().start()

    def wait_recv():
        each(lambda c: c.wait_recv())
        if own is not None:
            local().wait()

    def wait_send():
        each(lambda c: c.wait_send())

    return start, wait_recv, wait_send


def greet(kinds, sizes):
    barrier = pltpu.get_barrier_semaphore()
    greeted = 0
    for kind in kinds:
        me, total, place = peers(kind, *sizes)

        def step(k, carry, me=me, total=total, place=place):
            pl.semaphore_signal(
                barrier, inc=1, device_id=place(lax.rem(me + k, total)), device_id_type=MESH
            )
            return carry

        lax.fori_loop(1, total, step, 0)
        greeted += total - 1
    pl.semaphore_wait(barrier, greeted)


def attend_seq(block, s, x_ref, start_ref, gain_ref, wall_ref, qkv_ref, att_ref, hid_ref, lse_ref, lse_acc, stored):
    _, length, _ = x_ref.shape
    pairs = wall_ref.shape[0]
    lane = lax.broadcasted_iota(jnp.int32, (block, PAIR), 1)
    values = x_ref[s].astype(f32)
    normed = (unit_of(values)[0] * gain_ref[...]).astype(bf16)

    def one_pair(n, carry):
        proj = nn(normed, wall_ref[n, :, : 3 * PAIR]).astype(bf16)
        qkv_ref[s, n] = proj
        keys, vals = proj[:, PAIR : 2 * PAIR], proj[:, 2 * PAIR :]
        for i in range(length // block):
            rows = slice(i * block, (i + 1) * block)
            end = (i + 1) * block
            query = proj[rows, :PAIR] * jnp.asarray(HEAD_DIM**-0.5, bf16)
            key_at = lax.broadcasted_iota(jnp.int32, (block, end), 1)
            row_at = i * block + lax.broadcasted_iota(jnp.int32, (block, end), 0)
            allowed = (key_at >= start_ref[s, rows, :]) & (key_at <= row_at)
            got = []
            for j in range(2):
                own = (lane // HEAD_DIM) == j
                score = nt(jnp.where(own, query, jnp.zeros_like(query)), keys[:end])
                score = jnp.where(allowed, score, NEG)
                peak = jnp.max(score, axis=1, keepdims=True)
                expo = jnp.exp(score - peak)
                total = jnp.sum(expo, axis=1, keepdims=True)
                got.append(nn(expo.astype(bf16), vals[:end]) / total)
                lse_acc[rows, :] = jnp.where(
                    lane == 2 * n + j, peak + jnp.log(total), lse_acc[rows, :]
                )
            att_ref[s, n, rows, :] = jnp.where(lane < HEAD_DIM, got[0], got[1]).astype(bf16)
        stored(s, n)
        return carry

    lax.fori_loop(0, pairs, one_pair, 0)
    hidden = values
    for n in range(pairs):
        hidden = hidden + nt(att_ref[s, n], wall_ref[n, :, 3 * PAIR :])
    hid_ref[s] = hidden.astype(bf16)
    lse_ref[s] = jnp.transpose(lse_acc[...])[: 2 * pairs]


def forward_body(
    sizes,
    block,
    inputs_ref,
    cot_ref,
    wall_own_ref,
    start_ref,
    gain_ref,
    xmix_ref,
    gmix_ref,
    x_out,
    wall_out,
    qkv_out,
    att_out,
    lse_ref,
    x_ref,
    wall_ref,
    qkv_ref,
    att_ref,
    hid_ref,
    lse_acc,
    x_send,
    x_recv,
    x_own,
    wall_send,
    wall_recv,
    wall_local,
    share_send,
    share_recv,
    cot_send,
    cot_recv,
    cot_own,
    hid_send,
    hid_recv,
    hid_own,
    out_sem,
    keep_sem,
):
    narrow, wide, _ = sizes
    w, z = lax.axis_index("wide"), lax.axis_index("narrow")
    seqs, length, features = x_ref.shape
    seq_dev, local_len, _ = inputs_ref.shape
    pos_dev = local_len // wide
    pairs = wall_ref.shape[0]
    slice_rows = features // wide
    mine = rows_of(w, 1, slice_rows)
    everyone = wide * narrow

    greet(["all"], sizes)
    wall_z = copies(
        "narrow",
        sizes,
        lambda j: wall_own_ref.at[mine],
        lambda j: wall_ref.at[j, mine],
        wall_send,
        wall_recv,
        wall_local,
    )
    wall_w = copies(
        "wide",
        sizes,
        lambda j: wall_ref.at[:, mine],
        lambda j: wall_ref.at[:, rows_of(j, 1, slice_rows)],
        share_send,
        share_recv,
        None,
    )
    x_z = [
        copies(
            "narrow",
            sizes,
            lambda j, s=s: inputs_ref.at[j * seqs + s],
            lambda j, s=s: x_ref.at[s, rows_of(j, 1, local_len)],
            x_send,
            x_recv,
            x_own.at[s],
            s * narrow,
        )
        for s in range(seqs)
    ]
    cot_w = copies(
        "wide",
        sizes,
        lambda j: cot_ref.at[:, rows_of(j, 1, pos_dev)],
        lambda j: gmix_ref.at[pl.ds(j * seq_dev, seq_dev)],
        cot_send,
        cot_recv,
        cot_own,
    )
    hid_all = [
        copies(
            "all",
            sizes,
            lambda j, s=s: hid_ref.at[
                s, rows_of(lax.rem(j, narrow) * wide + j // narrow, 1, pos_dev)
            ],
            lambda j, s=s: xmix_ref.at[j * seqs + s],
            hid_send,
            hid_recv,
            hid_own.at[s],
            s * everyone,
        )
        for s in range(seqs)
    ]
    wall_z[0]()
    x_z[0][0]()
    wall_z[1]()
    wall_w[0]()
    x_z[0][1]()
    for s in range(1, seqs):
        x_z[s][0]()
    wall_w[1]()
    cot_w[0]()

    def kept(s, n):
        return (
            pltpu.make_async_copy(qkv_ref.at[s, n], qkv_out.at[s, n], out_sem.at[0, s, n]),
            pltpu.make_async_copy(att_ref.at[s, n], att_out.at[s, n], out_sem.at[1, s, n]),
        )

    def stored(s, n):
        for c in kept(s, n):
            c.start()

    wall_keep = pltpu.make_async_copy(wall_ref, wall_out, keep_sem.at[seqs])
    wall_keep.start()
    x_keep = [
        pltpu.make_async_copy(x_ref.at[s], x_out.at[s], keep_sem.at[s]) for s in range(seqs)
    ]
    for s in range(seqs):
        if s > 0:
            x_z[s][1]()
        x_keep[s].start()
        attend_seq(
            block, s, x_ref, start_ref, gain_ref, wall_ref, qkv_ref, att_ref, hid_ref, lse_ref, lse_acc, stored
        )
        hid_all[s][0]()
    wall_z[2]()
    wall_w[2]()
    cot_w[1]()
    cot_w[2]()
    wall_keep.wait()
    for s in range(seqs):
        x_z[s][2]()
        x_keep[s].wait()

        def settle(n, carry, s=s):
            for c in kept(s, n):
                c.wait()
            return carry

        lax.fori_loop(0, pairs, settle, 0)
    for s in range(seqs):
        hid_all[s][1]()
        hid_all[s][2]()


def forward(inputs, cot, wall_own, start_col, gain, sizes, number):
    narrow, wide, _ = sizes
    seq_dev, local_len, features = inputs.shape
    seqs, length, pairs = seq_dev // narrow, local_len * narrow, narrow
    everyone = wide * narrow
    pos_dev = local_len // wide
    dma = pltpu.SemaphoreType.DMA
    qkv_shape = (seqs, pairs, length, 3 * PAIR)
    att_shape = (seqs, pairs, length, PAIR)
    return pl.pallas_call(
        functools.partial(forward_body, sizes, min(256, length)),
        out_shape=[
            jax.ShapeDtypeStruct((seq_dev * wide, pos_dev, features), bf16),
            jax.ShapeDtypeStruct((seq_dev * wide, pos_dev, features), bf16),
            jax.ShapeDtypeStruct((seqs, length, features), bf16),
            jax.ShapeDtypeStruct((pairs,) + wall_own.shape, bf16),
            jax.ShapeDtypeStruct(qkv_shape, bf16),
            jax.ShapeDtypeStruct(att_shape, bf16),
            jax.ShapeDtypeStruct((seqs, 2 * pairs, length), f32),
        ],
        in_specs=[whole(pl.ANY)] * 3 + [whole()] * 2,
        out_specs=[whole(pl.ANY)] * 6 + [whole()],
        scratch_shapes=[
            pltpu.VMEM((seqs, length, features), bf16),
            pltpu.VMEM((pairs,) + wall_own.shape, bf16),
            pltpu.VMEM(qkv_shape, bf16),
            pltpu.VMEM(att_shape, bf16),
            pltpu.VMEM((seqs, length, features), bf16),
            pltpu.VMEM((length, PAIR), f32),
            dma((seqs * narrow,)),
            dma((seqs * narrow,)),
            dma((seqs,)),
            dma((narrow,)),
            dma((narrow,)),
            dma,
            dma((wide,)),
            dma((wide,)),
            dma((wide,)),
            dma((wide,)),
            dma,
            dma((seqs * everyone,)),
            dma((seqs * everyone,)),
            dma((seqs,)),
            dma((2, seqs, pairs)),
            dma((seqs + 1,)),
        ],
        compiler_params=pltpu.CompilerParams(
            collective_id=number, has_side_effects=True, vmem_limit_bytes=VMEM_LIMIT
        ),
    )(inputs, cot, wall_own, start_col, gain)


def attend_back_body(
    block,
    x_ref,
    start_ref,
    gain_ref,
    wall_ref,
    qkv_ref,
    att_ref,
    lse_ref,
    dh_ref,
    gx_ref,
    gwall_ref,
    ggain_ref,
    dq_acc,
    dproj_ref,
    gn_acc,
):
    seqs, length, _ = x_ref.shape
    pairs = wall_ref.shape[0]
    lane = lax.broadcasted_iota(jnp.int32, (length, PAIR), 1)
    scale = jnp.asarray(HEAD_DIM**-0.5, bf16)
    for s in range(seqs):
        values = x_ref[s].astype(f32)
        unit, scaling = unit_of(values)
        normed = (unit * gain_ref[...]).astype(bf16)
        gn_acc[...] = jnp.zeros_like(gn_acc)

        def one_pair(n, carry):
            dh = dh_ref[s]
            d_att = nn(dh, wall_ref[n, :, 3 * PAIR :]).astype(bf16)
            att = att_ref[s, n]
            g_out = tn(dh, att)
            prod = (d_att.astype(f32) * att.astype(f32)).astype(bf16)
            head_row = lax.broadcasted_iota(jnp.int32, (8, PAIR), 0)
            head_lane = lax.broadcasted_iota(jnp.int32, (8, PAIR), 1) // HEAD_DIM
            inner = nt((head_row == head_lane).astype(bf16), prod)
            query = qkv_ref[s, n, :, :PAIR] * scale
            keys, vals = qkv_ref[s, n, :, PAIR : 2 * PAIR], qkv_ref[s, n, :, 2 * PAIR :]
            zero = jnp.zeros_like(query)
            own = [(lane // HEAD_DIM) == j for j in range(2)]
            q_own = [jnp.where(o, query, zero) for o in own]
            k_own = [jnp.where(o, keys, zero) for o in own]
            d_own = [jnp.where(o, d_att, zero) for o in own]
            lse = lse_ref[s]
            head_at = lax.broadcasted_iota(jnp.int32, lse.shape, 0)
            lse_own = [
                jnp.sum(jnp.where(head_at == 2 * n + j, lse, 0.0), axis=0, keepdims=True)
                for j in range(2)
            ]
            dq_acc[...] = jnp.zeros_like(dq_acc)
            for i in range(length // block):
                rows, first = slice(i * block, (i + 1) * block), i * block
                shape = (block, length - first)
                key_at = first + lax.broadcasted_iota(jnp.int32, shape, 0)
                row_at = first + lax.broadcasted_iota(jnp.int32, shape, 1)
                allowed = (key_at >= start_ref[s, :, first:]) & (key_at <= row_at)
                dk = dv = None
                for j in range(2):
                    score = nt(keys[rows], q_own[j][first:])
                    prob = jnp.where(allowed, jnp.exp(score - lse_own[j][:, first:]), 0.0)
                    d_prob = nt(vals[rows], d_own[j][first:])
                    d_score = (prob * (d_prob - inner[j : j + 1, first:])).astype(bf16)
                    dv_part = nn(prob.astype(bf16), d_own[j][first:])
                    dk_part = nn(d_score, q_own[j][first:])
                    dv = dv_part if dv is None else dv + dv_part
                    dk = dk_part if dk is None else dk + dk_part
                    dq_acc[first:, :] += tn(d_score, k_own[j][rows])
                dproj_ref[rows, PAIR : 2 * PAIR] = dk.astype(bf16)
                dproj_ref[rows, 2 * PAIR :] = dv.astype(bf16)
            dproj_ref[:, :PAIR] = (dq_acc[...] * HEAD_DIM**-0.5).astype(bf16)
            d_proj = dproj_ref[...]
            gn_acc[...] += nt(d_proj, wall_ref[n, :, : 3 * PAIR])
            g_in = tn(normed, d_proj)
            if s == 0:
                gwall_ref[n, :, : 3 * PAIR] = g_in
                gwall_ref[n, :, 3 * PAIR :] = g_out
            else:
                gwall_ref[n, :, : 3 * PAIR] += g_in
                gwall_ref[n, :, 3 * PAIR :] += g_out
            return carry

        lax.fori_loop(0, pairs, one_pair, 0)
        grad = gn_acc[...]
        g_gain = jnp.sum(grad * unit, axis=0, keepdims=True)
        if s == 0:
            ggain_ref[...] = g_gain
        else:
            ggain_ref[...] += g_gain
        back = unit_back(grad, unit, scaling, gain_ref[...])
        gx_ref[s] = (dh_ref[s].astype(f32) + back).astype(bf16)


def attend_back(x, start_row, gain, wall, qkv, att, lse, dh):
    seqs, length, features = x.shape
    pairs = wall.shape[0]
    return pl.pallas_call(
        functools.partial(attend_back_body, min(256, length)),
        out_shape=[
            jax.ShapeDtypeStruct((seqs, length, features), bf16),
            jax.ShapeDtypeStruct((pairs, features, 4 * PAIR), f32),
            jax.ShapeDtypeStruct((1, features), f32),
        ],
        in_specs=[whole()] * 8,
        out_specs=[whole()] * 3,
        scratch_shapes=[
            pltpu.VMEM((length, PAIR), f32),
            pltpu.VMEM((length, 3 * PAIR), bf16),
            pltpu.VMEM((length, features), f32),
        ],
        compiler_params=pltpu.CompilerParams(vmem_limit_bytes=VMEM_LIMIT),
    )(x, start_row, gain, wall, qkv, att, lse, dh)


def mix_weights(logits, key_row, experts):
    columns = logits.shape[1]
    cells = 64
    spread = jnp.broadcast_to(logits[:, None, :], (experts, cells, columns)).reshape(
        experts * cells, columns
    )
    row = lax.broadcasted_iota(jnp.int32, (experts * cells, columns), 0)
    spread = jnp.where(lax.rem(row, cells) == key_row, spread, NEG)
    expo = jnp.exp(spread - jnp.max(spread, axis=1, keepdims=True))
    return expo / jnp.sum(expo, axis=1, keepdims=True)


def mix_body(x_ref, g_ref, key_ref, gain_ref, router_ref, mixed_ref, gexp_ref, w_ref):
    experts = router_ref.shape[0]
    values = x_ref[...].astype(f32)
    normed = (unit_of(values)[0] * gain_ref[...]).astype(bf16)
    weights = mix_weights(nt(router_ref[...], normed), key_ref[...], experts)
    w_ref[...] = weights
    low = weights.astype(bf16)
    mixed_ref[...] = nn(low, normed).astype(bf16)
    gexp_ref[...] = nn(low, g_ref[...]).astype(bf16)


def mix(x, g, key_row, gain, router):
    rows = router.shape[0] * 64
    tokens, features = x.shape
    return pl.pallas_call(
        mix_body,
        out_shape=[
            jax.ShapeDtypeStruct((rows, features), bf16),
            jax.ShapeDtypeStruct((rows, features), bf16),
            jax.ShapeDtypeStruct((rows, tokens), f32),
        ],
        in_specs=[whole()] * 5,
        out_specs=[whole()] * 3,
        compiler_params=pltpu.CompilerParams(vmem_limit_bytes=VMEM_LIMIT),
    )(x, g, key_row, gain, router)


def expert_body(m_ref, g_ref, up_ref, down_ref, out_ref, gm_ref, gup_ref, gdown_ref):
    parts = up_ref.shape[0]
    rows, grads = m_ref[...], g_ref[...]
    out = gm = None
    for h in range(parts):
        pre = nn(rows, up_ref[h])
        square = pre * pre
        inner = 0.7978845608028654 * (pre + 0.044715 * pre * square)
        tanh = jnp.tanh(inner)
        act = 0.5 * pre * (1.0 + tanh)
        slope = 0.5 * (1.0 + tanh) + 0.5 * pre * (1.0 - tanh * tanh) * (
            0.7978845608028654 * (1.0 + 3 * 0.044715 * square)
        )
        low = act.astype(bf16)
        g_pre = (nt(grads, down_ref[h]) * slope).astype(bf16)
        out_part, gm_part = nn(low, down_ref[h]), nt(g_pre, up_ref[h])
        out = out_part if out is None else out + out_part
        gm = gm_part if gm is None else gm + gm_part
        gup_ref[h] = tn(rows, g_pre).astype(bf16)
        gdown_ref[h] = tn(low, grads).astype(bf16)
    out_ref[...] = out.astype(bf16)
    gm_ref[...] = gm.astype(bf16)


def expert(rows, grads, up, down):
    return pl.pallas_call(
        expert_body,
        out_shape=[jax.ShapeDtypeStruct(a.shape, bf16) for a in (rows, grads, up, down)],
        in_specs=[whole()] * 4,
        out_specs=[whole()] * 4,
        compiler_params=pltpu.CompilerParams(vmem_limit_bytes=VMEM_LIMIT),
    )(rows, grads, up, down)


def mix_back_body(
    x_ref, g_ref, gain_ref, router_ref, w_ref, eo_ref, gm_ref, out_ref, gh_ref, ggain_ref, grouter_ref
):
    experts = router_ref.shape[0]
    values = x_ref[...].astype(f32)
    unit, scaling = unit_of(values)
    normed = (unit * gain_ref[...]).astype(bf16)
    weights = w_ref[...]
    low = weights.astype(bf16)
    low_t = jnp.transpose(low)
    out_ref[...] = (values + nn(low_t, eo_ref[...])).astype(bf16)
    g_weights = nt(eo_ref[...], g_ref[...]) + nt(gm_ref[...], normed)
    inner = jnp.sum(weights * g_weights, axis=1, keepdims=True)
    g_logits = weights * (g_weights - inner)
    columns = g_logits.shape[1]
    g_logits = jnp.sum(g_logits.reshape(experts, 64, columns), axis=1).astype(bf16)
    g_normed = nn(low_t, gm_ref[...]) + tn(g_logits, router_ref[...])
    grouter_ref[...] = nn(g_logits, normed)
    ggain_ref[...] = jnp.sum(g_normed * unit, axis=0, keepdims=True)
    back = unit_back(g_normed, unit, scaling, gain_ref[...])
    gh_ref[...] = (g_ref[...].astype(f32) + back).astype(bf16)


def mix_back(x, g, gain, router, weights, eo, gm):
    return pl.pallas_call(
        mix_back_body,
        out_shape=[
            jax.ShapeDtypeStruct(x.shape, bf16),
            jax.ShapeDtypeStruct(x.shape, bf16),
            jax.ShapeDtypeStruct((1, x.shape[1]), f32),
            jax.ShapeDtypeStruct(router.shape, f32),
        ],
        in_specs=[whole()] * 7,
        out_specs=[whole()] * 4,
        compiler_params=pltpu.CompilerParams(vmem_limit_bytes=VMEM_LIMIT),
    )(x, g, gain, router, weights, eo, gm)


def per_device(
    inputs,
    positions,
    members_index,
    members_mask,
    gain_attn,
    input_projection_weight,
    output_projection_weight,
    gain_mixer,
    weight_router,
    weight_up,
    weight_down,
    cotangent,
):
    narrow, wide = lax.axis_size("narrow"), lax.axis_size("wide")
    w, z = lax.axis_index("wide"), lax.axis_index("narrow")
    seq_dev, local_len, features = inputs.shape
    length = positions.shape[1]
    groups = members_index.shape[1]
    experts = weight_up.shape[0]
    own_seqs = seq_dev // narrow
    pos_dev = local_len // wide
    seq_total = seq_dev * wide
    sizes = (narrow, wide, experts)

    wall = jnp.concatenate(
        [
            input_projection_weight.reshape(features, -1),
            jnp.transpose(output_projection_weight),
        ],
        axis=1,
    )
    e = lax.rem(w, experts)
    up_full = lax.all_gather(
        lax.dynamic_index_in_dim(weight_up, e, 0, keepdims=False), "narrow", axis=0, tiled=False
    )
    down_full = lax.all_gather(
        lax.dynamic_index_in_dim(weight_down, e, 0, keepdims=False), "narrow", axis=0, tiled=False
    )

    row_pos = lax.dynamic_slice_in_dim(positions, z * own_seqs, own_seqs, 0)
    starts = jnp.arange(length, dtype=jnp.int32)[None, :] - row_pos
    offset_rows = w * pos_dev
    index_rows = lax.dynamic_slice_in_dim(members_index, offset_rows, pos_dev, 0)
    live = lax.dynamic_slice_in_dim(members_mask, offset_rows, pos_dev, 0) > 0
    named = (
        index_rows[..., None] == jnp.arange(seq_total, dtype=jnp.int32)[None, None, None, :]
    ) & live[..., None]
    group_of = jnp.max(
        jnp.where(named, jnp.arange(groups, dtype=jnp.int32)[None, :, None, None], 0), axis=(1, 2)
    )
    key_row = group_of + groups * jnp.arange(pos_dev, dtype=jnp.int32)[:, None]
    key_row = jnp.transpose(key_row).reshape(1, seq_total * pos_dev)

    gain_one, gain_two = gain_attn.reshape(1, features), gain_mixer.reshape(1, features)
    router = jnp.transpose(weight_router)

    x_mix, g_mix, x_seq, wall, qkv, att, lse = forward(
        inputs, cotangent, wall, starts[:, :, None], gain_one, sizes, 1
    )
    x_mix = x_mix.reshape(seq_total * pos_dev, features)
    g_mix = g_mix.reshape(seq_total * pos_dev, features)
    mixed, g_exp, weights = mix(x_mix, g_mix, key_row, gain_two, router)
    cells = pos_dev * groups

    def swap(a, b, number):
        shape = (experts, cells, features)
        plan = ("cluster", lambda r, j: r.at[j], lambda r, j: r.at[j], shape)
        a, b = exchange([plan, plan], [a.reshape(shape), b.reshape(shape)], sizes, number)
        return a.reshape(-1, features), b.reshape(-1, features)

    rows, row_grads = swap(mixed, g_exp, 3)
    eo, gm, g_up, g_down = expert(rows, row_grads, up_full, down_full)
    eo, gm = swap(eo, gm, 4)
    out_mix, gh_mix, g_gain_two, g_router = mix_back(
        x_mix, g_mix, gain_two, router, weights, eo, gm
    )
    dh, outputs = exchange(
        [
            (
                "all",
                lambda r, j: r.at[pl.ds(j * own_seqs, own_seqs)],
                lambda r, j: r.at[:, rows_of(lax.rem(j, narrow) * wide + j // narrow, 1, pos_dev)],
                (own_seqs, length, features),
            ),
            (
                "wide",
                lambda r, j: r.at[pl.ds(j * seq_dev, seq_dev)],
                lambda r, j: r.at[:, rows_of(j, 1, pos_dev)],
                inputs.shape,
            ),
        ],
        [
            gh_mix.reshape(seq_total, pos_dev, features),
            out_mix.reshape(seq_total, pos_dev, features),
        ],
        sizes,
        5,
    )
    gx, g_wall, g_gain_one = attend_back(
        x_seq, starts[:, None, :], gain_one, wall, qkv, att, lse, dh
    )
    (gx,) = exchange(
        [
            (
                "narrow",
                lambda r, j: r.at[:, rows_of(j, 1, local_len)],
                lambda r, j: r.at[pl.ds(j * own_seqs, own_seqs)],
                inputs.shape,
            )
        ],
        [gx],
        sizes,
        6,
    )
    grad_inputs = gx.astype(f32)

    def expert_grad(part):
        part = lax.psum_scatter(part, "narrow", scatter_dimension=0, tiled=False)
        part = lax.all_gather(part, "wide", axis=0, tiled=False)
        return jnp.sum(
            part.reshape((wide // experts, experts) + part.shape[1:]).astype(f32), axis=0
        )

    grad_up, grad_down = expert_grad(g_up), expert_grad(g_down)
    g_wall = lax.psum_scatter(g_wall.astype(bf16), "narrow", scatter_dimension=0, tiled=False)
    g_wall = lax.psum(g_wall, "wide").astype(f32)
    g_inproj = g_wall[:, : 3 * PAIR].reshape(input_projection_weight.shape)
    g_outproj = jnp.transpose(g_wall[:, 3 * PAIR :])
    g_gain_one, g_gain_two, g_router = lax.psum(
        (g_gain_one, g_gain_two, g_router), ("wide", "narrow")
    )
    return (
        outputs,
        grad_inputs,
        g_gain_one.reshape(features),
        g_inproj,
        g_outproj,
        g_gain_two.reshape(features),
        jnp.transpose(g_router),
        grad_up,
        grad_down,
    )


def solution(mesh):
    in_specs = (
        P("wide", "narrow", None),
        P("wide", None),
        P("narrow", None, None),
        P("narrow", None, None),
        P(),
        P(None, None, "narrow"),
        P("narrow", None),
        P(),
        P(),
        P(None, None, "narrow"),
        P(None, "narrow", None),
        P("wide", "narrow", None),
    )
    out_specs = (
        P("wide", "narrow", None),
        P("wide", "narrow", None),
        P(),
        P(None, None, "narrow"),
        P("narrow", None),
        P(),
        P(),
        P(None, None, "narrow"),
        P(None, "narrow", None),
    )
    return jax.shard_map(
        per_device, mesh=mesh, in_specs=in_specs, out_specs=out_specs, check_vma=False
    )
```

```python
import functools

import jax
import jax.numpy as jnp
from jax import lax
from jax.experimental import pallas as pl
from jax.experimental.pallas import tpu as pltpu
from jax.sharding import PartitionSpec as P

MESH = pl.DeviceIdType.MESH
HEAD_DIM = 64
PAIR = 2 * HEAD_DIM
EPS = 1e-06
NEG = -1e30
bf16 = jnp.bfloat16
f32 = jnp.float32
VMEM_LIMIT = 60 << 20


def nn(a, b):
    return lax.dot_general(a, b, (((1,), (0,)), ((), ())), preferred_element_type=f32)


def nt(a, b):
    return lax.dot_general(a, b, (((1,), (1,)), ((), ())), preferred_element_type=f32)


def tn(a, b):
    return lax.dot_general(a, b, (((0,), (0,)), ((), ())), preferred_element_type=f32)


def whole(memory=pltpu.VMEM):
    return pl.BlockSpec(memory_space=memory)


def rows_of(first, count, size):
    return pl.ds(pl.multiple_of(first * size, size), count * size)


def peers(kind, sizes):
    narrow, wide, twins = sizes
    w, z = lax.axis_index("wide"), lax.axis_index("narrow")
    first = (w // twins) * twins
    if kind == "narrow":
        return z, narrow, lambda j: (w, j)
    if kind == "wide":
        return w, wide, lambda j: (j, z)
    if kind == "twin":
        return w - first, twins, lambda j: (first + j, z)
    if kind == "row":
        return w // twins, wide // twins, lambda j: (j * twins + w - first, z)
    if kind == "column":
        return (
            z * twins + w - first,
            narrow * twins,
            lambda j: (first + lax.rem(j, twins), j // twins),
        )
    return w * narrow + z, wide * narrow, lambda j: (j // narrow, lax.rem(j, narrow))


def group_size(kind, sizes):
    narrow, wide, twins = sizes
    return {
        "narrow": narrow,
        "wide": wide,
        "twin": twins,
        "row": wide // twins,
        "column": narrow * twins,
        "all": wide * narrow,
    }[kind]


def plan(kinds, sizes):
    bases, used = {}, 0
    for name, kind in kinds.items():
        bases[name] = used
        used += group_size(kind, sizes)
    return bases, used


class Exchange:
    def __init__(self, kind, sizes, source_at, target_at, sems, base, own=None):
        self.me, self.total, self.place = peers(kind, sizes)
        self.source_at, self.target_at = source_at, target_at
        (self.send, self.recv, self.local), self.base, self.own = sems, base, own

    def copy_of(self, k):
        j = lax.rem(self.me + k, self.total)
        return pltpu.make_async_remote_copy(
            src_ref=self.source_at(j),
            dst_ref=self.target_at(self.me),
            send_sem=self.send.at[self.base + k],
            recv_sem=self.recv.at[self.base + k],
            device_id=self.place(j),
            device_id_type=MESH,
        )

    def each(self, action):
        def step(k, carry):
            action(self.copy_of(k))
            return carry

        lax.fori_loop(1, self.total, step, 0)

    def kept(self):
        return pltpu.make_async_copy(
            self.source_at(self.me), self.target_at(self.me), self.local.at[self.own]
        )

    def start(self):
        self.each(lambda c: c.start())
        if self.own is not None:
            self.kept().start()

    def wait_recv(self):
        self.each(lambda c: c.wait_recv())
        if self.own is not None:
            self.kept().wait()

    def wait_send(self):
        self.each(lambda c: c.wait_send())


def greet(sizes):
    barrier = pltpu.get_barrier_semaphore()
    me, total, place = peers("all", sizes)

    def step(k, carry):
        pl.semaphore_signal(
            barrier, inc=1, device_id=place(lax.rem(me + k, total)), device_id_type=MESH
        )
        return carry

    lax.fori_loop(1, total, step, 0)
    pl.semaphore_wait(barrier, total - 1)


def unit_of(values):
    scaling = lax.rsqrt(jnp.mean(values * values, axis=-1, keepdims=True) + EPS)
    return values * scaling, scaling


def unit_back(grad_rows, unit_rows, scaling, gain):
    grad_unit = grad_rows * gain
    inner = jnp.mean(grad_unit * unit_rows, axis=-1, keepdims=True)
    return scaling * (grad_unit - unit_rows * inner)


def wall_of(wall_ref, n):
    part = wall_ref[n]
    return part.reshape(-1, part.shape[-1])


def attend_pairs(
    block, s, low, high, normed, start_ref, wall_ref, qkv_ref, att_ref, lse_acc, stored
):
    length = normed.shape[0]
    lane = lax.broadcasted_iota(jnp.int32, (block, PAIR), 1)

    def one_pair(n, carry):
        proj = nn(normed[...], wall_of(wall_ref, n)[:, : 3 * PAIR]).astype(bf16)
        qkv_ref[s, n] = proj
        keys, vals = proj[:, PAIR : 2 * PAIR], proj[:, 2 * PAIR :]
        for i in range(length // block):
            rows = slice(i * block, (i + 1) * block)
            end = (i + 1) * block
            query = proj[rows, :PAIR] * jnp.asarray(HEAD_DIM**-0.5, bf16)
            key_at = lax.broadcasted_iota(jnp.int32, (block, end), 1)
            row_at = i * block + lax.broadcasted_iota(jnp.int32, (block, end), 0)
            allowed = (key_at >= start_ref[s, rows, :]) & (key_at <= row_at)
            got = []
            for j in range(2):
                own = (lane // HEAD_DIM) == j
                score = nt(jnp.where(own, query, jnp.zeros_like(query)), keys[:end])
                score = jnp.where(allowed, score, NEG)
                peak = jnp.max(score, axis=1, keepdims=True)
                expo = jnp.exp(score - peak)
                total = jnp.sum(expo, axis=1, keepdims=True)
                got.append(nn(expo.astype(bf16), vals[:end]) / total)
                lse_acc[rows, :] = jnp.where(
                    lane == 2 * n + j, peak + jnp.log(total), lse_acc[rows, :]
                )
            att_ref[s, n, rows, :] = jnp.where(lane < HEAD_DIM, got[0], got[1]).astype(bf16)
        stored(s, n)
        return carry

    lax.fori_loop(low, high, one_pair, 0)


def forward_kinds(seqs):
    kinds = {"wall": "narrow", "wall_row": "row", "wall_twin": "twin", "cot": "wide"}
    for t in range(2):
        kinds[f"weight{t}"], kinds[f"weight_row{t}"] = "narrow", "row"
    for s in range(seqs):
        kinds[f"x{s}"], kinds[f"hid{s}"] = "narrow", "all"
    return kinds


def forward_body(
    sizes,
    block,
    bases,
    inputs_ref,
    cot_ref,
    wall_own_ref,
    up_ref,
    down_ref,
    start_ref,
    gain_ref,
    xmix_ref,
    gmix_ref,
    weight_ref,
    x_out,
    wall_out,
    qkv_out,
    att_out,
    lse_ref,
    x_ref,
    wall_ref,
    qkv_ref,
    att_ref,
    hid_ref,
    normed_ref,
    lse_acc,
    send,
    recv,
    local,
    out_sem,
):
    narrow, wide, twins = sizes
    w, z = lax.axis_index("wide"), lax.axis_index("narrow")
    seqs, length, features = x_ref.shape
    seq_dev, local_len, _ = inputs_ref.shape
    pos_dev = local_len // wide
    pairs = wall_ref.shape[0]
    row, twin = w // twins, lax.rem(w, twins)
    wall_rows = features // wide
    weight_rows = features // (wide // twins)
    sems = (send, recv, local)

    def exchange(name, kind, source_at, target_at, own=None):
        return Exchange(kind, sizes, source_at, target_at, sems, bases[name], own)

    greet(sizes)
    wall = exchange(
        "wall",
        "narrow",
        lambda j: wall_own_ref.at[rows_of(w, 1, wall_rows)],
        lambda j: wall_ref.at[j, row, twin],
        0,
    )
    wall_row = exchange(
        "wall_row",
        "row",
        lambda j: wall_ref.at[:, row, twin],
        lambda j: wall_ref.at[:, j, twin],
    )
    wall_twin = exchange(
        "wall_twin", "twin", lambda j: wall_ref.at[:, :, twin], lambda j: wall_ref.at[:, :, j]
    )
    cot = exchange(
        "cot",
        "wide",
        lambda j: cot_ref.at[:, rows_of(j, 1, pos_dev)],
        lambda j: gmix_ref.at[pl.ds(j * seq_dev, seq_dev)],
        1,
    )
    mine = rows_of(row, 1, weight_rows)
    weight = [
        exchange(
            f"weight{t}",
            "narrow",
            lambda j, ref=ref: ref.at[j * twins + twin, mine],
            lambda j, t=t: weight_ref.at[t, j, mine],
            2 + t,
        )
        for t, ref in enumerate((up_ref, down_ref))
    ]
    weight_row = [
        exchange(
            f"weight_row{t}",
            "row",
            lambda j, t=t: weight_ref.at[t, :, mine],
            lambda j, t=t: weight_ref.at[t, :, rows_of(j, 1, weight_rows)],
        )
        for t in range(2)
    ]
    x_in = [
        exchange(
            f"x{s}",
            "narrow",
            lambda j, s=s: inputs_ref.at[j * seqs + s],
            lambda j, s=s: x_ref.at[s, rows_of(j, 1, local_len)],
            4 + s,
        )
        for s in range(seqs)
    ]
    hid = [
        exchange(
            f"hid{s}",
            "all",
            lambda j, s=s: hid_ref.at[
                s, rows_of(lax.rem(j, narrow) * wide + j // narrow, 1, pos_dev)
            ],
            lambda j, s=s: xmix_ref.at[j * seqs + s],
            4 + seqs + s,
        )
        for s in range(seqs)
    ]

    def kept(s, n):
        return (
            pltpu.make_async_copy(qkv_ref.at[s, n], qkv_out.at[s, n], out_sem.at[s, 2 * n]),
            pltpu.make_async_copy(att_ref.at[s, n], att_out.at[s, n], out_sem.at[s, 2 * n + 1]),
        )

    def stored(s, n):
        for c in kept(s, n):
            c.start()

    wall_keep = pltpu.make_async_copy(wall_ref, wall_out, out_sem.at[0, 2 * pairs])
    x_keep = [
        pltpu.make_async_copy(x_ref.at[s], x_out.at[s], out_sem.at[s, 2 * pairs + 1])
        for s in range(seqs)
    ]

    wall.start()
    x_in[0].start()
    wall.wait_recv()
    wall_row.start()
    wall_row.wait_recv()
    wall_twin.start()
    cot.start()
    wall_twin.wait_recv()
    x_in[0].wait_recv()
    weight[0].start()
    weight[1].start()
    wall_keep.start()
    for s in range(seqs):
        if s > 0:
            x_in[s].wait_recv()
        x_keep[s].start()
        normed_ref[...] = (unit_of(x_ref[s].astype(f32))[0] * gain_ref[...]).astype(bf16)

        def pairs_of(low, high, s=s):
            attend_pairs(
                block, s, low, high, normed_ref, start_ref, wall_ref, qkv_ref, att_ref, lse_acc, stored
            )

        pairs_of(0, pairs // 2)
        if s + 1 < seqs:
            x_in[s + 1].start()
        pairs_of(pairs // 2, pairs)
        hidden = x_ref[s].astype(f32)
        for n in range(pairs):
            hidden = hidden + nt(att_ref[s, n], wall_of(wall_ref, n)[:, 3 * PAIR :])
        hid_ref[s] = hidden.astype(bf16)
        hid[s].start()
        lse_ref[s] = jnp.transpose(lse_acc[...])[: 2 * pairs]
        if s == 0:
            for t in range(2):
                weight[t].wait_recv()
                weight_row[t].start()
    for e in (wall, wall_row, wall_twin, cot, *weight, *weight_row, *x_in):
        e.wait_send()
    cot.wait_recv()
    for t in range(2):
        weight_row[t].wait_recv()
    wall_keep.wait()
    for s in range(seqs):
        x_keep[s].wait()

        def settle(n, carry, s=s):
            for c in kept(s, n):
                c.wait()
            return carry

        lax.fori_loop(0, pairs, settle, 0)
    for s in range(seqs):
        hid[s].wait_recv()
        hid[s].wait_send()


def forward(inputs, cot, wall_own, up, down, start_col, gain, sizes):
    narrow, wide, twins = sizes
    seq_dev, local_len, features = inputs.shape
    seqs, length, pairs = seq_dev // narrow, local_len * narrow, narrow
    pos_dev = local_len // wide
    wall_shape = (pairs, wide // twins, twins, features // wide, wall_own.shape[1])
    bases, used = plan(forward_kinds(seqs), sizes)
    dma = pltpu.SemaphoreType.DMA
    qkv_shape = (seqs, pairs, length, 3 * PAIR)
    att_shape = (seqs, pairs, length, PAIR)
    mix_shape = (seq_dev * wide, pos_dev, features)
    return pl.pallas_call(
        functools.partial(forward_body, sizes, min(256, length), bases),
        out_shape=[
            jax.ShapeDtypeStruct(mix_shape, bf16),
            jax.ShapeDtypeStruct(mix_shape, bf16),
            jax.ShapeDtypeStruct((2, narrow) + up.shape[1:], bf16),
            jax.ShapeDtypeStruct((seqs, length, features), bf16),
            jax.ShapeDtypeStruct(wall_shape, bf16),
            jax.ShapeDtypeStruct(qkv_shape, bf16),
            jax.ShapeDtypeStruct(att_shape, bf16),
            jax.ShapeDtypeStruct((seqs, 2 * pairs, length), f32),
        ],
        in_specs=[whole(pl.ANY)] * 5 + [whole()] * 2,
        out_specs=[whole(pl.ANY)] * 7 + [whole()],
        scratch_shapes=[
            pltpu.VMEM((seqs, length, features), bf16),
            pltpu.VMEM(wall_shape, bf16),
            pltpu.VMEM(qkv_shape, bf16),
            pltpu.VMEM(att_shape, bf16),
            pltpu.VMEM((seqs, length, features), bf16),
            pltpu.VMEM((length, features), bf16),
            pltpu.VMEM((length, PAIR), f32),
            dma((used,)),
            dma((used,)),
            dma((4 + 2 * seqs,)),
            dma((seqs, 2 * pairs + 2)),
        ],
        compiler_params=pltpu.CompilerParams(
            collective_id=1, has_side_effects=True, vmem_limit_bytes=VMEM_LIMIT
        ),
    )(inputs, cot, wall_own, up, down, start_col, gain)


def mix_forward(experts, cells, x_ref, key_ref, gain_ref, router_ref, normed_ref, weight_ref, low_ref, logit_ref):
    tokens = x_ref.shape[0]
    chunk = min(512, tokens)

    def norm_rows(c, carry):
        rows = rows_of(c, 1, chunk)
        unit = unit_of(x_ref[rows, :].astype(f32))[0]
        normed_ref[rows, :] = (unit * gain_ref[...]).astype(bf16)
        return carry

    lax.fori_loop(0, tokens // chunk, norm_rows, 0)
    logit_ref[...] = nt(router_ref[...], normed_ref[...])

    def one_expert(e, carry):
        cell = lax.broadcasted_iota(jnp.int32, (cells, tokens), 0)
        score = jnp.where(cell == key_ref[...], logit_ref[pl.ds(e, 1), :], NEG)
        expo = jnp.exp(score - jnp.max(score, axis=1, keepdims=True))
        weights = expo / jnp.sum(expo, axis=1, keepdims=True)
        rows = rows_of(e, 1, cells)
        weight_ref[rows, :] = weights
        low_ref[rows, :] = weights.astype(bf16)
        return carry

    lax.fori_loop(0, experts, one_expert, 0)


def gelu_parts(pre):
    square = pre * pre
    tanh = jnp.tanh(0.7978845608028654 * (pre + 0.044715 * pre * square))
    act = 0.5 * pre * (1.0 + tanh)
    slope = 0.5 * (1.0 + tanh) + 0.5 * pre * (1.0 - tanh * tanh) * (
        0.7978845608028654 * (1.0 + 3 * 0.044715 * square)
    )
    return act, slope


def mix_weights_back(experts, cells, weight_ref, gw_ref, gl_ref):
    def one_expert(e, carry):
        rows = rows_of(e, 1, cells)
        weights, grads = weight_ref[rows, :], gw_ref[rows, :]
        inner = jnp.sum(weights * grads, axis=1, keepdims=True)
        gl_ref[pl.ds(e, 1), :] = jnp.sum(weights * (grads - inner), axis=0, keepdims=True)
        return carry

    lax.fori_loop(0, experts, one_expert, 0)


def attend_back_pairs(
    block, s, last, low, high, start_ref, lse_ref, x_n, x_nt, dh_ref, dh_t, wall_ref, qkv_ref, att_ref, dq_acc, dproj_ref, gn_acc, gw_acc, finished
):
    length = x_n.shape[0]
    lane = lax.broadcasted_iota(jnp.int32, (length, PAIR), 1)
    scale = jnp.asarray(HEAD_DIM**-0.5, bf16)

    def one_pair(n, carry):
        wall = wall_of(wall_ref, n)
        d_att = nn(dh_ref[s], wall[:, 3 * PAIR :]).astype(bf16)
        att = att_ref[s, n]
        g_out = nn(dh_t[...], att)
        prod = (d_att.astype(f32) * att.astype(f32)).astype(bf16)
        head_row = lax.broadcasted_iota(jnp.int32, (8, PAIR), 0)
        head_lane = lax.broadcasted_iota(jnp.int32, (8, PAIR), 1) // HEAD_DIM
        inner = nt((head_row == head_lane).astype(bf16), prod)
        query = qkv_ref[s, n, :, :PAIR] * scale
        keys, vals = qkv_ref[s, n, :, PAIR : 2 * PAIR], qkv_ref[s, n, :, 2 * PAIR :]
        zero = jnp.zeros_like(query)
        own = [(lane // HEAD_DIM) == j for j in range(2)]
        q_own = [jnp.where(o, query, zero) for o in own]
        k_own = [jnp.where(o, keys, zero) for o in own]
        d_own = [jnp.where(o, d_att, zero) for o in own]
        lse_own = [lse_ref[s, pl.ds(2 * n + j, 1), :] for j in range(2)]
        dq_acc[...] = jnp.zeros_like(dq_acc)
        for i in range(length // block):
            rows, first = slice(i * block, (i + 1) * block), i * block
            shape = (block, length - first)
            key_at = first + lax.broadcasted_iota(jnp.int32, shape, 0)
            row_at = first + lax.broadcasted_iota(jnp.int32, shape, 1)
            allowed = (key_at >= start_ref[s, :, first:]) & (key_at <= row_at)
            dk = dv = None
            for j in range(2):
                score = nt(keys[rows], q_own[j][first:])
                prob = jnp.where(allowed, jnp.exp(score - lse_own[j][:, first:]), 0.0)
                d_prob = nt(vals[rows], d_own[j][first:])
                d_score = (prob * (d_prob - inner[j : j + 1, first:])).astype(bf16)
                dv_part = nn(prob.astype(bf16), d_own[j][first:])
                dk_part = nn(d_score, q_own[j][first:])
                dv = dv_part if dv is None else dv + dv_part
                dk = dk_part if dk is None else dk + dk_part
                dq_acc[first:, :] += tn(d_score, k_own[j][rows])
            dproj_ref[rows, PAIR : 2 * PAIR] = dk.astype(bf16)
            dproj_ref[rows, 2 * PAIR :] = dv.astype(bf16)
        dproj_ref[:, :PAIR] = (dq_acc[...] * HEAD_DIM**-0.5).astype(bf16)
        d_proj = dproj_ref[...]
        gn_acc[...] += nt(d_proj, wall[:, : 3 * PAIR])
        g_in = nn(x_nt[...], d_proj)
        if s == 0:
            gw_acc[n, :, : 3 * PAIR] = g_in
            gw_acc[n, :, 3 * PAIR :] = g_out
        else:
            gw_acc[n, :, : 3 * PAIR] += g_in
            gw_acc[n, :, 3 * PAIR :] += g_out
        if last:
            finished(n)
        return carry

    lax.fori_loop(low, high, one_pair, 0)


def back_kinds(seqs, pairs):
    kinds = {name: "column" for name in ("mixed", "gexp", "eo", "gm")}
    kinds["out"] = "wide"
    for t in range(2):
        kinds[f"sum_row{t}"], kinds[f"sum_z{t}"] = "row", "narrow"
        kinds[f"full_row{t}"], kinds[f"full_twin{t}"] = "row", "twin"
    for s in range(seqs):
        kinds[f"dh{s}"], kinds[f"gx{s}"] = "all", "narrow"
    for n in range(pairs):
        kinds[f"wall_twin{n}"] = "twin"
    kinds["wall_row"], kinds["wall_z"], kinds["wall_full"] = "row", "narrow", "wide"
    kinds["small_w"], kinds["small_z"] = "wide", "narrow"
    return kinds


def backward_body(
    sizes,
    block,
    bases,
    xmix_in,
    gmix_in,
    weight_in,
    x_in,
    wall_in,
    qkv_in,
    att_in,
    key_ref,
    start_ref,
    lse_ref,
    gain_one,
    gain_two,
    router_ref,
    out_home,
    gx_home,
    full_ref,
    wall_out,
    small_out,
    mixed_src,
    gexp_src,
    eo_src,
    gm_src,
    mixed_land,
    gexp_land,
    eo_land,
    gm_land,
    grad_src,
    sum_land,
    sum_src,
    gh_ref,
    out_ref,
    dh_ref,
    gx_ref,
    gw_src,
    gw_twin,
    gw_half,
    gw_row,
    gw_z_src,
    gw_z,
    gw_last,
    small_ref,
    small_w,
    small_mid,
    small_z,
    send,
    recv,
    local,
    load_sem,
):
    narrow, wide, twins = sizes
    w, z = lax.axis_index("wide"), lax.axis_index("narrow")
    row, twin = w // twins, lax.rem(w, twins)
    row_count = wide // twins
    seqs, length, features = dh_ref.shape
    seq_total, pos_dev, _ = gh_ref.shape
    tokens = seq_total * pos_dev
    seq_dev, local_len, _ = out_home.shape
    experts = router_ref.shape[0]
    cells = mixed_src.shape[0] // experts
    pairs = gw_src.shape[0]
    part_rows = sum_src.shape[2]
    wall_rows = gw_last.shape[0]
    mine = rows_of(row, 1, part_rows)
    sems = (send, recv, local)
    owns = iter(range(local.shape[0]))

    def exchange(name, kind, source_at, target_at, own=False):
        return Exchange(
            kind, sizes, source_at, target_at, sems, bases[name], next(owns) if own else None
        )

    def column(name, source, target):
        return exchange(
            name,
            "column",
            lambda j: source.at[rows_of(j, 1, cells)],
            lambda j: target.at[rows_of(j, 1, cells)],
            True,
        )

    mixed_x = column("mixed", mixed_src, mixed_land)
    gexp_x = column("gexp", gexp_src, gexp_land)
    eo_x = column("eo", eo_src, eo_land)
    gm_x = column("gm", gm_src, gm_land)
    out_x = exchange(
        "out",
        "wide",
        lambda j: out_ref.at[pl.ds(j * seq_dev, seq_dev)],
        lambda j: out_home.at[:, rows_of(j, 1, pos_dev)],
        True,
    )
    sum_row = [
        exchange(
            f"sum_row{t}",
            "row",
            lambda j, t=t: grad_src.at[t, :, rows_of(j, 1, part_rows)],
            lambda j, t=t: sum_land.at[j, t],
        )
        for t in range(2)
    ]
    sum_z = [
        exchange(
            f"sum_z{t}",
            "narrow",
            lambda j, t=t: sum_src.at[t, j],
            lambda j, t=t: full_ref.at[t, j, twin, mine],
            True,
        )
        for t in range(2)
    ]
    full_row = [
        exchange(
            f"full_row{t}",
            "row",
            lambda j, t=t: full_ref.at[t, :, twin, mine],
            lambda j, t=t: full_ref.at[t, :, twin, rows_of(j, 1, part_rows)],
        )
        for t in range(2)
    ]
    full_twin = [
        exchange(
            f"full_twin{t}",
            "twin",
            lambda j, t=t: full_ref.at[t, :, twin],
            lambda j, t=t: full_ref.at[t, :, j],
        )
        for t in range(2)
    ]
    dh_x = [
        exchange(
            f"dh{s}",
            "all",
            lambda j, s=s: gh_ref.at[j * seqs + s],
            lambda j, s=s: dh_ref.at[
                s, rows_of(lax.rem(j, narrow) * wide + j // narrow, 1, pos_dev)
            ],
            True,
        )
        for s in range(seqs)
    ]
    gx_x = [
        exchange(
            f"gx{s}",
            "narrow",
            lambda j, s=s: gx_ref.at[s, rows_of(j, 1, local_len)],
            lambda j, s=s: gx_home.at[j * seqs + s],
            True,
        )
        for s in range(seqs)
    ]

    def wall_twin(n):
        e = exchange(
            "wall_twin0",
            "twin",
            lambda j: gw_src.at[n, :, j],
            lambda j: gw_twin.at[j, n],
        )
        e.base = bases["wall_twin0"] + n * twins
        return e

    wall_row = exchange(
        "wall_row", "row", lambda j: gw_half.at[:, j], lambda j: gw_row.at[j]
    )
    wall_z = exchange("wall_z", "narrow", lambda j: gw_z_src.at[j], lambda j: gw_z.at[j])
    wall_full = exchange(
        "wall_full",
        "wide",
        lambda j: gw_last,
        lambda j: wall_out.at[rows_of(j, 1, wall_rows)],
        True,
    )
    small_wide = exchange("small_w", "wide", lambda j: small_ref, lambda j: small_w.at[j])
    small_narrow = exchange("small_z", "narrow", lambda j: small_mid, lambda j: small_z.at[j])

    greet(sizes)

    def mixture(x_ref, g_ref, normed_ref, weight_ref, low_ref, low_t, logit_ref):
        x_load = pltpu.make_async_copy(xmix_in, x_ref, load_sem.at[0])
        g_load = pltpu.make_async_copy(gmix_in, g_ref, load_sem.at[1])
        x_load.start()
        g_load.start()

        def experts_of(up_down, act_ref, slope_ref, pre_ref):
            w_load = pltpu.make_async_copy(weight_in, up_down, load_sem.at[2])
            w_load.start()
            x_load.wait()
            mix_forward(
                experts, cells, x_ref, key_ref, gain_two, router_ref, normed_ref, weight_ref, low_ref, logit_ref
            )
            mixed_src[...] = nn(low_ref[...], normed_ref[...]).astype(bf16)
            mixed_x.start()
            g_load.wait()
            gexp_src[...] = nn(low_ref[...], g_ref[...]).astype(bf16)
            gexp_x.start()
            low_t[...] = jnp.transpose(low_ref[...])
            w_load.wait()
            mixed_x.wait_recv()
            rows = mixed_land[...]
            total = None
            for h in range(narrow):
                act, slope = gelu_parts(nn(rows, up_down[0, h]))
                act_ref[h] = act.astype(bf16)
                slope_ref[h] = slope.astype(bf16)
                part = nn(act_ref[h], up_down[1, h])
                total = part if total is None else total + part
            eo_src[...] = total.astype(bf16)
            eo_x.start()
            gexp_x.wait_recv()
            total = None
            for h in range(narrow):
                pre = nt(gexp_land[...], up_down[1, h]) * slope_ref[h].astype(f32)
                pre_ref[h] = pre.astype(bf16)
                part = nt(pre_ref[h], up_down[0, h])
                total = part if total is None else total + part
            gm_src[...] = total.astype(bf16)
            gm_x.start()
            rows_t = jnp.transpose(rows)
            for h in range(narrow):
                grad_src[0, h] = nn(rows_t, pre_ref[h]).astype(bf16)
            sum_row[0].start()
            for h in range(narrow):
                grad_src[1, h] = tn(act_ref[h], gexp_land[...]).astype(bf16)
            sum_row[1].start()

        part_shape = weight_in.shape[1:]
        pl.run_scoped(
            experts_of,
            pltpu.VMEM(weight_in.shape, bf16),
            pltpu.VMEM(part_shape, bf16),
            pltpu.VMEM(part_shape, bf16),
            pltpu.VMEM(part_shape, bf16),
        )

        def come_back(gw_ref, gl_ref):
            chunk = min(512, tokens)
            seq_chunk = chunk // pos_dev
            eo_x.wait_recv()

            def out_rows(c, carry):
                rows = rows_of(c, 1, chunk)
                got = x_ref[rows, :].astype(f32) + nn(low_t[rows, :], eo_land[...])
                out_ref[pl.ds(c * seq_chunk, seq_chunk)] = got.astype(bf16).reshape(
                    seq_chunk, pos_dev, features
                )
                return carry

            lax.fori_loop(0, tokens // chunk, out_rows, 0)
            gw_ref[...] = nt(eo_land[...], g_ref[...])
            gm_x.wait_recv()
            gw_ref[...] += nt(gm_land[...], normed_ref[...])
            mix_weights_back(experts, cells, weight_ref, gw_ref, gl_ref)
            g_logit = gl_ref[...].astype(bf16)
            small_ref[:experts, :] = nn(g_logit, normed_ref[...])
            small_ref[experts:, :] = jnp.zeros((small_ref.shape[0] - experts, features), f32)

            def back_rows(c, carry):
                rows = rows_of(c, 1, chunk)
                unit, scaling = unit_of(x_ref[rows, :].astype(f32))
                g_l = gl_ref[:, rows].astype(bf16)
                g_normed = nn(low_t[rows, :], gm_land[...]) + tn(g_l, router_ref[...])
                small_ref[experts : experts + 1, :] += jnp.sum(
                    g_normed * unit, axis=0, keepdims=True
                )
                got = g_ref[rows, :].astype(f32) + unit_back(g_normed, unit, scaling, gain_two[...])
                gh_ref[pl.ds(c * seq_chunk, seq_chunk)] = got.astype(bf16).reshape(
                    seq_chunk, pos_dev, features
                )
                return carry

            lax.fori_loop(0, tokens // chunk, back_rows, 0)

        pl.run_scoped(
            come_back,
            pltpu.VMEM((experts * cells, tokens), f32),
            pltpu.VMEM((experts, tokens), f32),
        )

    pl.run_scoped(
        mixture,
        pltpu.VMEM((tokens, features), bf16),
        pltpu.VMEM((tokens, features), bf16),
        pltpu.VMEM((tokens, features), bf16),
        pltpu.VMEM((experts * cells, tokens), f32),
        pltpu.VMEM((experts * cells, tokens), bf16),
        pltpu.VMEM((tokens, experts * cells), bf16),
        pltpu.VMEM((experts, tokens), f32),
    )
    dh_x[0].start()
    out_x.start()

    def sum_rows():
        for t in range(2):
            sum_row[t].wait_recv()
            for h in range(narrow):
                total = grad_src[t, h, mine, :].astype(f32)
                for k in range(1, row_count):
                    total = total + sum_land[lax.rem(row + k, row_count), t, h].astype(f32)
                sum_src[t, h] = total.astype(bf16)
            sum_z[t].start()

    def attention(x_ref, wall_ref, qkv_ref, att_ref, x_n, x_nt, dh_t, gn_acc, gw_acc, dq_acc, dproj_ref):
        loads = [
            pltpu.make_async_copy(source, target, load_sem.at[3 + i])
            for i, (source, target) in enumerate(
                ((x_in, x_ref), (wall_in, wall_ref), (qkv_in, qkv_ref), (att_in, att_ref))
            )
        ]
        for c in loads:
            c.start()
        for c in loads:
            c.wait()

        def finished(n):
            part = gw_acc[n].astype(bf16)
            gw_src[n] = part.reshape(gw_src.shape[1:])
            wall_twin(n).start()

        for s in range(seqs):
            unit, _ = unit_of(x_ref[s].astype(f32))
            x_n[...] = (unit * gain_one[...]).astype(bf16)
            x_nt[...] = jnp.transpose(x_n[...])
            gn_acc[...] = jnp.zeros_like(gn_acc)
            dh_x[s].wait_recv()
            if s + 1 < seqs:
                dh_x[s + 1].start()
            dh_t[...] = jnp.transpose(dh_ref[s])

            def pairs_of(low, high, s=s):
                attend_back_pairs(
                    block, s, s == seqs - 1, low, high, start_ref, lse_ref, x_n, x_nt, dh_ref, dh_t, wall_ref, qkv_ref, att_ref, dq_acc, dproj_ref, gn_acc, gw_acc, finished
                )

            pairs_of(0, pairs // 2)
            if s == 0:
                sum_rows()
            elif s == 1:
                for t in range(2):
                    sum_z[t].wait_recv()
                    full_row[t].start()
            pairs_of(pairs // 2, pairs)
            unit, scaling = unit_of(x_ref[s].astype(f32))
            grad = gn_acc[...]
            small_ref[experts + 1 : experts + 2, :] += jnp.sum(grad * unit, axis=0, keepdims=True)
            got = dh_ref[s].astype(f32) + unit_back(grad, unit, scaling, gain_one[...])
            gx_ref[s] = got.astype(bf16)
            gx_x[s].start()

    pl.run_scoped(
        attention,
        pltpu.VMEM(x_in.shape, bf16),
        pltpu.VMEM(wall_in.shape, bf16),
        pltpu.VMEM(qkv_in.shape, bf16),
        pltpu.VMEM(att_in.shape, bf16),
        pltpu.VMEM((length, features), bf16),
        pltpu.VMEM((features, length), bf16),
        pltpu.VMEM((features, length), bf16),
        pltpu.VMEM((length, features), f32),
        pltpu.VMEM((pairs, features, 4 * PAIR), f32),
        pltpu.VMEM((length, PAIR), f32),
        pltpu.VMEM((length, 3 * PAIR), bf16),
    )
    small_wide.start()
    for n in range(pairs):
        wall_twin(n).wait_recv()
        total = gw_src[n, :, twin].astype(f32)
        for k in range(1, twins):
            total = total + gw_twin[lax.rem(twin + k, twins), n].astype(f32)
        gw_half[n] = total.astype(bf16)
    wall_row.start()
    small_wide.wait_recv()
    small_w[w] = small_ref[...]
    total = small_w[0]
    for j in range(1, wide):
        total = total + small_w[j]
    small_mid[...] = total
    small_narrow.start()
    wall_row.wait_recv()
    total = gw_half[:, row].astype(f32)
    for k in range(1, row_count):
        total = total + gw_row[lax.rem(row + k, row_count)].astype(f32)
    gw_z_src[...] = total.astype(bf16)
    wall_z.start()
    small_narrow.wait_recv()
    small_z[z] = small_mid[...]
    total = small_z[0]
    for j in range(1, narrow):
        total = total + small_z[j]
    small_out[...] = total
    wall_z.wait_recv()
    total = gw_z_src[z].astype(f32)
    for k in range(1, narrow):
        total = total + gw_z[lax.rem(z + k, narrow)].astype(f32)
    gw_last[...] = total.astype(bf16)
    wall_full.start()
    for t in range(2):
        full_row[t].wait_recv()
        full_twin[t].start()
    for e in (mixed_x, gexp_x, eo_x, gm_x, out_x, *sum_row, *sum_z, *dh_x):
        e.wait_send()
    for n in range(pairs):
        wall_twin(n).wait_send()
    for e in (wall_row, wall_z, small_wide, small_narrow, *full_row):
        e.wait_send()
    out_x.wait_recv()
    for e in (*gx_x, wall_full, *full_twin):
        e.wait_recv()
        e.wait_send()


def backward(x_mix, g_mix, weights, x_seq, wall, qkv, att, key_row, start_row, lse, gain_one, gain_two, router, home, sizes):
    narrow, wide, twins = sizes
    seq_total, pos_dev, features = x_mix.shape
    seqs, length, _ = x_seq.shape
    pairs, experts = narrow, router.shape[0]
    row_count = wide // twins
    tokens = seq_total * pos_dev
    _, _, hidden_rows, columns = weights.shape
    part_rows = hidden_rows // row_count
    wall_rows = features // wide
    cells = pos_dev * key_row[1]
    bases, used = plan(back_kinds(seqs, pairs), sizes)
    dma = pltpu.SemaphoreType.DMA
    rows = (experts * cells, features)
    vm = pltpu.VMEM
    return pl.pallas_call(
        functools.partial(backward_body, sizes, min(256, length), bases),
        out_shape=[
            jax.ShapeDtypeStruct(home, bf16),
            jax.ShapeDtypeStruct(home, bf16),
            jax.ShapeDtypeStruct((2, narrow, twins, hidden_rows, columns), bf16),
            jax.ShapeDtypeStruct((features, 4 * PAIR), bf16),
            jax.ShapeDtypeStruct((2 * experts, features), f32),
        ],
        in_specs=[whole(pl.ANY)] * 7 + [whole()] * 6,
        out_specs=[whole(pl.ANY)] * 4 + [whole()],
        scratch_shapes=[vm(rows, bf16)] * 8
        + [
            vm((2, narrow, hidden_rows, columns), bf16),
            vm((row_count, 2, narrow, part_rows, columns), bf16),
            vm((2, narrow, part_rows, columns), bf16),
            vm(x_mix.shape, bf16),
            vm(x_mix.shape, bf16),
            vm(x_seq.shape, bf16),
            vm(x_seq.shape, bf16),
            vm((pairs, row_count, twins, wall_rows, 4 * PAIR), bf16),
            vm((twins, pairs, row_count, wall_rows, 4 * PAIR), bf16),
            vm((pairs, row_count, wall_rows, 4 * PAIR), bf16),
            vm((row_count, pairs, wall_rows, 4 * PAIR), bf16),
            vm((pairs, wall_rows, 4 * PAIR), bf16),
            vm((narrow, wall_rows, 4 * PAIR), bf16),
            vm((wall_rows, 4 * PAIR), bf16),
            vm((2 * experts, features), f32),
            vm((wide, 2 * experts, features), f32),
            vm((2 * experts, features), f32),
            vm((narrow, 2 * experts, features), f32),
            dma((used,)),
            dma((used,)),
            dma((8 + 2 * seqs,)),
            dma((7,)),
        ],
        compiler_params=pltpu.CompilerParams(
            collective_id=2, has_side_effects=True, vmem_limit_bytes=VMEM_LIMIT
        ),
    )(
        x_mix.reshape(tokens, features),
        g_mix.reshape(tokens, features),
        weights,
        x_seq,
        wall,
        qkv,
        att,
        key_row[0],
        start_row,
        lse,
        gain_one,
        gain_two,
        router,
    )


def per_device(
    inputs,
    positions,
    members_index,
    members_mask,
    gain_attn,
    input_projection_weight,
    output_projection_weight,
    gain_mixer,
    weight_router,
    weight_up,
    weight_down,
    cotangent,
):
    narrow, wide = lax.axis_size("narrow"), lax.axis_size("wide")
    w, z = lax.axis_index("wide"), lax.axis_index("narrow")
    seq_dev, local_len, features = inputs.shape
    length = positions.shape[1]
    groups = members_index.shape[1]
    experts = weight_up.shape[0]
    own_seqs = seq_dev // narrow
    pos_dev = local_len // wide
    seq_total = seq_dev * wide
    sizes = (narrow, wide, experts // narrow)

    wall_own = jnp.concatenate(
        [
            input_projection_weight.reshape(features, -1),
            jnp.transpose(output_projection_weight),
        ],
        axis=1,
    )
    row_pos = lax.dynamic_slice_in_dim(positions, z * own_seqs, own_seqs, 0)
    starts = jnp.arange(length, dtype=jnp.int32)[None, :] - row_pos
    offset_rows = w * pos_dev
    index_rows = lax.dynamic_slice_in_dim(members_index, offset_rows, pos_dev, 0)
    live = lax.dynamic_slice_in_dim(members_mask, offset_rows, pos_dev, 0) > 0
    named = (
        index_rows[..., None] == jnp.arange(seq_total, dtype=jnp.int32)[None, None, None, :]
    ) & live[..., None]
    group_of = jnp.max(
        jnp.where(named, jnp.arange(groups, dtype=jnp.int32)[None, :, None, None], 0), axis=(1, 2)
    )
    key_row = group_of + groups * jnp.arange(pos_dev, dtype=jnp.int32)[:, None]
    key_row = jnp.transpose(key_row).reshape(1, seq_total * pos_dev)

    gain_one, gain_two = gain_attn.reshape(1, features), gain_mixer.reshape(1, features)
    router = jnp.transpose(weight_router)
    x_mix, g_mix, weights, x_seq, wall, qkv, att, lse = forward(
        inputs, cotangent, wall_own, weight_up, weight_down, starts[:, :, None], gain_one, sizes
    )
    outputs, gx, full, g_wall, small = backward(
        x_mix,
        g_mix,
        weights,
        x_seq,
        wall,
        qkv,
        att,
        (key_row, groups),
        starts[:, None, :],
        lse,
        gain_one,
        gain_two,
        router,
        inputs.shape,
        sizes,
    )
    full = full.reshape((2, experts) + full.shape[3:]).astype(f32)
    g_wall = g_wall.astype(f32)
    return (
        outputs,
        gx.astype(f32),
        small[experts + 1],
        g_wall[:, : 3 * PAIR].reshape(input_projection_weight.shape),
        jnp.transpose(g_wall[:, 3 * PAIR :]),
        small[experts],
        jnp.transpose(small[:experts]),
        full[0],
        full[1],
    )


def solution(mesh):
    in_specs = (
        P("wide", "narrow", None),
        P("wide", None),
        P("narrow", None, None),
        P("narrow", None, None),
        P(),
        P(None, None, "narrow"),
        P("narrow", None),
        P(),
        P(),
        P(None, None, "narrow"),
        P(None, "narrow", None),
        P("wide", "narrow", None),
    )
    out_specs = (
        P("wide", "narrow", None),
        P("wide", "narrow", None),
        P(),
        P(None, None, "narrow"),
        P("narrow", None),
        P(),
        P(),
        P(None, None, "narrow"),
        P(None, "narrow", None),
    )
    return jax.shard_map(
        per_device, mesh=mesh, in_specs=in_specs, out_specs=out_specs, check_vma=False
    )
```

```python
import functools
import math

import jax
import jax.numpy as jnp
from jax import lax
from jax.experimental import pallas as pl
from jax.experimental.pallas import tpu as pltpu
from jax.sharding import PartitionSpec as P

MESH = pl.DeviceIdType.MESH
HEAD_DIM = 64
PAIR = 2 * HEAD_DIM
EPS = 1e-06
NEG = -1e30
bf16 = jnp.bfloat16
f32 = jnp.float32
VMEM_LIMIT = 60 << 20


def nn(a, b):
    return lax.dot_general(a, b, (((1,), (0,)), ((), ())), preferred_element_type=f32)


def nt(a, b):
    return lax.dot_general(a, b, (((1,), (1,)), ((), ())), preferred_element_type=f32)


def tn(a, b):
    return lax.dot_general(a, b, (((0,), (0,)), ((), ())), preferred_element_type=f32)


def whole(memory=pltpu.VMEM):
    return pl.BlockSpec(memory_space=memory)


def rows_of(first, count, size):
    return pl.ds(pl.multiple_of(first * size, size), count * size)


def peers(kind, sizes):
    narrow, wide, twins = sizes
    w, z = lax.axis_index("wide"), lax.axis_index("narrow")
    first = (w // twins) * twins
    if kind == "narrow":
        return z, narrow, lambda j: (w, j)
    if kind == "wide":
        return w, wide, lambda j: (j, z)
    if kind == "twin":
        return w - first, twins, lambda j: (first + j, z)
    if kind == "row":
        return w // twins, wide // twins, lambda j: (j * twins + w - first, z)
    if kind in ("x", "y"):
        side = math.isqrt(wide // twins)
        row = w // twins
        line, place = lax.rem(row, side), row // side
        if kind == "x":
            return line, side, lambda j: ((place * side + j) * twins + w - first, z)
        return place, side, lambda j: ((j * side + line) * twins + w - first, z)
    if kind == "column":
        return (
            z * twins + w - first,
            narrow * twins,
            lambda j: (first + lax.rem(j, twins), j // twins),
        )
    return w * narrow + z, wide * narrow, lambda j: (j // narrow, lax.rem(j, narrow))


def group_size(kind, sizes):
    narrow, wide, twins = sizes
    return {
        "narrow": narrow,
        "wide": wide,
        "twin": twins,
        "row": wide // twins,
        "x": math.isqrt(wide // twins),
        "y": math.isqrt(wide // twins),
        "column": narrow * twins,
        "all": wide * narrow,
    }[kind]


def plan(kinds, sizes):
    bases, used = {}, 0
    for name, kind in kinds.items():
        bases[name] = used
        used += group_size(kind, sizes)
    return bases, used


class Exchange:
    def __init__(self, kind, sizes, source_at, target_at, sems, base, own=None, slots=False):
        self.slots = slots
        self.me, self.total, self.place = peers(kind, sizes)
        self.source_at, self.target_at = source_at, target_at
        (self.send, self.recv, self.local), self.base, self.own = sems, base, own

    def copy_of(self, k):
        j = lax.rem(self.me + k, self.total)
        return pltpu.make_async_remote_copy(
            src_ref=self.source_at(j),
            dst_ref=self.target_at(k - 1 if self.slots else self.me),
            send_sem=self.send.at[self.base + k],
            recv_sem=self.recv.at[self.base + k],
            device_id=self.place(j),
            device_id_type=MESH,
        )

    def each(self, action):
        def step(k, carry):
            action(self.copy_of(k))
            return carry

        lax.fori_loop(1, self.total, step, 0)

    def kept(self):
        return pltpu.make_async_copy(
            self.source_at(self.me), self.target_at(self.me), self.local.at[self.own]
        )

    def start(self):
        self.each(lambda c: c.start())
        if self.own is not None:
            self.kept().start()

    def wait_recv(self):
        self.each(lambda c: c.wait_recv())
        if self.own is not None:
            self.kept().wait()

    def wait_send(self):
        self.each(lambda c: c.wait_send())


def greet(sizes):
    barrier = pltpu.get_barrier_semaphore()
    me, total, place = peers("all", sizes)

    def step(k, carry):
        pl.semaphore_signal(
            barrier, inc=1, device_id=place(lax.rem(me + k, total)), device_id_type=MESH
        )
        return carry

    lax.fori_loop(1, total, step, 0)
    pl.semaphore_wait(barrier, total - 1)


def unit_of(values):
    scaling = lax.rsqrt(jnp.mean(values * values, axis=-1, keepdims=True) + EPS)
    return values * scaling, scaling


def unit_back(grad_rows, unit_rows, scaling, gain):
    grad_unit = grad_rows * gain
    inner = jnp.mean(grad_unit * unit_rows, axis=-1, keepdims=True)
    return scaling * (grad_unit - unit_rows * inner)


def wall_of(wall_ref, n):
    part = wall_ref[n]
    return part.reshape(-1, part.shape[-1])


def attend_pairs(
    block, s, low, high, normed, start_ref, wall_ref, qkv_ref, att_ref, lse_acc, stored
):
    length = normed.shape[0]
    lane = lax.broadcasted_iota(jnp.int32, (block, PAIR), 1)

    def one_pair(n, carry):
        proj = nn(normed[...], wall_of(wall_ref, n)[:, : 3 * PAIR]).astype(bf16)
        qkv_ref[s, n] = proj
        keys, vals = proj[:, PAIR : 2 * PAIR], proj[:, 2 * PAIR :]
        for i in range(length // block):
            rows = slice(i * block, (i + 1) * block)
            end = (i + 1) * block
            query = proj[rows, :PAIR] * jnp.asarray(HEAD_DIM**-0.5, bf16)
            key_at = lax.broadcasted_iota(jnp.int32, (block, end), 1)
            row_at = i * block + lax.broadcasted_iota(jnp.int32, (block, end), 0)
            allowed = (key_at >= start_ref[s, rows, :]) & (key_at <= row_at)
            got = []
            for j in range(2):
                own = (lane // HEAD_DIM) == j
                score = nt(jnp.where(own, query, jnp.zeros_like(query)), keys[:end])
                score = jnp.where(allowed, score, NEG)
                peak = jnp.max(score, axis=1, keepdims=True)
                expo = jnp.exp(score - peak)
                total = jnp.sum(expo, axis=1, keepdims=True)
                got.append(nn(expo.astype(bf16), vals[:end]) / total)
                lse_acc[rows, :] = jnp.where(
                    lane == 2 * n + j, peak + jnp.log(total), lse_acc[rows, :]
                )
            att_ref[s, n, rows, :] = jnp.where(lane < HEAD_DIM, got[0], got[1]).astype(bf16)
        stored(s, n)
        return carry

    lax.fori_loop(low, high, one_pair, 0)


def forward_kinds(seqs):
    kinds = {"wall": "narrow", "wall_row": "row", "wall_twin": "twin", "cot": "wide"}
    for t in range(2):
        kinds[f"weight{t}"] = "narrow"
        kinds[f"weight_a{t}"], kinds[f"weight_b{t}"] = ("x", "y") if t == 0 else ("y", "x")
    for s in range(seqs):
        kinds[f"x{s}"], kinds[f"hid{s}"] = "narrow", "all"
    return kinds


def forward_body(
    sizes,
    block,
    bases,
    inputs_ref,
    cot_ref,
    up_ref,
    down_ref,
    in_ref,
    outproj_ref,
    pos_ref,
    gain_ref,
    xmix_ref,
    gmix_ref,
    weight_ref,
    x_out,
    wall_out,
    qkv_out,
    att_out,
    lse_ref,
    x_ref,
    wall_ref,
    qkv_ref,
    att_ref,
    hid_ref,
    normed_ref,
    lse_acc,
    wall_own_ref,
    start_ref,
    send,
    recv,
    local,
    out_sem,
):
    narrow, wide, twins = sizes
    w, z = lax.axis_index("wide"), lax.axis_index("narrow")
    seqs, length, features = x_ref.shape
    seq_dev, local_len, _ = inputs_ref.shape
    pos_dev = local_len // wide
    pairs = wall_ref.shape[0]
    row, twin = w // twins, lax.rem(w, twins)
    wall_rows = features // wide
    side = weight_ref.shape[2]
    row_y, row_x = row // side, lax.rem(row, side)
    weight_rows = weight_ref.shape[4]
    sems = (send, recv, local)

    def exchange(name, kind, source_at, target_at, own=None):
        return Exchange(kind, sizes, source_at, target_at, sems, bases[name], own)

    for c in range(3):
        wall_own_ref[:, c * PAIR : (c + 1) * PAIR] = in_ref[c]
    wall_own_ref[:, 3 * PAIR :] = jnp.transpose(outproj_ref[...])
    greet(sizes)
    wall = exchange(
        "wall",
        "narrow",
        lambda j: wall_own_ref.at[rows_of(w, 1, wall_rows)],
        lambda j: wall_ref.at[j, row, twin],
        0,
    )
    wall_row = exchange(
        "wall_row",
        "row",
        lambda j: wall_ref.at[:, row, twin],
        lambda j: wall_ref.at[:, j, twin],
    )
    wall_twin = exchange(
        "wall_twin", "twin", lambda j: wall_ref.at[:, :, twin], lambda j: wall_ref.at[:, :, j]
    )
    cot = exchange(
        "cot",
        "wide",
        lambda j: cot_ref.at[:, rows_of(j, 1, pos_dev)],
        lambda j: gmix_ref.at[pl.ds(j * seq_dev, seq_dev)],
        1,
    )
    mine = rows_of(row, 1, weight_rows)
    weight = [
        exchange(
            f"weight{t}",
            "narrow",
            lambda j, ref=ref: ref.at[j * twins + twin, mine],
            lambda j, t=t: weight_ref.at[t, j, row_y, row_x],
            2 + t,
        )
        for t, ref in enumerate((up_ref, down_ref))
    ]
    along_x, along_y = (
        lambda j, t: weight_ref.at[t, :, row_y, j],
        lambda j, t: weight_ref.at[t, :, j, row_x],
    )
    weight_a = [
        exchange(
            f"weight_a{t}",
            "x" if t == 0 else "y",
            lambda j, t=t: weight_ref.at[t, :, row_y, row_x],
            functools.partial(along_x if t == 0 else along_y, t=t),
        )
        for t in range(2)
    ]
    line_y, line_x = (
        lambda j, t: weight_ref.at[t, :, j],
        lambda j, t: weight_ref.at[t, :, :, j],
    )
    weight_b = [
        exchange(
            f"weight_b{t}",
            "y" if t == 0 else "x",
            lambda j, t=t: line_y(row_y, t) if t == 0 else line_x(row_x, t),
            functools.partial(line_y if t == 0 else line_x, t=t),
        )
        for t in range(2)
    ]
    x_in = [
        exchange(
            f"x{s}",
            "narrow",
            lambda j, s=s: inputs_ref.at[j * seqs + s],
            lambda j, s=s: x_ref.at[s, rows_of(j, 1, local_len)],
            4 + s,
        )
        for s in range(seqs)
    ]
    hid = [
        exchange(
            f"hid{s}",
            "all",
            lambda j, s=s: hid_ref.at[
                s, rows_of(lax.rem(j, narrow) * wide + j // narrow, 1, pos_dev)
            ],
            lambda j, s=s: xmix_ref.at[j * seqs + s],
            4 + seqs + s,
        )
        for s in range(seqs)
    ]

    def kept(s, n):
        return (
            pltpu.make_async_copy(qkv_ref.at[s, n], qkv_out.at[s, n], out_sem.at[s, 2 * n]),
            pltpu.make_async_copy(att_ref.at[s, n], att_out.at[s, n], out_sem.at[s, 2 * n + 1]),
        )

    def stored(s, n):
        for c in kept(s, n):
            c.start()

    wall_keep = pltpu.make_async_copy(wall_ref, wall_out, out_sem.at[0, 2 * pairs])
    x_keep = [
        pltpu.make_async_copy(x_ref.at[s], x_out.at[s], out_sem.at[s, 2 * pairs + 1])
        for s in range(seqs)
    ]

    wall.start()
    x_in[0].start()
    wall.wait_recv()
    wall_row.start()
    wall_row.wait_recv()
    wall_twin.start()
    cot.start()
    pos_t = jnp.transpose(pos_ref[...])
    seq_at = lax.broadcasted_iota(jnp.int32, pos_t.shape, 1)
    token_at = lax.broadcasted_iota(jnp.int32, (length, 1), 0)
    for s in range(seqs):
        own = jnp.sum(jnp.where(seq_at == z * seqs + s, pos_t, 0), axis=1, keepdims=True)
        start_ref[s] = token_at - own
    wall_twin.wait_recv()
    x_in[0].wait_recv()
    weight[0].start()
    weight[1].start()
    wall_keep.start()
    for s in range(seqs):
        if s > 0:
            x_in[s].wait_recv()
        x_keep[s].start()
        normed_ref[...] = (unit_of(x_ref[s].astype(f32))[0] * gain_ref[...]).astype(bf16)

        def pairs_of(low, high, s=s):
            attend_pairs(
                block, s, low, high, normed_ref, start_ref, wall_ref, qkv_ref, att_ref, lse_acc, stored
            )

        pairs_of(0, pairs // 2)
        if s + 1 < seqs:
            x_in[s + 1].start()
        pairs_of(pairs // 2, pairs)
        hidden = x_ref[s].astype(f32)
        for n in range(pairs):
            hidden = hidden + nt(att_ref[s, n], wall_of(wall_ref, n)[:, 3 * PAIR :])
        hid_ref[s] = hidden.astype(bf16)
        hid[s].start()
        lse_ref[s] = jnp.transpose(lse_acc[...])[: 2 * pairs]
        if s == 0:
            for t in range(2):
                weight[t].wait_recv()
                weight_a[t].start()
        if s == 1:
            for t in range(2):
                weight_a[t].wait_recv()
                weight_b[t].start()
    for e in (wall, wall_row, wall_twin, cot, *weight, *weight_a, *weight_b, *x_in):
        e.wait_send()
    cot.wait_recv()
    for t in range(2):
        weight_b[t].wait_recv()
    wall_keep.wait()
    for s in range(seqs):
        x_keep[s].wait()

        def settle(n, carry, s=s):
            for c in kept(s, n):
                c.wait()
            return carry

        lax.fori_loop(0, pairs, settle, 0)
    for s in range(seqs):
        hid[s].wait_recv()
        hid[s].wait_send()


def forward(inputs, cot, up, down, in_parts, outproj, positions, gain, sizes):
    narrow, wide, twins = sizes
    seq_dev, local_len, features = inputs.shape
    seqs, length, pairs = seq_dev // narrow, local_len * narrow, narrow
    pos_dev = local_len // wide
    wall_shape = (pairs, wide // twins, twins, features // wide, 4 * PAIR)
    bases, used = plan(forward_kinds(seqs), sizes)
    dma = pltpu.SemaphoreType.DMA
    side = math.isqrt(wide // twins)
    qkv_shape = (seqs, pairs, length, 3 * PAIR)
    att_shape = (seqs, pairs, length, PAIR)
    mix_shape = (seq_dev * wide, pos_dev, features)
    return pl.pallas_call(
        functools.partial(forward_body, sizes, min(256, length), bases),
        out_shape=[
            jax.ShapeDtypeStruct(mix_shape, bf16),
            jax.ShapeDtypeStruct(mix_shape, bf16),
            jax.ShapeDtypeStruct(
                (2, narrow, side, side, up.shape[1] // side**2, up.shape[2]), bf16
            ),
            jax.ShapeDtypeStruct((seqs, length, features), bf16),
            jax.ShapeDtypeStruct(wall_shape, bf16),
            jax.ShapeDtypeStruct(qkv_shape, bf16),
            jax.ShapeDtypeStruct(att_shape, bf16),
            jax.ShapeDtypeStruct((seqs, 2 * pairs, length), f32),
        ],
        in_specs=[whole(pl.ANY)] * 4 + [whole()] * 4,
        out_specs=[whole(pl.ANY)] * 7 + [whole()],
        scratch_shapes=[
            pltpu.VMEM((seqs, length, features), bf16),
            pltpu.VMEM(wall_shape, bf16),
            pltpu.VMEM(qkv_shape, bf16),
            pltpu.VMEM(att_shape, bf16),
            pltpu.VMEM((seqs, length, features), bf16),
            pltpu.VMEM((length, features), bf16),
            pltpu.VMEM((length, PAIR), f32),
            pltpu.VMEM((features, 4 * PAIR), bf16),
            pltpu.VMEM((seqs, length, 1), jnp.int32),
            dma((used,)),
            dma((used,)),
            dma((4 + 2 * seqs,)),
            dma((seqs, 2 * pairs + 2)),
        ],
        compiler_params=pltpu.CompilerParams(
            collective_id=1, has_side_effects=True, vmem_limit_bytes=VMEM_LIMIT
        ),
    )(inputs, cot, up, down, in_parts, outproj, positions, gain)


def mix_forward(experts, cells, x_ref, key_ref, gain_ref, router_ref, normed_ref, weight_ref, low_ref, logit_ref):
    tokens = x_ref.shape[0]
    chunk = min(512, tokens)

    def norm_rows(c, carry):
        rows = rows_of(c, 1, chunk)
        unit = unit_of(x_ref[rows, :].astype(f32))[0]
        normed_ref[rows, :] = (unit * gain_ref[...]).astype(bf16)
        return carry

    lax.fori_loop(0, tokens // chunk, norm_rows, 0)
    logit_ref[...] = nt(router_ref[...], normed_ref[...])

    def one_expert(e, carry):
        cell = lax.broadcasted_iota(jnp.int32, (cells, tokens), 0)
        score = jnp.where(cell == key_ref[...], logit_ref[pl.ds(e, 1), :], NEG)
        expo = jnp.exp(score - jnp.max(score, axis=1, keepdims=True))
        weights = expo / jnp.sum(expo, axis=1, keepdims=True)
        rows = rows_of(e, 1, cells)
        weight_ref[rows, :] = weights
        low_ref[rows, :] = weights.astype(bf16)
        return carry

    lax.fori_loop(0, experts, one_expert, 0)


def gelu_parts(pre):
    square = pre * pre
    tanh = jnp.tanh(0.7978845608028654 * (pre + 0.044715 * pre * square))
    act = 0.5 * pre * (1.0 + tanh)
    slope = 0.5 * (1.0 + tanh) + 0.5 * pre * (1.0 - tanh * tanh) * (
        0.7978845608028654 * (1.0 + 3 * 0.044715 * square)
    )
    return act, slope


def mix_weights_back(experts, cells, weight_ref, gw_ref, gl_ref):
    def one_expert(e, carry):
        rows = rows_of(e, 1, cells)
        weights, grads = weight_ref[rows, :], gw_ref[rows, :]
        inner = jnp.sum(weights * grads, axis=1, keepdims=True)
        gl_ref[pl.ds(e, 1), :] = jnp.sum(weights * (grads - inner), axis=0, keepdims=True)
        return carry

    lax.fori_loop(0, experts, one_expert, 0)


def attend_back_pairs(
    block, s, start_ref, lse_ref, x_nt, dh_ref, dh_t, wall_ref, qkv_ref, att_ref, dq_acc, dproj_ref, gw_acc, hooks
):
    length = dh_ref.shape[1]
    lane = lax.broadcasted_iota(jnp.int32, (length, PAIR), 1)
    scale = jnp.asarray(HEAD_DIM**-0.5, bf16)

    def one_pair(n, carry):
        wall = wall_of(wall_ref, n)
        d_att = nn(dh_ref[s], wall[:, 3 * PAIR :]).astype(bf16)
        prod = (d_att.astype(f32) * att_ref[s, n].astype(f32)).astype(bf16)
        head_row = lax.broadcasted_iota(jnp.int32, (8, PAIR), 0)
        head_lane = lax.broadcasted_iota(jnp.int32, (8, PAIR), 1) // HEAD_DIM
        inner = nt((head_row == head_lane).astype(bf16), prod)
        query = qkv_ref[s, n, :, :PAIR] * scale
        keys, vals = qkv_ref[s, n, :, PAIR : 2 * PAIR], qkv_ref[s, n, :, 2 * PAIR :]
        keys_t = jnp.transpose(keys)
        zero = jnp.zeros_like(query)
        own = [(lane // HEAD_DIM) == j for j in range(2)]
        q_own = [jnp.where(o, query, zero) for o in own]
        d_own = [jnp.where(o, d_att, zero) for o in own]
        lse_own = [lse_ref[s, pl.ds(2 * n + j, 1), :] for j in range(2)]
        for i in range(length // block):
            rows, first = slice(i * block, (i + 1) * block), i * block
            shape = (block, length - first)
            key_at = first + lax.broadcasted_iota(jnp.int32, shape, 0)
            row_at = first + lax.broadcasted_iota(jnp.int32, shape, 1)
            allowed = (key_at >= start_ref[s, :, first:]) & (key_at <= row_at)
            dk = dv = None
            for j in range(2):
                head = slice(j * HEAD_DIM, (j + 1) * HEAD_DIM)
                score = nt(keys[rows], q_own[j][first:])
                prob = jnp.where(allowed, jnp.exp(score - lse_own[j][:, first:]), 0.0)
                d_prob = nt(vals[rows], d_own[j][first:])
                d_score = (prob * (d_prob - inner[j : j + 1, first:])).astype(bf16)
                dv_part = nn(prob.astype(bf16), d_own[j][first:])
                dk_part = nn(d_score, q_own[j][first:])
                dv = dv_part if dv is None else dv + dv_part
                dk = dk_part if dk is None else dk + dk_part
                dq_part = nn(keys_t[head, rows], d_score)
                if i == 0:
                    dq_acc[head, :] = dq_part
                else:
                    dq_acc[head, first:] += dq_part
            dproj_ref[n, rows, PAIR : 2 * PAIR] = dk.astype(bf16)
            dproj_ref[n, rows, 2 * PAIR :] = dv.astype(bf16)
        dproj_ref[n, :, :PAIR] = jnp.transpose((dq_acc[...] * HEAD_DIM**-0.5).astype(bf16))
        g_in, g_out = nn(x_nt[...], dproj_ref[n]), nn(dh_t[...], att_ref[s, n])
        if s == 0:
            gw_acc[n, :, : 3 * PAIR] = g_in
            gw_acc[n, :, 3 * PAIR :] = g_out
        else:
            gw_acc[n, :, : 3 * PAIR] += g_in
            gw_acc[n, :, 3 * PAIR :] += g_out
        hooks(n)
        return carry

    lax.fori_loop(0, wall_ref.shape[0], one_pair, 0)


def back_kinds(seqs, pairs):
    kinds = {name: "column" for name in ("mixed", "gexp", "eo", "gm")}
    kinds["out"] = "wide"
    for t in range(2):
        first, second = ("x", "y") if t == 0 else ("y", "x")
        kinds[f"sum_a{t}"], kinds[f"sum_b{t}"], kinds[f"sum_z{t}"] = first, second, "narrow"
        kinds[f"full_a{t}"], kinds[f"full_b{t}"], kinds[f"full_twin{t}"] = first, second, "twin"
    for s in range(seqs):
        kinds[f"dh{s}"], kinds[f"gx{s}"] = "all", "narrow"
    for n in range(pairs):
        kinds[f"wall_twin{n}"] = "twin"
    for n in range(pairs):
        kinds[f"wall_row{n}"] = "row"
    kinds["wall_z"], kinds["wall_full"] = "narrow", "wide"
    kinds["small_w"], kinds["small_z"] = "wide", "narrow"
    return kinds


def backward_body(
    sizes,
    block,
    bases,
    xmix_in,
    gmix_in,
    weight_in,
    x_in,
    wall_in,
    qkv_in,
    att_in,
    key_ref,
    start_ref,
    lse_ref,
    gain_one,
    gain_two,
    router_ref,
    out_home,
    gx_home,
    full_up,
    full_down,
    wall_out,
    small_out,
    mixed_src,
    gexp_src,
    eo_src,
    gm_src,
    mixed_land,
    gexp_land,
    eo_land,
    gm_land,
    grad_src,
    land_a,
    sum_mid,
    land_b,
    sum_src,
    gh_ref,
    out_ref,
    dh_ref,
    gx_ref,
    gw_src,
    gw_twin,
    gw_half,
    gw_row,
    gw_z_src,
    gw_z,
    gw_last,
    small_ref,
    small_w,
    small_mid,
    small_z,
    send,
    recv,
    local,
    load_sem,
):
    narrow, wide, twins = sizes
    w, z = lax.axis_index("wide"), lax.axis_index("narrow")
    row, twin = w // twins, lax.rem(w, twins)
    row_count = wide // twins
    seqs, length, features = dh_ref.shape
    seq_total, pos_dev, _ = gh_ref.shape
    tokens = seq_total * pos_dev
    seq_dev, local_len, _ = out_home.shape
    experts = router_ref.shape[0]
    cells = mixed_src.shape[0] // experts
    pairs = gw_src.shape[0]
    side = grad_src.shape[2]
    row_y, row_x = row // side, lax.rem(row, side)
    wall_rows = gw_last.shape[0]
    sems = (send, recv, local)
    owns = iter(range(local.shape[0]))

    def exchange(name, kind, source_at, target_at, own=False, slots=False):
        return Exchange(
            kind, sizes, source_at, target_at, sems, bases[name], next(owns) if own else None, slots
        )

    def column(name, source, target):
        return exchange(
            name,
            "column",
            lambda j: source.at[rows_of(j, 1, cells)],
            lambda j: target.at[rows_of(j, 1, cells)],
            True,
        )

    mixed_x = column("mixed", mixed_src, mixed_land)
    gexp_x = column("gexp", gexp_src, gexp_land)
    eo_x = column("eo", eo_src, eo_land)
    gm_x = column("gm", gm_src, gm_land)
    out_x = exchange(
        "out",
        "wide",
        lambda j: out_ref.at[pl.ds(j * seq_dev, seq_dev)],
        lambda j: out_home.at[:, rows_of(j, 1, pos_dev)],
        True,
    )
    first_kind, second_kind = ("x", "y"), ("y", "x")
    full_ref = (full_up, full_down)

    def line_of(ref, t, j, along):
        return ref.at[t, :, :, j] if along == "x" else ref.at[t, :, j]

    sum_a = [
        exchange(
            f"sum_a{t}",
            first_kind[t],
            lambda j, t=t: line_of(grad_src, t, j, first_kind[t]),
            lambda k, t=t: land_a.at[k, t],
            slots=True,
        )
        for t in range(2)
    ]
    sum_b = [
        exchange(
            f"sum_b{t}",
            second_kind[t],
            lambda j, t=t: sum_mid.at[t, :, j],
            lambda k, t=t: land_b.at[k, t],
            slots=True,
        )
        for t in range(2)
    ]
    sum_z = [
        exchange(
            f"sum_z{t}",
            "narrow",
            lambda j, t=t: sum_src.at[t, j],
            lambda j, t=t: full_ref[t].at[j, twin, row_y, row_x],
            True,
        )
        for t in range(2)
    ]
    full_a = [
        exchange(
            f"full_a{t}",
            first_kind[t],
            lambda j, t=t: full_ref[t].at[:, twin, row_y, row_x],
            lambda j, t=t: (
                full_ref[t].at[:, twin, row_y, j]
                if first_kind[t] == "x"
                else full_ref[t].at[:, twin, j, row_x]
            ),
        )
        for t in range(2)
    ]

    def full_line(j, along, t):
        return full_ref[t].at[:, twin, j] if along == "y" else full_ref[t].at[:, twin, :, j]

    full_b = [
        exchange(
            f"full_b{t}",
            second_kind[t],
            lambda j, t=t: full_line(
                row_y if second_kind[t] == "y" else row_x, second_kind[t], t
            ),
            lambda j, t=t: full_line(j, second_kind[t], t),
        )
        for t in range(2)
    ]
    full_twin = [
        exchange(
            f"full_twin{t}",
            "twin",
            lambda j, t=t: full_ref[t].at[:, twin],
            lambda j, t=t: full_ref[t].at[:, j],
        )
        for t in range(2)
    ]
    dh_x = [
        exchange(
            f"dh{s}",
            "all",
            lambda j, s=s: gh_ref.at[j * seqs + s],
            lambda j, s=s: dh_ref.at[
                s, rows_of(lax.rem(j, narrow) * wide + j // narrow, 1, pos_dev)
            ],
            True,
        )
        for s in range(seqs)
    ]
    gx_x = [
        exchange(
            f"gx{s}",
            "narrow",
            lambda j, s=s: gx_ref.at[s, rows_of(j, 1, local_len)],
            lambda j, s=s: gx_home.at[j * seqs + s],
            True,
        )
        for s in range(seqs)
    ]

    def wall_twin(n):
        e = exchange(
            "wall_twin0",
            "twin",
            lambda j: gw_src.at[n, :, j],
            lambda k: gw_twin.at[k, n],
            slots=True,
        )
        e.base = bases["wall_twin0"] + n * twins
        return e

    def wall_row(n):
        e = exchange(
            "wall_row0", "row", lambda j: gw_half.at[n, j], lambda k: gw_row.at[k, n], slots=True
        )
        e.base = bases["wall_row0"] + n * row_count
        return e

    wall_z = exchange(
        "wall_z", "narrow", lambda j: gw_z_src.at[j], lambda k: gw_z.at[k], slots=True
    )
    wall_full = exchange(
        "wall_full",
        "wide",
        lambda j: gw_last,
        lambda j: wall_out.at[rows_of(j, 1, wall_rows)],
        True,
    )
    small_wide = exchange("small_w", "wide", lambda j: small_ref, lambda j: small_w.at[j])
    small_narrow = exchange("small_z", "narrow", lambda j: small_mid, lambda j: small_z.at[j])

    greet(sizes)

    def mixture(x_ref, g_ref, normed_ref, weight_ref, low_ref, low_t, logit_ref):
        x_load = pltpu.make_async_copy(xmix_in, x_ref, load_sem.at[0])
        g_load = pltpu.make_async_copy(gmix_in, g_ref, load_sem.at[1])
        x_load.start()
        g_load.start()

        def experts_of(up_down, act_ref, slope_ref, pre_ref):
            w_load = pltpu.make_async_copy(weight_in, up_down, load_sem.at[2])

            def weight_of(t, h):
                return up_down[t, h].reshape(-1, up_down.shape[-1])

            w_load.start()
            x_load.wait()
            mix_forward(
                experts, cells, x_ref, key_ref, gain_two, router_ref, normed_ref, weight_ref, low_ref, logit_ref
            )
            mixed_src[...] = nn(low_ref[...], normed_ref[...]).astype(bf16)
            mixed_x.start()
            g_load.wait()
            gexp_src[...] = nn(low_ref[...], g_ref[...]).astype(bf16)
            gexp_x.start()
            low_t[...] = jnp.transpose(low_ref[...])
            w_load.wait()
            mixed_x.wait_recv()
            rows = mixed_land[...]
            total = None
            for h in range(narrow):
                act, slope = gelu_parts(nn(rows, weight_of(0, h)))
                act_ref[h] = act.astype(bf16)
                slope_ref[h] = slope.astype(bf16)
                part = nn(act_ref[h], weight_of(1, h))
                total = part if total is None else total + part
            eo_src[...] = total.astype(bf16)
            eo_x.start()
            gexp_x.wait_recv()
            total = None
            for h in range(narrow):
                pre = nt(gexp_land[...], weight_of(1, h)) * slope_ref[h].astype(f32)
                pre_ref[h] = pre.astype(bf16)
                part = nt(pre_ref[h], weight_of(0, h))
                total = part if total is None else total + part
            gm_src[...] = total.astype(bf16)
            gm_x.start()
            rows_t = jnp.transpose(rows)
            for h in range(narrow):
                grad_src[0, h] = nn(rows_t, pre_ref[h]).astype(bf16).reshape(grad_src.shape[2:])
            sum_a[0].start()
            for h in range(narrow):
                grad_src[1, h] = (
                    tn(act_ref[h], gexp_land[...]).astype(bf16).reshape(grad_src.shape[2:])
                )
            sum_a[1].start()

        part_shape = (narrow, experts * cells, weight_in.shape[-1])
        pl.run_scoped(
            experts_of,
            pltpu.VMEM(weight_in.shape, bf16),
            pltpu.VMEM(part_shape, bf16),
            pltpu.VMEM(part_shape, bf16),
            pltpu.VMEM(part_shape, bf16),
        )

        def come_back(gw_ref, gl_ref):
            chunk = min(512, tokens)
            seq_chunk = chunk // pos_dev
            eo_x.wait_recv()

            def out_rows(c, carry):
                rows = rows_of(c, 1, chunk)
                got = x_ref[rows, :].astype(f32) + nn(low_t[rows, :], eo_land[...])
                out_ref[pl.ds(c * seq_chunk, seq_chunk)] = got.astype(bf16).reshape(
                    seq_chunk, pos_dev, features
                )
                return carry

            lax.fori_loop(0, tokens // chunk, out_rows, 0)
            gw_ref[...] = nt(eo_land[...], g_ref[...])
            gm_x.wait_recv()
            gw_ref[...] += nt(gm_land[...], normed_ref[...])
            mix_weights_back(experts, cells, weight_ref, gw_ref, gl_ref)
            g_logit = gl_ref[...].astype(bf16)
            small_ref[:experts, :] = nn(g_logit, normed_ref[...])
            small_ref[experts:, :] = jnp.zeros((small_ref.shape[0] - experts, features), f32)

            def back_rows(c, carry):
                rows = rows_of(c, 1, chunk)
                unit, scaling = unit_of(x_ref[rows, :].astype(f32))
                g_l = gl_ref[:, rows].astype(bf16)
                g_normed = nn(low_t[rows, :], gm_land[...]) + tn(g_l, router_ref[...])
                small_ref[experts : experts + 1, :] += jnp.sum(
                    g_normed * unit, axis=0, keepdims=True
                )
                got = g_ref[rows, :].astype(f32) + unit_back(g_normed, unit, scaling, gain_two[...])
                gh_ref[pl.ds(c * seq_chunk, seq_chunk)] = got.astype(bf16).reshape(
                    seq_chunk, pos_dev, features
                )
                return carry

            lax.fori_loop(0, tokens // chunk, back_rows, 0)

        pl.run_scoped(
            come_back,
            pltpu.VMEM((experts * cells, tokens), f32),
            pltpu.VMEM((experts, tokens), f32),
        )

    pl.run_scoped(
        mixture,
        pltpu.VMEM((tokens, features), bf16),
        pltpu.VMEM((tokens, features), bf16),
        pltpu.VMEM((tokens, features), bf16),
        pltpu.VMEM((experts * cells, tokens), f32),
        pltpu.VMEM((experts * cells, tokens), bf16),
        pltpu.VMEM((tokens, experts * cells), bf16),
        pltpu.VMEM((experts, tokens), f32),
    )
    dh_x[0].start()

    def sum_first():
        for t in range(2):
            sum_a[t].wait_recv()
            for h in range(narrow):
                if first_kind[t] == "x":
                    total = grad_src[t, h, :, row_x].astype(f32)
                else:
                    total = grad_src[t, h, row_y].astype(f32)
                for k in range(side - 1):
                    total = total + land_a[k, t, h].astype(f32)
                sum_mid[t, h] = total.astype(bf16)
            sum_b[t].start()

    def sum_second():
        for t in range(2):
            place = row_y if second_kind[t] == "y" else row_x
            sum_b[t].wait_recv()
            for h in range(narrow):
                total = sum_mid[t, h, place].astype(f32)
                for k in range(side - 1):
                    total = total + land_b[k, t, h].astype(f32)
                sum_src[t, h] = total.astype(bf16)
            sum_z[t].start()

    def spread_first():
        for t in range(2):
            sum_z[t].wait_recv()
            full_a[t].start()

    def spread_second():
        for t in range(2):
            full_a[t].wait_recv()
            full_b[t].start()

    def spread_third():
        for t in range(2):
            full_b[t].wait_recv()
            full_twin[t].start()

    def wall_halves(n):
        wall_twin(n).wait_recv()
        total = gw_src[n, :, twin].astype(f32)
        for k in range(twins - 1):
            total = total + gw_twin[k, n].astype(f32)
        gw_half[n] = total.astype(bf16)
        wall_row(n).start()

    def attention(x_ref, wall_ref, qkv_ref, att_ref, x_nt, dh_t, gw_acc, dq_acc, dproj_ref):
        loads = [
            pltpu.make_async_copy(source, target, load_sem.at[3 + i])
            for i, (source, target) in enumerate(
                ((x_in, x_ref), (wall_in, wall_ref), (qkv_in, qkv_ref), (att_in, att_ref))
            )
        ]
        for c in loads:
            c.start()
        sum_first()
        for c in loads:
            c.wait()

        def finished(n):
            part = gw_acc[n].astype(bf16)
            gw_src[n] = part.reshape(gw_src.shape[1:])
            wall_twin(n).start()

            @pl.when(n > 0)
            def _():
                wall_halves(n - 1)

        def hooks_of(s):
            steps = {}
            if s == 0:
                steps[0] = (sum_second, out_x.start)
            elif s == 1:
                steps[0] = (spread_first,)
                steps[pairs - 1] = (spread_second,)

            def hooks(n):
                if s == seqs - 1:
                    finished(n)
                for at, actions in steps.items():

                    @pl.when(n == at)
                    def _(actions=actions):
                        for action in actions:
                            action()

            return hooks

        def rows_back(s, k):
            j = lax.rem(z + k, narrow)
            rows = rows_of(j, 1, local_len)
            grad = nt(dproj_ref[0, rows, :], wall_of(wall_ref, 0)[:, : 3 * PAIR])
            for n in range(1, pairs):
                grad = grad + nt(dproj_ref[n, rows, :], wall_of(wall_ref, n)[:, : 3 * PAIR])
            unit, scaling = unit_of(x_ref[s, rows, :].astype(f32))
            small_ref[experts + 1 : experts + 2, :] += jnp.sum(grad * unit, axis=0, keepdims=True)
            got = dh_ref[s, rows, :].astype(f32) + unit_back(grad, unit, scaling, gain_one[...])
            gx_ref[s, rows, :] = got.astype(bf16)

        for s in range(seqs):
            unit, _ = unit_of(x_ref[s].astype(f32))
            x_nt[...] = jnp.transpose((unit * gain_one[...]).astype(bf16))
            dh_x[s].wait_recv()
            if s + 1 < seqs:
                dh_x[s + 1].start()
            dh_t[...] = jnp.transpose(dh_ref[s])
            attend_back_pairs(
                block, s, start_ref, lse_ref, x_nt, dh_ref, dh_t, wall_ref, qkv_ref, att_ref, dq_acc, dproj_ref, gw_acc, hooks_of(s)
            )

            def to_peer(k, carry, s=s):
                rows_back(s, k)
                gx_x[s].copy_of(k).start()
                return carry

            lax.fori_loop(1, narrow, to_peer, 0)
            rows_back(s, 0)
            gx_x[s].kept().start()
            if s == seqs - 1:
                wall_halves(pairs - 1)

    pl.run_scoped(
        attention,
        pltpu.VMEM(x_in.shape, bf16),
        pltpu.VMEM(wall_in.shape, bf16),
        pltpu.VMEM(qkv_in.shape, bf16),
        pltpu.VMEM(att_in.shape, bf16),
        pltpu.VMEM((features, length), bf16),
        pltpu.VMEM((features, length), bf16),
        pltpu.VMEM((pairs, features, 4 * PAIR), f32),
        pltpu.VMEM((PAIR, length), f32),
        pltpu.VMEM((pairs, length, 3 * PAIR), bf16),
    )
    small_wide.start()
    total = gw_half[:, row].astype(f32)
    for n in range(pairs):
        wall_row(n).wait_recv()
    for k in range(row_count - 1):
        total = total + gw_row[k].astype(f32)
    gw_z_src[...] = total.astype(bf16)
    wall_z.start()
    small_wide.wait_recv()
    small_w[w] = small_ref[...]
    total = small_w[0]
    for j in range(1, wide):
        total = total + small_w[j]
    small_mid[...] = total
    small_narrow.start()
    spread_third()
    wall_z.wait_recv()
    total = gw_z_src[z].astype(f32)
    for k in range(narrow - 1):
        total = total + gw_z[k].astype(f32)
    gw_last[...] = total.astype(bf16)
    wall_full.start()
    small_narrow.wait_recv()
    small_z[z] = small_mid[...]
    total = small_z[0]
    for j in range(1, narrow):
        total = total + small_z[j]
    small_out[...] = total
    for e in (mixed_x, gexp_x, eo_x, gm_x, out_x, *sum_a, *sum_b, *sum_z, *dh_x):
        e.wait_send()
    for n in range(pairs):
        wall_twin(n).wait_send()
        wall_row(n).wait_send()
    for e in (wall_z, small_wide, small_narrow, *full_a, *full_b):
        e.wait_send()
    out_x.wait_recv()
    for e in (*gx_x, wall_full, *full_twin):
        e.wait_recv()
        e.wait_send()


def backward(x_mix, g_mix, weights, x_seq, wall, qkv, att, key_row, start_row, lse, gain_one, gain_two, router, home, sizes):
    narrow, wide, twins = sizes
    seq_total, pos_dev, features = x_mix.shape
    seqs, length, _ = x_seq.shape
    pairs, experts = narrow, router.shape[0]
    row_count = wide // twins
    tokens = seq_total * pos_dev
    side, part_rows, columns = weights.shape[3:]
    wall_rows = features // wide
    cells = pos_dev * key_row[1]
    bases, used = plan(back_kinds(seqs, pairs), sizes)
    dma = pltpu.SemaphoreType.DMA
    rows = (experts * cells, features)
    vm = pltpu.VMEM
    return pl.pallas_call(
        functools.partial(backward_body, sizes, min(256, length), bases),
        out_shape=[
            jax.ShapeDtypeStruct(home, bf16),
            jax.ShapeDtypeStruct(home, bf16),
            jax.ShapeDtypeStruct((narrow, twins, side, side, part_rows, columns), bf16),
            jax.ShapeDtypeStruct((narrow, twins, side, side, part_rows, columns), bf16),
            jax.ShapeDtypeStruct((features, 4 * PAIR), bf16),
            jax.ShapeDtypeStruct((2 * experts, features), f32),
        ],
        in_specs=[whole(pl.ANY)] * 7 + [whole()] * 6,
        out_specs=[whole(pl.ANY)] * 5 + [whole()],
        scratch_shapes=[vm(rows, bf16)] * 8
        + [
            vm(weights.shape, bf16),
            vm((side - 1, 2, narrow, side, part_rows, columns), bf16),
            vm((2, narrow, side, part_rows, columns), bf16),
            vm((side - 1, 2, narrow, part_rows, columns), bf16),
            vm((2, narrow, part_rows, columns), bf16),
            vm(x_mix.shape, bf16),
            vm(x_mix.shape, bf16),
            vm(x_seq.shape, bf16),
            vm(x_seq.shape, bf16),
            vm((pairs, row_count, twins, wall_rows, 4 * PAIR), bf16),
            vm((twins - 1, pairs, row_count, wall_rows, 4 * PAIR), bf16),
            vm((pairs, row_count, wall_rows, 4 * PAIR), bf16),
            vm((row_count - 1, pairs, wall_rows, 4 * PAIR), bf16),
            vm((pairs, wall_rows, 4 * PAIR), bf16),
            vm((narrow - 1, wall_rows, 4 * PAIR), bf16),
            vm((wall_rows, 4 * PAIR), bf16),
            vm((2 * experts, features), f32),
            vm((wide, 2 * experts, features), f32),
            vm((2 * experts, features), f32),
            vm((narrow, 2 * experts, features), f32),
            dma((used,)),
            dma((used,)),
            dma((8 + 2 * seqs,)),
            dma((7,)),
        ],
        compiler_params=pltpu.CompilerParams(
            collective_id=2, has_side_effects=True, vmem_limit_bytes=VMEM_LIMIT
        ),
    )(
        x_mix.reshape(tokens, features),
        g_mix.reshape(tokens, features),
        weights,
        x_seq,
        wall,
        qkv,
        att,
        key_row[0],
        start_row,
        lse,
        gain_one,
        gain_two,
        router,
    )


def widen_body(*refs):
    half = len(refs) // 2
    for source, target in zip(refs[:half], refs[half:]):
        target[...] = source[...].astype(f32)


def widen(arrays, steps):
    flat = [a.reshape(steps, -1, a.shape[-1]) for a in arrays]
    specs = [pl.BlockSpec((1,) + a.shape[1:], lambda i: (i, 0, 0)) for a in flat]
    wide = pl.pallas_call(
        widen_body,
        grid=(steps,),
        out_shape=[jax.ShapeDtypeStruct(a.shape, f32) for a in flat],
        in_specs=specs,
        out_specs=specs,
        compiler_params=pltpu.CompilerParams(vmem_limit_bytes=VMEM_LIMIT),
    )(*flat)
    return [b.reshape(a.shape) for a, b in zip(arrays, wide)]


def per_device(
    inputs,
    positions,
    members_index,
    members_mask,
    gain_attn,
    input_projection_weight,
    output_projection_weight,
    gain_mixer,
    weight_router,
    weight_up,
    weight_down,
    cotangent,
):
    narrow, wide = lax.axis_size("narrow"), lax.axis_size("wide")
    w, z = lax.axis_index("wide"), lax.axis_index("narrow")
    seq_dev, local_len, features = inputs.shape
    length = positions.shape[1]
    groups = members_index.shape[1]
    experts = weight_up.shape[0]
    own_seqs = seq_dev // narrow
    pos_dev = local_len // wide
    seq_total = seq_dev * wide
    sizes = (narrow, wide, experts // narrow)

    row_pos = lax.dynamic_slice_in_dim(positions, z * own_seqs, own_seqs, 0)
    starts = jnp.arange(length, dtype=jnp.int32)[None, :] - row_pos
    offset_rows = w * pos_dev
    index_rows = lax.dynamic_slice_in_dim(members_index, offset_rows, pos_dev, 0)
    live = lax.dynamic_slice_in_dim(members_mask, offset_rows, pos_dev, 0) > 0
    named = (
        index_rows[..., None] == jnp.arange(seq_total, dtype=jnp.int32)[None, None, None, :]
    ) & live[..., None]
    group_of = jnp.max(
        jnp.where(named, jnp.arange(groups, dtype=jnp.int32)[None, :, None, None], 0), axis=(1, 2)
    )
    key_row = group_of + groups * jnp.arange(pos_dev, dtype=jnp.int32)[:, None]
    key_row = jnp.transpose(key_row).reshape(1, seq_total * pos_dev)

    gain_one, gain_two = gain_attn.reshape(1, features), gain_mixer.reshape(1, features)
    router = jnp.transpose(weight_router)
    x_mix, g_mix, weights, x_seq, wall, qkv, att, lse = forward(
        inputs,
        cotangent,
        weight_up,
        weight_down,
        jnp.transpose(input_projection_weight, (1, 0, 2)),
        output_projection_weight,
        positions,
        gain_one,
        sizes,
    )
    outputs, gx, full_up, full_down, g_wall, small = backward(
        x_mix,
        g_mix,
        weights,
        x_seq,
        wall,
        qkv,
        att,
        (key_row, groups),
        starts[:, None, :],
        lse,
        gain_one,
        gain_two,
        router,
        inputs.shape,
        sizes,
    )
    g_up, g_down, gx = widen(
        [full_up.reshape(weight_up.shape), full_down.reshape(weight_down.shape), gx], 8
    )
    g_wall = g_wall.astype(f32)
    return (
        outputs,
        gx,
        small[experts + 1],
        g_wall[:, : 3 * PAIR].reshape(input_projection_weight.shape),
        jnp.transpose(g_wall[:, 3 * PAIR :]),
        small[experts],
        jnp.transpose(small[:experts]),
        g_up,
        g_down,
    )


def solution(mesh):
    in_specs = (
        P("wide", "narrow", None),
        P("wide", None),
        P("narrow", None, None),
        P("narrow", None, None),
        P(),
        P(None, None, "narrow"),
        P("narrow", None),
        P(),
        P(),
        P(None, None, "narrow"),
        P(None, "narrow", None),
        P("wide", "narrow", None),
    )
    out_specs = (
        P("wide", "narrow", None),
        P("wide", "narrow", None),
        P(),
        P(None, None, "narrow"),
        P("narrow", None),
        P(),
        P(),
        P(None, None, "narrow"),
        P(None, "narrow", None),
    )
    return jax.shard_map(
        per_device, mesh=mesh, in_specs=in_specs, out_specs=out_specs, check_vma=False
    )
```

```python
import functools
import math

import jax
import jax.numpy as jnp
from jax import lax
from jax.experimental import pallas as pl
from jax.experimental.pallas import tpu as pltpu
from jax.sharding import PartitionSpec as P

MESH = pl.DeviceIdType.MESH
HEAD_DIM = 64
PAIR = 2 * HEAD_DIM
EPS = 1e-06
NEG = -1e30
bf16 = jnp.bfloat16
f32 = jnp.float32
VMEM_LIMIT = 60 << 20


def nn(a, b):
    return lax.dot_general(a, b, (((1,), (0,)), ((), ())), preferred_element_type=f32)


def nt(a, b):
    return lax.dot_general(a, b, (((1,), (1,)), ((), ())), preferred_element_type=f32)


def tn(a, b):
    return lax.dot_general(a, b, (((0,), (0,)), ((), ())), preferred_element_type=f32)


def whole(memory=pltpu.VMEM):
    return pl.BlockSpec(memory_space=memory)


def rows_of(first, count, size):
    return pl.ds(pl.multiple_of(first * size, size), count * size)


def peers(kind, sizes):
    narrow, wide, twins = sizes
    w, z = lax.axis_index("wide"), lax.axis_index("narrow")
    first = (w // twins) * twins
    if kind == "narrow":
        return z, narrow, lambda j: (w, j)
    if kind == "wide":
        return w, wide, lambda j: (j, z)
    if kind == "twin":
        return w - first, twins, lambda j: (first + j, z)
    if kind == "row":
        return w // twins, wide // twins, lambda j: (j * twins + w - first, z)
    if kind in ("x", "y"):
        side = math.isqrt(wide // twins)
        row = w // twins
        line, place = lax.rem(row, side), row // side
        if kind == "x":
            return line, side, lambda j: ((place * side + j) * twins + w - first, z)
        return place, side, lambda j: ((j * side + line) * twins + w - first, z)
    if kind == "column":
        return (
            z * twins + w - first,
            narrow * twins,
            lambda j: (first + lax.rem(j, twins), j // twins),
        )
    return w * narrow + z, wide * narrow, lambda j: (j // narrow, lax.rem(j, narrow))


def group_size(kind, sizes):
    narrow, wide, twins = sizes
    return {
        "narrow": narrow,
        "wide": wide,
        "twin": twins,
        "row": wide // twins,
        "x": math.isqrt(wide // twins),
        "y": math.isqrt(wide // twins),
        "column": narrow * twins,
        "all": wide * narrow,
    }[kind]


def plan(kinds, sizes):
    bases, used = {}, 0
    for name, kind in kinds.items():
        bases[name] = used
        used += group_size(kind, sizes)
    return bases, used


class Exchange:
    def __init__(self, kind, sizes, source_at, target_at, sems, base, own=None, slots=False):
        self.slots = slots
        self.me, self.total, self.place = peers(kind, sizes)
        self.source_at, self.target_at = source_at, target_at
        (self.send, self.recv, self.local), self.base, self.own = sems, base, own

    def copy_of(self, k):
        j = lax.rem(self.me + k, self.total)
        return pltpu.make_async_remote_copy(
            src_ref=self.source_at(j),
            dst_ref=self.target_at(k - 1 if self.slots else self.me),
            send_sem=self.send.at[self.base + k],
            recv_sem=self.recv.at[self.base + k],
            device_id=self.place(j),
            device_id_type=MESH,
        )

    def each(self, action):
        def step(k, carry):
            action(self.copy_of(k))
            return carry

        lax.fori_loop(1, self.total, step, 0)

    def kept(self):
        return pltpu.make_async_copy(
            self.source_at(self.me), self.target_at(self.me), self.local.at[self.own]
        )

    def start(self):
        self.each(lambda c: c.start())
        if self.own is not None:
            self.kept().start()

    def wait_recv(self):
        self.each(lambda c: c.wait_recv())
        if self.own is not None:
            self.kept().wait()

    def wait_send(self):
        self.each(lambda c: c.wait_send())


def greet(sizes):
    barrier = pltpu.get_barrier_semaphore()
    me, total, place = peers("all", sizes)

    def step(k, carry):
        pl.semaphore_signal(
            barrier, inc=1, device_id=place(lax.rem(me + k, total)), device_id_type=MESH
        )
        return carry

    lax.fori_loop(1, total, step, 0)
    pl.semaphore_wait(barrier, total - 1)


def unit_of(values):
    scaling = lax.rsqrt(jnp.mean(values * values, axis=-1, keepdims=True) + EPS)
    return values * scaling, scaling


def unit_back(grad_rows, unit_rows, scaling, gain):
    grad_unit = grad_rows * gain
    inner = jnp.mean(grad_unit * unit_rows, axis=-1, keepdims=True)
    return scaling * (grad_unit - unit_rows * inner)


def wall_of(wall_ref, n):
    part = wall_ref[n]
    return part.reshape(-1, part.shape[-1])


def attend_pairs(
    block, s, low, high, normed, start_ref, wall_ref, qkv_ref, att_ref, lse_acc, stored
):
    length = normed.shape[0]
    lane = lax.broadcasted_iota(jnp.int32, (block, PAIR), 1)

    def one_pair(n, carry):
        proj = nn(normed[...], wall_of(wall_ref, n)[:, : 3 * PAIR]).astype(bf16)
        qkv_ref[s, n] = proj
        keys, vals = proj[:, PAIR : 2 * PAIR], proj[:, 2 * PAIR :]
        for i in range(length // block):
            rows = slice(i * block, (i + 1) * block)
            end = (i + 1) * block
            query = proj[rows, :PAIR] * jnp.asarray(HEAD_DIM**-0.5, bf16)
            key_at = lax.broadcasted_iota(jnp.int32, (block, end), 1)
            row_at = i * block + lax.broadcasted_iota(jnp.int32, (block, end), 0)
            allowed = (key_at >= start_ref[s, rows, :]) & (key_at <= row_at)
            got = []
            for j in range(2):
                own = (lane // HEAD_DIM) == j
                score = nt(jnp.where(own, query, jnp.zeros_like(query)), keys[:end])
                score = jnp.where(allowed, score, NEG)
                peak = jnp.max(score, axis=1, keepdims=True)
                expo = jnp.exp(score - peak)
                total = jnp.sum(expo, axis=1, keepdims=True)
                got.append(nn(expo.astype(bf16), vals[:end]) / total)
                lse_acc[rows, :] = jnp.where(
                    lane == 2 * n + j, peak + jnp.log(total), lse_acc[rows, :]
                )
            att_ref[s, n, rows, :] = jnp.where(lane < HEAD_DIM, got[0], got[1]).astype(bf16)
        stored(s, n)
        return carry

    lax.fori_loop(low, high, one_pair, 0)


def prob_pairs(block, s, start_row, qkv_ref, lse_row, prob_refs, prob_outs, prob_sem):
    length, pairs = qkv_ref.shape[2], qkv_ref.shape[1]
    lane = lax.broadcasted_iota(jnp.int32, (length, PAIR), 1)

    def outs(n, slot):
        return [
            pltpu.make_async_copy(ref.at[slot], out.at[s, n], prob_sem.at[i, slot])
            for i, (ref, out) in enumerate(zip(prob_refs, prob_outs))
        ]

    def one_pair(n, carry):
        slot = lax.rem(n, 2)

        @pl.when(n >= 2)
        def _():
            for c in outs(n - 2, slot):
                c.wait()

        query = qkv_ref[s, n, :, :PAIR] * jnp.asarray(HEAD_DIM**-0.5, bf16)
        keys = qkv_ref[s, n, :, PAIR : 2 * PAIR]
        for j in range(2):
            q_own = jnp.where((lane // HEAD_DIM) == j, query, jnp.zeros_like(query))
            lse = lse_row[pl.ds(2 * n + j, 1), :]
            for i, ref in enumerate(prob_refs):
                first = i * block
                shape = (block, length - first)
                key_at = first + lax.broadcasted_iota(jnp.int32, shape, 0)
                row_at = first + lax.broadcasted_iota(jnp.int32, shape, 1)
                allowed = (key_at >= start_row[:, first:]) & (key_at <= row_at)
                score = nt(keys[first : first + block], q_own[first:])
                prob = jnp.where(allowed, jnp.exp(score - lse[:, first:]), 0.0)
                ref[slot, j] = prob.astype(bf16)
        for c in outs(n, slot):
            c.start()
        return carry

    lax.fori_loop(0, pairs, one_pair, 0)
    for n in range(max(0, pairs - 2), pairs):
        for c in outs(n, n % 2):
            c.wait()


def forward_kinds(seqs):
    kinds = {"wall": "narrow", "wall_row": "row", "wall_twin": "twin", "cot": "wide"}
    for t in range(2):
        kinds[f"weight{t}"] = "narrow"
        kinds[f"weight_a{t}"], kinds[f"weight_b{t}"] = ("x", "y") if t == 0 else ("y", "x")
    for s in range(seqs):
        kinds[f"x{s}"], kinds[f"hid{s}"] = "narrow", "all"
    return kinds


def forward_body(
    sizes,
    block,
    bases,
    inputs_ref,
    cot_ref,
    up_ref,
    down_ref,
    in_ref,
    outproj_ref,
    pos_ref,
    gain_ref,
    xmix_ref,
    gmix_ref,
    weight_ref,
    x_out,
    wall_out,
    qkv_out,
    att_out,
    *refs,
):
    blocks = (len(refs) - 15) // 2
    prob_outs, prob_refs = refs[:blocks], refs[blocks : 2 * blocks]
    (
        lse_ref,
        x_ref,
        wall_ref,
        qkv_ref,
        att_ref,
        hid_ref,
        normed_ref,
        lse_acc,
        wall_own_ref,
        start_ref,
        send,
        recv,
        local,
        out_sem,
        prob_sem,
    ) = refs[2 * blocks :]
    narrow, wide, twins = sizes
    w, z = lax.axis_index("wide"), lax.axis_index("narrow")
    seqs, length, features = x_ref.shape
    seq_dev, local_len, _ = inputs_ref.shape
    pos_dev = local_len // wide
    pairs = wall_ref.shape[0]
    row, twin = w // twins, lax.rem(w, twins)
    wall_rows = features // wide
    side = weight_ref.shape[2]
    row_y, row_x = row // side, lax.rem(row, side)
    weight_rows = weight_ref.shape[4]
    sems = (send, recv, local)

    def exchange(name, kind, source_at, target_at, own=None):
        return Exchange(kind, sizes, source_at, target_at, sems, bases[name], own)

    for c in range(3):
        wall_own_ref[:, c * PAIR : (c + 1) * PAIR] = in_ref[c]
    wall_own_ref[:, 3 * PAIR :] = jnp.transpose(outproj_ref[...])
    greet(sizes)
    wall = exchange(
        "wall",
        "narrow",
        lambda j: wall_own_ref.at[rows_of(w, 1, wall_rows)],
        lambda j: wall_ref.at[j, row, twin],
        0,
    )
    wall_row = exchange(
        "wall_row",
        "row",
        lambda j: wall_ref.at[:, row, twin],
        lambda j: wall_ref.at[:, j, twin],
    )
    wall_twin = exchange(
        "wall_twin", "twin", lambda j: wall_ref.at[:, :, twin], lambda j: wall_ref.at[:, :, j]
    )
    cot = exchange(
        "cot",
        "wide",
        lambda j: cot_ref.at[:, rows_of(j, 1, pos_dev)],
        lambda j: gmix_ref.at[pl.ds(j * seq_dev, seq_dev)],
        1,
    )
    mine = rows_of(row, 1, weight_rows)
    weight = [
        exchange(
            f"weight{t}",
            "narrow",
            lambda j, ref=ref: ref.at[j * twins + twin, mine],
            lambda j, t=t: weight_ref.at[t, j, row_y, row_x],
            2 + t,
        )
        for t, ref in enumerate((up_ref, down_ref))
    ]
    along_x, along_y = (
        lambda j, t: weight_ref.at[t, :, row_y, j],
        lambda j, t: weight_ref.at[t, :, j, row_x],
    )
    weight_a = [
        exchange(
            f"weight_a{t}",
            "x" if t == 0 else "y",
            lambda j, t=t: weight_ref.at[t, :, row_y, row_x],
            functools.partial(along_x if t == 0 else along_y, t=t),
        )
        for t in range(2)
    ]
    line_y, line_x = (
        lambda j, t: weight_ref.at[t, :, j],
        lambda j, t: weight_ref.at[t, :, :, j],
    )
    weight_b = [
        exchange(
            f"weight_b{t}",
            "y" if t == 0 else "x",
            lambda j, t=t: line_y(row_y, t) if t == 0 else line_x(row_x, t),
            functools.partial(line_y if t == 0 else line_x, t=t),
        )
        for t in range(2)
    ]
    x_in = [
        exchange(
            f"x{s}",
            "narrow",
            lambda j, s=s: inputs_ref.at[j * seqs + s],
            lambda j, s=s: x_ref.at[s, rows_of(j, 1, local_len)],
            4 + s,
        )
        for s in range(seqs)
    ]
    hid = [
        exchange(
            f"hid{s}",
            "all",
            lambda j, s=s: hid_ref.at[
                s, rows_of(lax.rem(j, narrow) * wide + j // narrow, 1, pos_dev)
            ],
            lambda j, s=s: xmix_ref.at[j * seqs + s],
            4 + seqs + s,
        )
        for s in range(seqs)
    ]

    def kept(s, n):
        return (
            pltpu.make_async_copy(qkv_ref.at[s, n], qkv_out.at[s, n], out_sem.at[s, 2 * n]),
            pltpu.make_async_copy(att_ref.at[s, n], att_out.at[s, n], out_sem.at[s, 2 * n + 1]),
        )

    def stored(s, n):
        for c in kept(s, n):
            c.start()

    wall_keep = pltpu.make_async_copy(wall_ref, wall_out, out_sem.at[0, 2 * pairs])
    x_keep = [
        pltpu.make_async_copy(x_ref.at[s], x_out.at[s], out_sem.at[s, 2 * pairs + 1])
        for s in range(seqs)
    ]

    wall.start()
    x_in[0].start()
    wall.wait_recv()
    wall_row.start()
    wall_row.wait_recv()
    wall_twin.start()
    cot.start()
    pos_t = jnp.transpose(pos_ref[...])
    seq_at = lax.broadcasted_iota(jnp.int32, pos_t.shape, 1)
    token_at = lax.broadcasted_iota(jnp.int32, (length, 1), 0)
    for s in range(seqs):
        own = jnp.sum(jnp.where(seq_at == z * seqs + s, pos_t, 0), axis=1, keepdims=True)
        start_ref[s] = token_at - own
    wall_twin.wait_recv()
    x_in[0].wait_recv()
    weight[0].start()
    weight[1].start()
    wall_keep.start()
    for s in range(seqs):
        if s > 0:
            x_in[s].wait_recv()
        x_keep[s].start()
        normed_ref[...] = (unit_of(x_ref[s].astype(f32))[0] * gain_ref[...]).astype(bf16)

        def pairs_of(low, high, s=s):
            attend_pairs(
                block, s, low, high, normed_ref, start_ref, wall_ref, qkv_ref, att_ref, lse_acc, stored
            )

        pairs_of(0, pairs // 2)
        if s + 1 < seqs:
            x_in[s + 1].start()
        pairs_of(pairs // 2, pairs)
        hidden = x_ref[s].astype(f32)
        for n in range(pairs):
            hidden = hidden + nt(att_ref[s, n], wall_of(wall_ref, n)[:, 3 * PAIR :])
        hid_ref[s] = hidden.astype(bf16)
        hid[s].start()
        lse_ref[...] = jnp.transpose(lse_acc[...])[: 2 * pairs]
        start_row = lax.broadcasted_iota(jnp.int32, (1, length), 1) - pos_ref[
            pl.ds(z * seqs + s, 1), :
        ]
        if s == 0:
            for t in range(2):
                weight[t].wait_recv()
                weight_a[t].start()
        if s == 1:
            for t in range(2):
                weight_a[t].wait_recv()
                weight_b[t].start()
        prob_pairs(block, s, start_row, qkv_ref, lse_ref, prob_refs, prob_outs, prob_sem)
    for e in (wall, wall_row, wall_twin, cot, *weight, *weight_a, *weight_b, *x_in):
        e.wait_send()
    cot.wait_recv()
    for t in range(2):
        weight_b[t].wait_recv()
    wall_keep.wait()
    for s in range(seqs):
        x_keep[s].wait()

        def settle(n, carry, s=s):
            for c in kept(s, n):
                c.wait()
            return carry

        lax.fori_loop(0, pairs, settle, 0)
    for s in range(seqs):
        hid[s].wait_recv()
        hid[s].wait_send()


def forward(inputs, cot, up, down, in_parts, outproj, positions, gain, sizes):
    narrow, wide, twins = sizes
    seq_dev, local_len, features = inputs.shape
    seqs, length, pairs = seq_dev // narrow, local_len * narrow, narrow
    pos_dev = local_len // wide
    wall_shape = (pairs, wide // twins, twins, features // wide, 4 * PAIR)
    bases, used = plan(forward_kinds(seqs), sizes)
    dma = pltpu.SemaphoreType.DMA
    side = math.isqrt(wide // twins)
    qkv_shape = (seqs, pairs, length, 3 * PAIR)
    att_shape = (seqs, pairs, length, PAIR)
    mix_shape = (seq_dev * wide, pos_dev, features)
    block = min(256, length)
    widths = [length - first for first in range(0, length, block)]
    return pl.pallas_call(
        functools.partial(forward_body, sizes, min(256, length), bases),
        out_shape=[
            jax.ShapeDtypeStruct(mix_shape, bf16),
            jax.ShapeDtypeStruct(mix_shape, bf16),
            jax.ShapeDtypeStruct(
                (2, narrow, side, side, up.shape[1] // side**2, up.shape[2]), bf16
            ),
            jax.ShapeDtypeStruct((seqs, length, features), bf16),
            jax.ShapeDtypeStruct(wall_shape, bf16),
            jax.ShapeDtypeStruct(qkv_shape, bf16),
            jax.ShapeDtypeStruct(att_shape, bf16),
            *(jax.ShapeDtypeStruct((seqs, pairs, 2, block, width), bf16) for width in widths),
        ],
        in_specs=[whole(pl.ANY)] * 4 + [whole()] * 4,
        out_specs=[whole(pl.ANY)] * (7 + len(widths)),
        scratch_shapes=[
            *(pltpu.VMEM((2, 2, block, width), bf16) for width in widths),
            pltpu.VMEM((2 * pairs, length), f32),
            pltpu.VMEM((seqs, length, features), bf16),
            pltpu.VMEM(wall_shape, bf16),
            pltpu.VMEM(qkv_shape, bf16),
            pltpu.VMEM(att_shape, bf16),
            pltpu.VMEM((seqs, length, features), bf16),
            pltpu.VMEM((length, features), bf16),
            pltpu.VMEM((length, PAIR), f32),
            pltpu.VMEM((features, 4 * PAIR), bf16),
            pltpu.VMEM((seqs, length, 1), jnp.int32),
            dma((used,)),
            dma((used,)),
            dma((4 + 2 * seqs,)),
            dma((seqs, 2 * pairs + 2)),
            dma((len(widths), 2)),
        ],
        compiler_params=pltpu.CompilerParams(
            collective_id=1, has_side_effects=True, vmem_limit_bytes=VMEM_LIMIT
        ),
    )(inputs, cot, up, down, in_parts, outproj, positions, gain)


def mix_forward(experts, cells, x_ref, key_ref, gain_ref, router_ref, normed_ref, weight_ref, low_ref, logit_ref):
    tokens = x_ref.shape[0]
    chunk = min(512, tokens)

    def norm_rows(c, carry):
        rows = rows_of(c, 1, chunk)
        unit = unit_of(x_ref[rows, :].astype(f32))[0]
        normed_ref[rows, :] = (unit * gain_ref[...]).astype(bf16)
        return carry

    lax.fori_loop(0, tokens // chunk, norm_rows, 0)
    logit_ref[...] = nt(router_ref[...], normed_ref[...])

    def one_expert(e, carry):
        cell = lax.broadcasted_iota(jnp.int32, (cells, tokens), 0)
        score = jnp.where(cell == key_ref[...], logit_ref[pl.ds(e, 1), :], NEG)
        expo = jnp.exp(score - jnp.max(score, axis=1, keepdims=True))
        weights = expo / jnp.sum(expo, axis=1, keepdims=True)
        rows = rows_of(e, 1, cells)
        weight_ref[rows, :] = weights
        low_ref[rows, :] = weights.astype(bf16)
        return carry

    lax.fori_loop(0, experts, one_expert, 0)


def gelu_parts(pre):
    square = pre * pre
    tanh = jnp.tanh(0.7978845608028654 * (pre + 0.044715 * pre * square))
    act = 0.5 * pre * (1.0 + tanh)
    slope = 0.5 * (1.0 + tanh) + 0.5 * pre * (1.0 - tanh * tanh) * (
        0.7978845608028654 * (1.0 + 3 * 0.044715 * square)
    )
    return act, slope


def mix_weights_back(experts, cells, weight_ref, gw_ref, gl_ref):
    def one_expert(e, carry):
        rows = rows_of(e, 1, cells)
        weights, grads = weight_ref[rows, :], gw_ref[rows, :]
        inner = jnp.sum(weights * grads, axis=1, keepdims=True)
        gl_ref[pl.ds(e, 1), :] = jnp.sum(weights * (grads - inner), axis=0, keepdims=True)
        return carry

    lax.fori_loop(0, experts, one_expert, 0)


def attend_back_pairs(
    block, s, probs, x_nt, dh_ref, dh_t, wall_ref, qkv_ref, att_ref, dq_acc, dproj_ref, gw_acc, hooks
):
    length = dh_ref.shape[1]
    lane = lax.broadcasted_iota(jnp.int32, (length, PAIR), 1)
    scale = jnp.asarray(HEAD_DIM**-0.5, bf16)

    def one_pair(n, carry):
        wall = wall_of(wall_ref, n)
        d_att = nn(dh_ref[s], wall[:, 3 * PAIR :]).astype(bf16)
        prod = (d_att.astype(f32) * att_ref[s, n].astype(f32)).astype(bf16)
        head_row = lax.broadcasted_iota(jnp.int32, (8, PAIR), 0)
        head_lane = lax.broadcasted_iota(jnp.int32, (8, PAIR), 1) // HEAD_DIM
        inner = nt((head_row == head_lane).astype(bf16), prod)
        query = qkv_ref[s, n, :, :PAIR] * scale
        keys, vals = qkv_ref[s, n, :, PAIR : 2 * PAIR], qkv_ref[s, n, :, 2 * PAIR :]
        keys_t = jnp.transpose(keys)
        zero = jnp.zeros_like(query)
        own = [(lane // HEAD_DIM) == j for j in range(2)]
        q_own = [jnp.where(o, query, zero) for o in own]
        d_own = [jnp.where(o, d_att, zero) for o in own]
        slot = lax.rem(n, 2)
        prob_refs, load = probs
        for c in load(s, n, slot):
            c.wait()

        @pl.when(n + 1 < wall_ref.shape[0])
        def _():
            for c in load(s, n + 1, 1 - slot):
                c.start()

        for i in range(length // block):
            rows, first = slice(i * block, (i + 1) * block), i * block
            dk = dv = None
            for j in range(2):
                head = slice(j * HEAD_DIM, (j + 1) * HEAD_DIM)
                prob = prob_refs[i][slot, j]
                d_prob = nt(vals[rows], d_own[j][first:])
                d_score = (prob.astype(f32) * (d_prob - inner[j : j + 1, first:])).astype(bf16)
                dv_part = nn(prob, d_own[j][first:])
                dk_part = nn(d_score, q_own[j][first:])
                dv = dv_part if dv is None else dv + dv_part
                dk = dk_part if dk is None else dk + dk_part
                dq_part = nn(keys_t[head, rows], d_score)
                if i == 0:
                    dq_acc[head, :] = dq_part
                else:
                    dq_acc[head, first:] += dq_part
            dproj_ref[n, rows, PAIR : 2 * PAIR] = dk.astype(bf16)
            dproj_ref[n, rows, 2 * PAIR :] = dv.astype(bf16)
        dproj_ref[n, :, :PAIR] = jnp.transpose((dq_acc[...] * HEAD_DIM**-0.5).astype(bf16))
        g_in, g_out = nn(x_nt[...], dproj_ref[n]), nn(dh_t[...], att_ref[s, n])
        if s == 0:
            gw_acc[n, :, : 3 * PAIR] = g_in
            gw_acc[n, :, 3 * PAIR :] = g_out
        else:
            gw_acc[n, :, : 3 * PAIR] += g_in
            gw_acc[n, :, 3 * PAIR :] += g_out
        hooks(n)
        return carry

    lax.fori_loop(0, wall_ref.shape[0], one_pair, 0)


def back_kinds(seqs, pairs, side):
    kinds = {name: "column" for name in ("mixed", "gexp", "eo", "gm")}
    kinds["out"] = "wide"
    for t in range(2):
        first, second = ("x", "y") if t == 0 else ("y", "x")
        kinds[f"sum_a{t}"], kinds[f"sum_b{t}"], kinds[f"sum_z{t}"] = first, second, "narrow"
        kinds[f"full_a{t}"], kinds[f"full_b{t}"] = first, second
        for m in range(side):
            kinds[f"full_twin{t}_{m}"] = "twin"
    for s in range(seqs):
        kinds[f"dh{s}"], kinds[f"gx{s}"] = "all", "narrow"
    for n in range(pairs):
        kinds[f"wall_twin{n}"] = "twin"
    for n in range(pairs):
        kinds[f"wall_row{n}"] = "row"
    kinds["wall_z"], kinds["wall_full"] = "narrow", "wide"
    kinds["small_w"], kinds["small_z"] = "wide", "narrow"
    return kinds


def backward_body(
    sizes,
    block,
    bases,
    xmix_in,
    gmix_in,
    weight_in,
    x_in,
    wall_in,
    qkv_in,
    att_in,
    key_ref,
    gain_one,
    gain_two,
    router_ref,
    *refs,
):
    count = len(refs) - 39
    backward_rest(
        sizes,
        block,
        bases,
        (xmix_in, gmix_in, weight_in, x_in, wall_in, qkv_in, att_in),
        (key_ref, gain_one, gain_two, router_ref),
        refs[:count],
        *refs[count:],
    )


def backward_rest(
    sizes,
    block,
    bases,
    arrays,
    small_arrays,
    prob_ins,
    out_home,
    gx_home,
    full_up,
    full_down,
    wall_out,
    small_out,
    mixed_src,
    gexp_src,
    eo_src,
    gm_src,
    mixed_land,
    gexp_land,
    eo_land,
    gm_land,
    grad_src,
    land_a,
    sum_mid,
    land_b,
    sum_src,
    gh_ref,
    out_ref,
    dh_ref,
    gx_ref,
    gw_src,
    gw_twin,
    gw_half,
    gw_row,
    gw_z_src,
    gw_z,
    gw_last,
    small_ref,
    small_w,
    small_mid,
    small_z,
    send,
    recv,
    local,
    load_sem,
    prob_sem,
):
    xmix_in, gmix_in, weight_in, x_in, wall_in, qkv_in, att_in = arrays
    key_ref, gain_one, gain_two, router_ref = small_arrays
    narrow, wide, twins = sizes
    w, z = lax.axis_index("wide"), lax.axis_index("narrow")
    row, twin = w // twins, lax.rem(w, twins)
    row_count = wide // twins
    seqs, length, features = dh_ref.shape
    seq_total, pos_dev, _ = gh_ref.shape
    tokens = seq_total * pos_dev
    seq_dev, local_len, _ = out_home.shape
    experts = router_ref.shape[0]
    cells = mixed_src.shape[0] // experts
    pairs = gw_src.shape[0]
    side = grad_src.shape[2]
    row_y, row_x = row // side, lax.rem(row, side)
    wall_rows = gw_last.shape[0]
    sems = (send, recv, local)
    owns = iter(range(local.shape[0]))

    def exchange(name, kind, source_at, target_at, own=False, slots=False):
        return Exchange(
            kind, sizes, source_at, target_at, sems, bases[name], next(owns) if own else None, slots
        )

    def column(name, source, target):
        return exchange(
            name,
            "column",
            lambda j: source.at[rows_of(j, 1, cells)],
            lambda j: target.at[rows_of(j, 1, cells)],
            True,
        )

    mixed_x = column("mixed", mixed_src, mixed_land)
    gexp_x = column("gexp", gexp_src, gexp_land)
    eo_x = column("eo", eo_src, eo_land)
    gm_x = column("gm", gm_src, gm_land)
    out_x = exchange(
        "out",
        "wide",
        lambda j: out_ref.at[pl.ds(j * seq_dev, seq_dev)],
        lambda j: out_home.at[:, rows_of(j, 1, pos_dev)],
        True,
    )
    first_kind, second_kind = ("x", "y"), ("y", "x")
    full_ref = (full_up, full_down)

    def line_of(ref, t, j, along):
        return ref.at[t, :, :, j] if along == "x" else ref.at[t, :, j]

    sum_a = [
        exchange(
            f"sum_a{t}",
            first_kind[t],
            lambda j, t=t: line_of(grad_src, t, j, first_kind[t]),
            lambda k, t=t: land_a.at[k, t],
            slots=True,
        )
        for t in range(2)
    ]
    sum_b = [
        exchange(
            f"sum_b{t}",
            second_kind[t],
            lambda j, t=t: sum_mid.at[t, :, j],
            lambda k, t=t: land_b.at[k, t],
            slots=True,
        )
        for t in range(2)
    ]
    sum_z = [
        exchange(
            f"sum_z{t}",
            "narrow",
            lambda j, t=t: sum_src.at[t, j],
            lambda j, t=t: full_ref[t].at[j, twin, row_y, row_x],
            True,
        )
        for t in range(2)
    ]
    full_a = [
        exchange(
            f"full_a{t}",
            first_kind[t],
            lambda j, t=t: full_ref[t].at[:, twin, row_y, row_x],
            lambda j, t=t: (
                full_ref[t].at[:, twin, row_y, j]
                if first_kind[t] == "x"
                else full_ref[t].at[:, twin, j, row_x]
            ),
        )
        for t in range(2)
    ]

    def full_line(j, along, t):
        return full_ref[t].at[:, twin, j] if along == "y" else full_ref[t].at[:, twin, :, j]

    full_b = [
        exchange(
            f"full_b{t}",
            second_kind[t],
            lambda j, t=t: full_line(
                row_y if second_kind[t] == "y" else row_x, second_kind[t], t
            ),
            lambda j, t=t: full_line(j, second_kind[t], t),
        )
        for t in range(2)
    ]
    def twin_line(j, t, m):
        place = lax.rem((row_y if second_kind[t] == "y" else row_x) + m, side)
        return (
            full_ref[t].at[:, j, place] if second_kind[t] == "y" else full_ref[t].at[:, j, :, place]
        )

    full_twin = [
        [
            exchange(
                f"full_twin{t}_{m}",
                "twin",
                lambda j, t=t, m=m: twin_line(twin, t, m),
                lambda j, t=t, m=m: twin_line(j, t, m),
            )
            for m in range(side)
        ]
        for t in range(2)
    ]
    dh_x = [
        exchange(
            f"dh{s}",
            "all",
            lambda j, s=s: gh_ref.at[j * seqs + s],
            lambda j, s=s: dh_ref.at[
                s, rows_of(lax.rem(j, narrow) * wide + j // narrow, 1, pos_dev)
            ],
            True,
        )
        for s in range(seqs)
    ]
    gx_x = [
        exchange(
            f"gx{s}",
            "narrow",
            lambda j, s=s: gx_ref.at[s, rows_of(j, 1, local_len)],
            lambda j, s=s: gx_home.at[j * seqs + s],
            True,
        )
        for s in range(seqs)
    ]

    def wall_twin(n):
        e = exchange(
            "wall_twin0",
            "twin",
            lambda j: gw_src.at[n, :, j],
            lambda k: gw_twin.at[k, n],
            slots=True,
        )
        e.base = bases["wall_twin0"] + n * twins
        return e

    def wall_row(n):
        e = exchange(
            "wall_row0", "row", lambda j: gw_half.at[n, j], lambda k: gw_row.at[k, n], slots=True
        )
        e.base = bases["wall_row0"] + n * row_count
        return e

    wall_z = exchange(
        "wall_z", "narrow", lambda j: gw_z_src.at[j], lambda k: gw_z.at[k], slots=True
    )
    wall_full = exchange(
        "wall_full",
        "wide",
        lambda j: gw_last,
        lambda j: wall_out.at[rows_of(j, 1, wall_rows)],
        True,
    )
    small_wide = exchange("small_w", "wide", lambda j: small_ref, lambda j: small_w.at[j])
    small_narrow = exchange("small_z", "narrow", lambda j: small_mid, lambda j: small_z.at[j])

    greet(sizes)

    def mixture(x_ref, g_ref, normed_ref, weight_ref, low_ref, low_t, logit_ref):
        x_load = pltpu.make_async_copy(xmix_in, x_ref, load_sem.at[0])
        g_load = pltpu.make_async_copy(gmix_in, g_ref, load_sem.at[1])
        x_load.start()
        g_load.start()

        def experts_of(up_down, act_ref, slope_ref, pre_ref):
            w_load = pltpu.make_async_copy(weight_in, up_down, load_sem.at[2])

            def weight_of(t, h):
                return up_down[t, h].reshape(-1, up_down.shape[-1])

            w_load.start()
            x_load.wait()
            mix_forward(
                experts, cells, x_ref, key_ref, gain_two, router_ref, normed_ref, weight_ref, low_ref, logit_ref
            )
            mixed_src[...] = nn(low_ref[...], normed_ref[...]).astype(bf16)
            mixed_x.start()
            g_load.wait()
            gexp_src[...] = nn(low_ref[...], g_ref[...]).astype(bf16)
            gexp_x.start()
            low_t[...] = jnp.transpose(low_ref[...])
            w_load.wait()
            mixed_x.wait_recv()
            rows = mixed_land[...]
            total = None
            for h in range(narrow):
                act, slope = gelu_parts(nn(rows, weight_of(0, h)))
                act_ref[h] = act.astype(bf16)
                slope_ref[h] = slope.astype(bf16)
                part = nn(act_ref[h], weight_of(1, h))
                total = part if total is None else total + part
            eo_src[...] = total.astype(bf16)
            eo_x.start()
            gexp_x.wait_recv()
            total = None
            for h in range(narrow):
                pre = nt(gexp_land[...], weight_of(1, h)) * slope_ref[h].astype(f32)
                pre_ref[h] = pre.astype(bf16)
                part = nt(pre_ref[h], weight_of(0, h))
                total = part if total is None else total + part
            gm_src[...] = total.astype(bf16)
            gm_x.start()
            rows_t = jnp.transpose(rows)
            for h in range(narrow):
                grad_src[0, h] = nn(rows_t, pre_ref[h]).astype(bf16).reshape(grad_src.shape[2:])
            sum_a[0].start()
            for h in range(narrow):
                grad_src[1, h] = (
                    tn(act_ref[h], gexp_land[...]).astype(bf16).reshape(grad_src.shape[2:])
                )
            sum_a[1].start()

        part_shape = (narrow, experts * cells, weight_in.shape[-1])
        pl.run_scoped(
            experts_of,
            pltpu.VMEM(weight_in.shape, bf16),
            pltpu.VMEM(part_shape, bf16),
            pltpu.VMEM(part_shape, bf16),
            pltpu.VMEM(part_shape, bf16),
        )

        def come_back(gw_ref, gl_ref):
            chunk = min(512, tokens)
            seq_chunk = chunk // pos_dev
            eo_x.wait_recv()

            def out_rows(c, carry):
                rows = rows_of(c, 1, chunk)
                got = x_ref[rows, :].astype(f32) + nn(low_t[rows, :], eo_land[...])
                out_ref[pl.ds(c * seq_chunk, seq_chunk)] = got.astype(bf16).reshape(
                    seq_chunk, pos_dev, features
                )
                return carry

            lax.fori_loop(0, tokens // chunk, out_rows, 0)
            gw_ref[...] = nt(eo_land[...], g_ref[...])
            gm_x.wait_recv()
            gw_ref[...] += nt(gm_land[...], normed_ref[...])
            mix_weights_back(experts, cells, weight_ref, gw_ref, gl_ref)
            g_logit = gl_ref[...].astype(bf16)
            small_ref[:experts, :] = nn(g_logit, normed_ref[...])
            small_ref[experts:, :] = jnp.zeros((small_ref.shape[0] - experts, features), f32)

            def back_rows(c, carry):
                rows = rows_of(c, 1, chunk)
                unit, scaling = unit_of(x_ref[rows, :].astype(f32))
                g_l = gl_ref[:, rows].astype(bf16)
                g_normed = nn(low_t[rows, :], gm_land[...]) + tn(g_l, router_ref[...])
                small_ref[experts : experts + 1, :] += jnp.sum(
                    g_normed * unit, axis=0, keepdims=True
                )
                got = g_ref[rows, :].astype(f32) + unit_back(g_normed, unit, scaling, gain_two[...])
                gh_ref[pl.ds(c * seq_chunk, seq_chunk)] = got.astype(bf16).reshape(
                    seq_chunk, pos_dev, features
                )
                return carry

            lax.fori_loop(0, tokens // chunk, back_rows, 0)

        pl.run_scoped(
            come_back,
            pltpu.VMEM((experts * cells, tokens), f32),
            pltpu.VMEM((experts, tokens), f32),
        )

    pl.run_scoped(
        mixture,
        pltpu.VMEM((tokens, features), bf16),
        pltpu.VMEM((tokens, features), bf16),
        pltpu.VMEM((tokens, features), bf16),
        pltpu.VMEM((experts * cells, tokens), f32),
        pltpu.VMEM((experts * cells, tokens), bf16),
        pltpu.VMEM((tokens, experts * cells), bf16),
        pltpu.VMEM((experts, tokens), f32),
    )
    dh_x[0].start()

    def sum_first():
        for t in range(2):
            sum_a[t].wait_recv()
            for h in range(narrow):
                if first_kind[t] == "x":
                    total = grad_src[t, h, :, row_x].astype(f32)
                else:
                    total = grad_src[t, h, row_y].astype(f32)
                for k in range(side - 1):
                    total = total + land_a[k, t, h].astype(f32)
                sum_mid[t, h] = total.astype(bf16)
            sum_b[t].start()

    def sum_second():
        for t in range(2):
            place = row_y if second_kind[t] == "y" else row_x
            sum_b[t].wait_recv()
            for h in range(narrow):
                total = sum_mid[t, h, place].astype(f32)
                for k in range(side - 1):
                    total = total + land_b[k, t, h].astype(f32)
                sum_src[t, h] = total.astype(bf16)

    def start_sum_z():
        for t in range(2):
            sum_z[t].start()

    def spread_first():
        for t in range(2):
            sum_z[t].wait_recv()
            full_a[t].start()

    def spread_second():
        for t in range(2):
            full_a[t].wait_recv()
            full_b[t].start()
            full_twin[t][0].start()

    def spread_third():
        for t in range(2):
            full_b[t].wait_recv()
            for e in full_twin[t][1:]:
                e.start()

    def wall_halves(n):
        wall_twin(n).wait_recv()
        total = gw_src[n, :, twin].astype(f32)
        for k in range(twins - 1):
            total = total + gw_twin[k, n].astype(f32)
        gw_half[n] = total.astype(bf16)
        wall_row(n).start()

    def attention(
        x_ref, wall_ref, qkv_ref, att_ref, x_nt, dh_t, gw_acc, dq_acc, dproj_ref, *prob_refs
    ):
        def load(s, n, slot):
            return [
                pltpu.make_async_copy(source.at[s, n], ref.at[slot], prob_sem.at[i, slot])
                for i, (source, ref) in enumerate(zip(prob_ins, prob_refs))
            ]

        loads = [
            pltpu.make_async_copy(source, target, load_sem.at[3 + i])
            for i, (source, target) in enumerate(
                ((x_in, x_ref), (wall_in, wall_ref), (qkv_in, qkv_ref), (att_in, att_ref))
            )
        ]
        for c in loads:
            c.start()
        sum_first()
        for c in loads:
            c.wait()

        def finished(n):
            part = gw_acc[n].astype(bf16)
            gw_src[n] = part.reshape(gw_src.shape[1:])
            wall_twin(n).start()

            @pl.when(n > 0)
            def _():
                wall_halves(n - 1)

        def hooks_of(s):
            steps = {}
            if s == 0:
                steps[0] = (out_x.start,)
                steps[1] = (sum_second, start_sum_z)
            elif s == 1:
                steps[pairs - 2] = (spread_first,)

            def hooks(n):
                if s == seqs - 1:
                    finished(n)
                for at, actions in steps.items():

                    @pl.when(n == at)
                    def _(actions=actions):
                        for action in actions:
                            action()

            return hooks

        def rows_back(s, k):
            j = lax.rem(z + k, narrow)
            rows = rows_of(j, 1, local_len)
            grad = nt(dproj_ref[0, rows, :], wall_of(wall_ref, 0)[:, : 3 * PAIR])
            for n in range(1, pairs):
                grad = grad + nt(dproj_ref[n, rows, :], wall_of(wall_ref, n)[:, : 3 * PAIR])
            unit, scaling = unit_of(x_ref[s, rows, :].astype(f32))
            small_ref[experts + 1 : experts + 2, :] += jnp.sum(grad * unit, axis=0, keepdims=True)
            got = dh_ref[s, rows, :].astype(f32) + unit_back(grad, unit, scaling, gain_one[...])
            gx_ref[s, rows, :] = got.astype(bf16)

        for s in range(seqs):
            for c in load(s, 0, 0):
                c.start()
            unit, _ = unit_of(x_ref[s].astype(f32))
            x_nt[...] = jnp.transpose((unit * gain_one[...]).astype(bf16))
            dh_x[s].wait_recv()
            if s + 1 < seqs:
                dh_x[s + 1].start()
            dh_t[...] = jnp.transpose(dh_ref[s])
            attend_back_pairs(
                block, s, (prob_refs, load), x_nt, dh_ref, dh_t, wall_ref, qkv_ref, att_ref, dq_acc, dproj_ref, gw_acc, hooks_of(s)
            )

            def to_peer(k, carry, s=s):
                rows_back(s, k)
                gx_x[s].copy_of(k).start()
                return carry

            lax.fori_loop(1, narrow, to_peer, 0)
            rows_back(s, 0)
            gx_x[s].kept().start()
            if s == seqs - 1:
                wall_halves(pairs - 1)

    pl.run_scoped(
        attention,
        pltpu.VMEM(x_in.shape, bf16),
        pltpu.VMEM(wall_in.shape, bf16),
        pltpu.VMEM(qkv_in.shape, bf16),
        pltpu.VMEM(att_in.shape, bf16),
        pltpu.VMEM((features, length), bf16),
        pltpu.VMEM((features, length), bf16),
        pltpu.VMEM((pairs, features, 4 * PAIR), f32),
        pltpu.VMEM((PAIR, length), f32),
        pltpu.VMEM((pairs, length, 3 * PAIR), bf16),
        *(pltpu.VMEM((2,) + ref.shape[2:], bf16) for ref in prob_ins),
    )
    small_wide.start()
    total = gw_half[:, row].astype(f32)
    for n in range(pairs):
        wall_row(n).wait_recv()
    for k in range(row_count - 1):
        total = total + gw_row[k].astype(f32)
    gw_z_src[...] = total.astype(bf16)
    wall_z.start()
    spread_second()
    small_wide.wait_recv()
    small_w[w] = small_ref[...]
    total = small_w[0]
    for j in range(1, wide):
        total = total + small_w[j]
    small_mid[...] = total
    small_narrow.start()
    wall_z.wait_recv()
    total = gw_z_src[z].astype(f32)
    for k in range(narrow - 1):
        total = total + gw_z[k].astype(f32)
    gw_last[...] = total.astype(bf16)
    wall_full.start()
    spread_third()
    small_narrow.wait_recv()
    small_z[z] = small_mid[...]
    total = small_z[0]
    for j in range(1, narrow):
        total = total + small_z[j]
    small_out[...] = total
    for e in (mixed_x, gexp_x, eo_x, gm_x, out_x, *sum_a, *sum_b, *sum_z, *dh_x):
        e.wait_send()
    for n in range(pairs):
        wall_twin(n).wait_send()
        wall_row(n).wait_send()
    for e in (wall_z, small_wide, small_narrow, *full_a, *full_b):
        e.wait_send()
    out_x.wait_recv()
    for e in (*gx_x, wall_full, *full_twin[0], *full_twin[1]):
        e.wait_recv()
        e.wait_send()


def backward(x_mix, g_mix, weights, x_seq, wall, qkv, att, probs, key_row, gain_one, gain_two, router, home, sizes):
    narrow, wide, twins = sizes
    seq_total, pos_dev, features = x_mix.shape
    seqs, length, _ = x_seq.shape
    pairs, experts = narrow, router.shape[0]
    row_count = wide // twins
    tokens = seq_total * pos_dev
    side, part_rows, columns = weights.shape[3:]
    wall_rows = features // wide
    cells = pos_dev * key_row[1]
    bases, used = plan(back_kinds(seqs, pairs, math.isqrt(row_count)), sizes)
    dma = pltpu.SemaphoreType.DMA
    rows = (experts * cells, features)
    vm = pltpu.VMEM
    return pl.pallas_call(
        functools.partial(backward_body, sizes, min(256, length), bases),
        out_shape=[
            jax.ShapeDtypeStruct(home, bf16),
            jax.ShapeDtypeStruct(home, bf16),
            jax.ShapeDtypeStruct((narrow, twins, side, side, part_rows, columns), bf16),
            jax.ShapeDtypeStruct((narrow, twins, side, side, part_rows, columns), bf16),
            jax.ShapeDtypeStruct((features, 4 * PAIR), bf16),
            jax.ShapeDtypeStruct((2 * experts, features), f32),
        ],
        in_specs=[whole(pl.ANY)] * 7 + [whole()] * 4 + [whole(pl.ANY)] * len(probs),
        out_specs=[whole(pl.ANY)] * 5 + [whole()],
        scratch_shapes=[vm(rows, bf16)] * 8
        + [
            vm(weights.shape, bf16),
            vm((side - 1, 2, narrow, side, part_rows, columns), bf16),
            vm((2, narrow, side, part_rows, columns), bf16),
            vm((side - 1, 2, narrow, part_rows, columns), bf16),
            vm((2, narrow, part_rows, columns), bf16),
            vm(x_mix.shape, bf16),
            vm(x_mix.shape, bf16),
            vm(x_seq.shape, bf16),
            vm(x_seq.shape, bf16),
            vm((pairs, row_count, twins, wall_rows, 4 * PAIR), bf16),
            vm((twins - 1, pairs, row_count, wall_rows, 4 * PAIR), bf16),
            vm((pairs, row_count, wall_rows, 4 * PAIR), bf16),
            vm((row_count - 1, pairs, wall_rows, 4 * PAIR), bf16),
            vm((pairs, wall_rows, 4 * PAIR), bf16),
            vm((narrow - 1, wall_rows, 4 * PAIR), bf16),
            vm((wall_rows, 4 * PAIR), bf16),
            vm((2 * experts, features), f32),
            vm((wide, 2 * experts, features), f32),
            vm((2 * experts, features), f32),
            vm((narrow, 2 * experts, features), f32),
            dma((used,)),
            dma((used,)),
            dma((8 + 2 * seqs,)),
            dma((7,)),
            dma((len(probs), 2)),
        ],
        compiler_params=pltpu.CompilerParams(
            collective_id=2, has_side_effects=True, vmem_limit_bytes=VMEM_LIMIT
        ),
    )(
        x_mix.reshape(tokens, features),
        g_mix.reshape(tokens, features),
        weights,
        x_seq,
        wall,
        qkv,
        att,
        key_row[0],
        gain_one,
        gain_two,
        router,
        *probs,
    )


def widen_body(*refs):
    half = len(refs) // 2
    for source, target in zip(refs[:half], refs[half:]):
        target[...] = source[...].astype(f32)


def widen(arrays, steps):
    flat = [a.reshape(steps, -1, a.shape[-1]) for a in arrays]
    specs = [pl.BlockSpec((1,) + a.shape[1:], lambda i: (i, 0, 0)) for a in flat]
    wide = pl.pallas_call(
        widen_body,
        grid=(steps,),
        out_shape=[jax.ShapeDtypeStruct(a.shape, f32) for a in flat],
        in_specs=specs,
        out_specs=specs,
        compiler_params=pltpu.CompilerParams(vmem_limit_bytes=VMEM_LIMIT),
    )(*flat)
    return [b.reshape(a.shape) for a, b in zip(arrays, wide)]


def per_device(
    inputs,
    positions,
    members_index,
    members_mask,
    gain_attn,
    input_projection_weight,
    output_projection_weight,
    gain_mixer,
    weight_router,
    weight_up,
    weight_down,
    cotangent,
):
    narrow, wide = lax.axis_size("narrow"), lax.axis_size("wide")
    w, z = lax.axis_index("wide"), lax.axis_index("narrow")
    seq_dev, local_len, features = inputs.shape
    length = positions.shape[1]
    groups = members_index.shape[1]
    experts = weight_up.shape[0]
    own_seqs = seq_dev // narrow
    pos_dev = local_len // wide
    seq_total = seq_dev * wide
    sizes = (narrow, wide, experts // narrow)

    offset_rows = w * pos_dev
    index_rows = lax.dynamic_slice_in_dim(members_index, offset_rows, pos_dev, 0)
    live = lax.dynamic_slice_in_dim(members_mask, offset_rows, pos_dev, 0) > 0
    named = (
        index_rows[..., None] == jnp.arange(seq_total, dtype=jnp.int32)[None, None, None, :]
    ) & live[..., None]
    group_of = jnp.max(
        jnp.where(named, jnp.arange(groups, dtype=jnp.int32)[None, :, None, None], 0), axis=(1, 2)
    )
    key_row = group_of + groups * jnp.arange(pos_dev, dtype=jnp.int32)[:, None]
    key_row = jnp.transpose(key_row).reshape(1, seq_total * pos_dev)

    gain_one, gain_two = gain_attn.reshape(1, features), gain_mixer.reshape(1, features)
    router = jnp.transpose(weight_router)
    x_mix, g_mix, weights, x_seq, wall, qkv, att, *probs = forward(
        inputs,
        cotangent,
        weight_up,
        weight_down,
        jnp.transpose(input_projection_weight, (1, 0, 2)),
        output_projection_weight,
        positions,
        gain_one,
        sizes,
    )
    outputs, gx, full_up, full_down, g_wall, small = backward(
        x_mix,
        g_mix,
        weights,
        x_seq,
        wall,
        qkv,
        att,
        probs,
        (key_row, groups),
        gain_one,
        gain_two,
        router,
        inputs.shape,
        sizes,
    )
    g_up, g_down, gx = widen(
        [full_up.reshape(weight_up.shape), full_down.reshape(weight_down.shape), gx], 4
    )
    g_wall = g_wall.astype(f32)
    return (
        outputs,
        gx,
        small[experts + 1],
        g_wall[:, : 3 * PAIR].reshape(input_projection_weight.shape),
        jnp.transpose(g_wall[:, 3 * PAIR :]),
        small[experts],
        jnp.transpose(small[:experts]),
        g_up,
        g_down,
    )


def solution(mesh):
    in_specs = (
        P("wide", "narrow", None),
        P("wide", None),
        P("narrow", None, None),
        P("narrow", None, None),
        P(),
        P(None, None, "narrow"),
        P("narrow", None),
        P(),
        P(),
        P(None, None, "narrow"),
        P(None, "narrow", None),
        P("wide", "narrow", None),
    )
    out_specs = (
        P("wide", "narrow", None),
        P("wide", "narrow", None),
        P(),
        P(None, None, "narrow"),
        P("narrow", None),
        P(),
        P(),
        P(None, None, "narrow"),
        P(None, "narrow", None),
    )
    return jax.shard_map(
        per_device, mesh=mesh, in_specs=in_specs, out_specs=out_specs, check_vma=False
    )
```

```python
import functools
import math

import jax
import jax.numpy as jnp
from jax import lax
from jax.experimental import pallas as pl
from jax.experimental.pallas import tpu as pltpu
from jax.sharding import PartitionSpec as P

MESH = pl.DeviceIdType.MESH
HEAD_DIM = 64
PAIR = 2 * HEAD_DIM
EPS = 1e-06
NEG = -1e30
bf16 = jnp.bfloat16
f32 = jnp.float32
VMEM_LIMIT = 60 << 20


def nn(a, b):
    return lax.dot_general(a, b, (((1,), (0,)), ((), ())), preferred_element_type=f32)


def nt(a, b):
    return lax.dot_general(a, b, (((1,), (1,)), ((), ())), preferred_element_type=f32)


def tn(a, b):
    return lax.dot_general(a, b, (((0,), (0,)), ((), ())), preferred_element_type=f32)


def whole(memory=pltpu.VMEM):
    return pl.BlockSpec(memory_space=memory)


def rows_of(first, count, size):
    return pl.ds(pl.multiple_of(first * size, size), count * size)


def peers(kind, sizes):
    narrow, wide, twins = sizes
    w, z = lax.axis_index("wide"), lax.axis_index("narrow")
    first = (w // twins) * twins
    if kind == "narrow":
        return z, narrow, lambda j: (w, j)
    if kind == "wide":
        return w, wide, lambda j: (j, z)
    if kind == "twin":
        return w - first, twins, lambda j: (first + j, z)
    if kind == "row":
        return w // twins, wide // twins, lambda j: (j * twins + w - first, z)
    if kind in ("x", "y"):
        side = math.isqrt(wide // twins)
        row = w // twins
        line, place = lax.rem(row, side), row // side
        if kind == "x":
            return line, side, lambda j: ((place * side + j) * twins + w - first, z)
        return place, side, lambda j: ((j * side + line) * twins + w - first, z)
    if kind == "column":
        return (
            z * twins + w - first,
            narrow * twins,
            lambda j: (first + lax.rem(j, twins), j // twins),
        )
    return w * narrow + z, wide * narrow, lambda j: (j // narrow, lax.rem(j, narrow))


def group_size(kind, sizes):
    narrow, wide, twins = sizes
    return {
        "narrow": narrow,
        "wide": wide,
        "twin": twins,
        "row": wide // twins,
        "x": math.isqrt(wide // twins),
        "y": math.isqrt(wide // twins),
        "column": narrow * twins,
        "all": wide * narrow,
    }[kind]


def plan(kinds, sizes):
    bases, used = {}, 0
    for name, kind in kinds.items():
        bases[name] = used
        used += group_size(kind, sizes)
    return bases, used


class Exchange:
    def __init__(self, kind, sizes, source_at, target_at, sems, base, own=None, slots=False):
        self.slots = slots
        self.me, self.total, self.place = peers(kind, sizes)
        self.source_at, self.target_at = source_at, target_at
        (self.send, self.recv, self.local), self.base, self.own = sems, base, own

    def copy_of(self, k):
        j = lax.rem(self.me + k, self.total)
        return pltpu.make_async_remote_copy(
            src_ref=self.source_at(j),
            dst_ref=self.target_at(k - 1 if self.slots else self.me),
            send_sem=self.send.at[self.base + k],
            recv_sem=self.recv.at[self.base + k],
            device_id=self.place(j),
            device_id_type=MESH,
        )

    def each(self, action):
        def step(k, carry):
            action(self.copy_of(k))
            return carry

        lax.fori_loop(1, self.total, step, 0)

    def kept(self):
        return pltpu.make_async_copy(
            self.source_at(self.me), self.target_at(self.me), self.local.at[self.own]
        )

    def start(self):
        self.each(lambda c: c.start())
        if self.own is not None:
            self.kept().start()

    def wait_recv(self):
        self.each(lambda c: c.wait_recv())
        if self.own is not None:
            self.kept().wait()

    def wait_send(self):
        self.each(lambda c: c.wait_send())


def greet(sizes):
    barrier = pltpu.get_barrier_semaphore()
    me, total, place = peers("all", sizes)

    def step(k, carry):
        pl.semaphore_signal(
            barrier, inc=1, device_id=place(lax.rem(me + k, total)), device_id_type=MESH
        )
        return carry

    lax.fori_loop(1, total, step, 0)
    pl.semaphore_wait(barrier, total - 1)


def unit_of(values):
    scaling = lax.rsqrt(jnp.mean(values * values, axis=-1, keepdims=True) + EPS)
    return values * scaling, scaling


def unit_back(grad_rows, unit_rows, scaling, gain):
    grad_unit = grad_rows * gain
    inner = jnp.mean(grad_unit * unit_rows, axis=-1, keepdims=True)
    return scaling * (grad_unit - unit_rows * inner)


def wall_of(wall_ref, n):
    part = wall_ref[n]
    return part.reshape(-1, part.shape[-1])


def attend_pairs(
    block, s, low, high, normed, start_ref, wall_ref, qkv_ref, att_ref, lse_acc, stored
):
    length = normed.shape[0]
    lane = lax.broadcasted_iota(jnp.int32, (block, PAIR), 1)

    def one_pair(n, carry):
        proj = nn(normed[...], wall_of(wall_ref, n)[:, : 3 * PAIR]).astype(bf16)
        qkv_ref[s, n] = proj
        keys, vals = proj[:, PAIR : 2 * PAIR], proj[:, 2 * PAIR :]
        for i in range(length // block):
            rows = slice(i * block, (i + 1) * block)
            end = (i + 1) * block
            query = proj[rows, :PAIR] * jnp.asarray(HEAD_DIM**-0.5, bf16)
            key_at = lax.broadcasted_iota(jnp.int32, (block, end), 1)
            row_at = i * block + lax.broadcasted_iota(jnp.int32, (block, end), 0)
            allowed = (key_at >= start_ref[s, rows, :]) & (key_at <= row_at)
            got = []
            for j in range(2):
                own = (lane // HEAD_DIM) == j
                score = nt(jnp.where(own, query, jnp.zeros_like(query)), keys[:end])
                score = jnp.where(allowed, score, NEG)
                peak = jnp.max(score, axis=1, keepdims=True)
                expo = jnp.exp(score - peak)
                total = jnp.sum(expo, axis=1, keepdims=True)
                got.append(nn(expo.astype(bf16), vals[:end]) / total)
                lse_acc[rows, :] = jnp.where(
                    lane == 2 * n + j, peak + jnp.log(total), lse_acc[rows, :]
                )
            att_ref[s, n, rows, :] = jnp.where(lane < HEAD_DIM, got[0], got[1]).astype(bf16)
        stored(s, n)
        return carry

    lax.fori_loop(low, high, one_pair, 0)


def prob_pairs(block, s, start_row, qkv_ref, lse_row, prob_refs, prob_outs, prob_sem):
    length, pairs = qkv_ref.shape[2], qkv_ref.shape[1]
    lane = lax.broadcasted_iota(jnp.int32, (length, PAIR), 1)

    def outs(n, slot):
        return [
            pltpu.make_async_copy(ref.at[slot], out.at[s, n], prob_sem.at[i, slot])
            for i, (ref, out) in enumerate(zip(prob_refs, prob_outs))
        ]

    def one_pair(n, carry):
        slot = lax.rem(n, 2)

        @pl.when(n >= 2)
        def _():
            for c in outs(n - 2, slot):
                c.wait()

        query = qkv_ref[s, n, :, :PAIR] * jnp.asarray(HEAD_DIM**-0.5, bf16)
        keys = qkv_ref[s, n, :, PAIR : 2 * PAIR]
        for j in range(2):
            q_own = jnp.where((lane // HEAD_DIM) == j, query, jnp.zeros_like(query))
            lse = lse_row[pl.ds(2 * n + j, 1), :]
            for i, ref in enumerate(prob_refs):
                first = i * block
                shape = (block, length - first)
                key_at = first + lax.broadcasted_iota(jnp.int32, shape, 0)
                row_at = first + lax.broadcasted_iota(jnp.int32, shape, 1)
                allowed = (key_at >= start_row[:, first:]) & (key_at <= row_at)
                score = nt(keys[first : first + block], q_own[first:])
                prob = jnp.where(allowed, jnp.exp(score - lse[:, first:]), 0.0)
                ref[slot, j] = prob.astype(bf16)
        for c in outs(n, slot):
            c.start()
        return carry

    lax.fori_loop(0, pairs, one_pair, 0)
    for n in range(max(0, pairs - 2), pairs):
        for c in outs(n, n % 2):
            c.wait()


def forward_kinds(seqs):
    kinds = {"wall": "narrow", "wall_row": "row", "wall_twin": "twin", "cot": "wide"}
    for t in range(2):
        kinds[f"weight{t}"] = "narrow"
        kinds[f"weight_a{t}"], kinds[f"weight_b{t}"] = ("x", "y") if t == 0 else ("y", "x")
    for s in range(seqs):
        kinds[f"x{s}"], kinds[f"hid{s}"] = "narrow", "all"
    return kinds


def forward_body(
    sizes,
    block,
    bases,
    inputs_ref,
    cot_ref,
    up_ref,
    down_ref,
    in_ref,
    outproj_ref,
    pos_ref,
    gain_ref,
    xmix_ref,
    gmix_ref,
    weight_ref,
    x_out,
    wall_out,
    qkv_out,
    att_out,
    *refs,
):
    blocks = (len(refs) - 15) // 2
    prob_outs, prob_refs = refs[:blocks], refs[blocks : 2 * blocks]
    (
        lse_ref,
        x_ref,
        wall_ref,
        qkv_ref,
        att_ref,
        hid_ref,
        normed_ref,
        lse_acc,
        wall_own_ref,
        start_ref,
        send,
        recv,
        local,
        out_sem,
        prob_sem,
    ) = refs[2 * blocks :]
    narrow, wide, twins = sizes
    w, z = lax.axis_index("wide"), lax.axis_index("narrow")
    seqs, length, features = x_ref.shape
    seq_dev, local_len, _ = inputs_ref.shape
    pos_dev = local_len // wide
    pairs = wall_ref.shape[0]
    row, twin = w // twins, lax.rem(w, twins)
    wall_rows = features // wide
    side = weight_ref.shape[2]
    row_y, row_x = row // side, lax.rem(row, side)
    weight_rows = weight_ref.shape[4]
    sems = (send, recv, local)

    def exchange(name, kind, source_at, target_at, own=None):
        return Exchange(kind, sizes, source_at, target_at, sems, bases[name], own)

    for c in range(3):
        wall_own_ref[:, c * PAIR : (c + 1) * PAIR] = in_ref[c]
    wall_own_ref[:, 3 * PAIR :] = jnp.transpose(outproj_ref[...])
    greet(sizes)
    wall = exchange(
        "wall",
        "narrow",
        lambda j: wall_own_ref.at[rows_of(w, 1, wall_rows)],
        lambda j: wall_ref.at[j, row, twin],
        0,
    )
    wall_row = exchange(
        "wall_row",
        "row",
        lambda j: wall_ref.at[:, row, twin],
        lambda j: wall_ref.at[:, j, twin],
    )
    wall_twin = exchange(
        "wall_twin", "twin", lambda j: wall_ref.at[:, :, twin], lambda j: wall_ref.at[:, :, j]
    )
    cot = exchange(
        "cot",
        "wide",
        lambda j: cot_ref.at[:, rows_of(j, 1, pos_dev)],
        lambda j: gmix_ref.at[pl.ds(j * seq_dev, seq_dev)],
        1,
    )
    mine = rows_of(row, 1, weight_rows)
    weight = [
        exchange(
            f"weight{t}",
            "narrow",
            lambda j, ref=ref: ref.at[j * twins + twin, mine],
            lambda j, t=t: weight_ref.at[t, j, row_y, row_x],
            2 + t,
        )
        for t, ref in enumerate((up_ref, down_ref))
    ]
    along_x, along_y = (
        lambda j, t: weight_ref.at[t, :, row_y, j],
        lambda j, t: weight_ref.at[t, :, j, row_x],
    )
    weight_a = [
        exchange(
            f"weight_a{t}",
            "x" if t == 0 else "y",
            lambda j, t=t: weight_ref.at[t, :, row_y, row_x],
            functools.partial(along_x if t == 0 else along_y, t=t),
        )
        for t in range(2)
    ]
    line_y, line_x = (
        lambda j, t: weight_ref.at[t, :, j],
        lambda j, t: weight_ref.at[t, :, :, j],
    )
    weight_b = [
        exchange(
            f"weight_b{t}",
            "y" if t == 0 else "x",
            lambda j, t=t: line_y(row_y, t) if t == 0 else line_x(row_x, t),
            functools.partial(line_y if t == 0 else line_x, t=t),
        )
        for t in range(2)
    ]
    x_in = [
        exchange(
            f"x{s}",
            "narrow",
            lambda j, s=s: inputs_ref.at[j * seqs + s],
            lambda j, s=s: x_ref.at[s, rows_of(j, 1, local_len)],
            4 + s,
        )
        for s in range(seqs)
    ]
    hid = [
        exchange(
            f"hid{s}",
            "all",
            lambda j, s=s: hid_ref.at[
                s, rows_of(lax.rem(j, narrow) * wide + j // narrow, 1, pos_dev)
            ],
            lambda j, s=s: xmix_ref.at[j * seqs + s],
            4 + seqs + s,
        )
        for s in range(seqs)
    ]

    def kept(s, n):
        return (
            pltpu.make_async_copy(qkv_ref.at[s, n], qkv_out.at[s, n], out_sem.at[s, 2 * n]),
            pltpu.make_async_copy(att_ref.at[s, n], att_out.at[s, n], out_sem.at[s, 2 * n + 1]),
        )

    def stored(s, n):
        for c in kept(s, n):
            c.start()

    wall_keep = pltpu.make_async_copy(wall_ref, wall_out, out_sem.at[0, 2 * pairs])
    x_keep = [
        pltpu.make_async_copy(x_ref.at[s], x_out.at[s], out_sem.at[s, 2 * pairs + 1])
        for s in range(seqs)
    ]

    wall.start()
    x_in[0].start()
    wall.wait_recv()
    wall_row.start()
    wall_row.wait_recv()
    wall_twin.start()
    cot.start()
    pos_t = jnp.transpose(pos_ref[...])
    seq_at = lax.broadcasted_iota(jnp.int32, pos_t.shape, 1)
    token_at = lax.broadcasted_iota(jnp.int32, (length, 1), 0)
    for s in range(seqs):
        own = jnp.sum(jnp.where(seq_at == z * seqs + s, pos_t, 0), axis=1, keepdims=True)
        start_ref[s] = token_at - own
    wall_twin.wait_recv()
    x_in[0].wait_recv()
    weight[0].start()
    weight[1].start()
    wall_keep.start()
    for s in range(seqs):
        if s > 0:
            x_in[s].wait_recv()
        x_keep[s].start()
        normed_ref[...] = (unit_of(x_ref[s].astype(f32))[0] * gain_ref[...]).astype(bf16)

        def pairs_of(low, high, s=s):
            attend_pairs(
                block, s, low, high, normed_ref, start_ref, wall_ref, qkv_ref, att_ref, lse_acc, stored
            )

        pairs_of(0, pairs // 2)
        if s + 1 < seqs:
            x_in[s + 1].start()
        pairs_of(pairs // 2, pairs)
        hidden = x_ref[s].astype(f32)
        for n in range(pairs):
            hidden = hidden + nt(att_ref[s, n], wall_of(wall_ref, n)[:, 3 * PAIR :])
        hid_ref[s] = hidden.astype(bf16)
        hid[s].start()
        lse_ref[...] = jnp.transpose(lse_acc[...])[: 2 * pairs]
        start_row = lax.broadcasted_iota(jnp.int32, (1, length), 1) - pos_ref[
            pl.ds(z * seqs + s, 1), :
        ]
        if s == 0:
            for t in range(2):
                weight[t].wait_recv()
                weight_a[t].start()
        if s == 1:
            for t in range(2):
                weight_a[t].wait_recv()
                weight_b[t].start()
        prob_pairs(block, s, start_row, qkv_ref, lse_ref, prob_refs, prob_outs, prob_sem)
    for e in (wall, wall_row, wall_twin, cot, *weight, *weight_a, *weight_b, *x_in):
        e.wait_send()
    cot.wait_recv()
    for t in range(2):
        weight_b[t].wait_recv()
    wall_keep.wait()
    for s in range(seqs):
        x_keep[s].wait()

        def settle(n, carry, s=s):
            for c in kept(s, n):
                c.wait()
            return carry

        lax.fori_loop(0, pairs, settle, 0)
    for s in range(seqs):
        hid[s].wait_recv()
        hid[s].wait_send()


def forward(inputs, cot, up, down, in_parts, outproj, positions, gain, sizes):
    narrow, wide, twins = sizes
    seq_dev, local_len, features = inputs.shape
    seqs, length, pairs = seq_dev // narrow, local_len * narrow, narrow
    pos_dev = local_len // wide
    wall_shape = (pairs, wide // twins, twins, features // wide, 4 * PAIR)
    bases, used = plan(forward_kinds(seqs), sizes)
    dma = pltpu.SemaphoreType.DMA
    side = math.isqrt(wide // twins)
    qkv_shape = (seqs, pairs, length, 3 * PAIR)
    att_shape = (seqs, pairs, length, PAIR)
    mix_shape = (seq_dev * wide, pos_dev, features)
    block = min(256, length)
    widths = [length - first for first in range(0, length, block)]
    return pl.pallas_call(
        functools.partial(forward_body, sizes, min(256, length), bases),
        out_shape=[
            jax.ShapeDtypeStruct(mix_shape, bf16),
            jax.ShapeDtypeStruct(mix_shape, bf16),
            jax.ShapeDtypeStruct(
                (2, narrow, side, side, up.shape[1] // side**2, up.shape[2]), bf16
            ),
            jax.ShapeDtypeStruct((seqs, length, features), bf16),
            jax.ShapeDtypeStruct(wall_shape, bf16),
            jax.ShapeDtypeStruct(qkv_shape, bf16),
            jax.ShapeDtypeStruct(att_shape, bf16),
            *(jax.ShapeDtypeStruct((seqs, pairs, 2, block, width), bf16) for width in widths),
        ],
        in_specs=[whole(pl.ANY)] * 4 + [whole()] * 4,
        out_specs=[whole(pl.ANY)] * (7 + len(widths)),
        scratch_shapes=[
            *(pltpu.VMEM((2, 2, block, width), bf16) for width in widths),
            pltpu.VMEM((2 * pairs, length), f32),
            pltpu.VMEM((seqs, length, features), bf16),
            pltpu.VMEM(wall_shape, bf16),
            pltpu.VMEM(qkv_shape, bf16),
            pltpu.VMEM(att_shape, bf16),
            pltpu.VMEM((seqs, length, features), bf16),
            pltpu.VMEM((length, features), bf16),
            pltpu.VMEM((length, PAIR), f32),
            pltpu.VMEM((features, 4 * PAIR), bf16),
            pltpu.VMEM((seqs, length, 1), jnp.int32),
            dma((used,)),
            dma((used,)),
            dma((4 + 2 * seqs,)),
            dma((seqs, 2 * pairs + 2)),
            dma((len(widths), 2)),
        ],
        compiler_params=pltpu.CompilerParams(
            collective_id=1, has_side_effects=True, vmem_limit_bytes=VMEM_LIMIT
        ),
    )(inputs, cot, up, down, in_parts, outproj, positions, gain)


def mix_forward(experts, cells, x_ref, key_ref, gain_ref, router_ref, normed_ref, weight_ref, low_ref, logit_ref):
    tokens = x_ref.shape[0]
    chunk = min(512, tokens)

    def norm_rows(c, carry):
        rows = rows_of(c, 1, chunk)
        unit = unit_of(x_ref[rows, :].astype(f32))[0]
        normed_ref[rows, :] = (unit * gain_ref[...]).astype(bf16)
        return carry

    lax.fori_loop(0, tokens // chunk, norm_rows, 0)
    logit_ref[...] = nt(router_ref[...], normed_ref[...])

    def one_expert(e, carry):
        cell = lax.broadcasted_iota(jnp.int32, (cells, tokens), 0)
        score = jnp.where(cell == key_ref[...], logit_ref[pl.ds(e, 1), :], NEG)
        expo = jnp.exp(score - jnp.max(score, axis=1, keepdims=True))
        weights = expo / jnp.sum(expo, axis=1, keepdims=True)
        rows = rows_of(e, 1, cells)
        weight_ref[rows, :] = weights
        low_ref[rows, :] = weights.astype(bf16)
        return carry

    lax.fori_loop(0, experts, one_expert, 0)


def gelu_parts(pre):
    square = pre * pre
    tanh = jnp.tanh(0.7978845608028654 * (pre + 0.044715 * pre * square))
    act = 0.5 * pre * (1.0 + tanh)
    slope = 0.5 * (1.0 + tanh) + 0.5 * pre * (1.0 - tanh * tanh) * (
        0.7978845608028654 * (1.0 + 3 * 0.044715 * square)
    )
    return act, slope


def mix_weights_back(experts, cells, weight_ref, gw_ref, gl_ref):
    def one_expert(e, carry):
        rows = rows_of(e, 1, cells)
        weights, grads = weight_ref[rows, :], gw_ref[rows, :]
        inner = jnp.sum(weights * grads, axis=1, keepdims=True)
        gl_ref[pl.ds(e, 1), :] = jnp.sum(weights * (grads - inner), axis=0, keepdims=True)
        return carry

    lax.fori_loop(0, experts, one_expert, 0)


def attend_back_pairs(
    block, s, probs, x_nt, dh_ref, dh_t, wall_ref, qkv_ref, att_ref, dq_acc, dproj_ref, gw_acc, hooks
):
    length = dh_ref.shape[1]
    lane = lax.broadcasted_iota(jnp.int32, (length, PAIR), 1)
    scale = jnp.asarray(HEAD_DIM**-0.5, bf16)

    def one_pair(n, carry):
        wall = wall_of(wall_ref, n)
        d_att = nn(dh_ref[s], wall[:, 3 * PAIR :]).astype(bf16)
        prod = (d_att.astype(f32) * att_ref[s, n].astype(f32)).astype(bf16)
        head_row = lax.broadcasted_iota(jnp.int32, (8, PAIR), 0)
        head_lane = lax.broadcasted_iota(jnp.int32, (8, PAIR), 1) // HEAD_DIM
        inner = nt((head_row == head_lane).astype(bf16), prod)
        query = qkv_ref[s, n, :, :PAIR] * scale
        keys, vals = qkv_ref[s, n, :, PAIR : 2 * PAIR], qkv_ref[s, n, :, 2 * PAIR :]
        keys_t = jnp.transpose(keys)
        zero = jnp.zeros_like(query)
        own = [(lane // HEAD_DIM) == j for j in range(2)]
        q_own = [jnp.where(o, query, zero) for o in own]
        d_own = [jnp.where(o, d_att, zero) for o in own]
        slot = lax.rem(n, 2)
        prob_refs, load = probs
        for c in load(s, n, slot):
            c.wait()

        @pl.when(n + 1 < wall_ref.shape[0])
        def _():
            for c in load(s, n + 1, 1 - slot):
                c.start()

        for i in range(length // block):
            rows, first = slice(i * block, (i + 1) * block), i * block
            dk = dv = None
            for j in range(2):
                head = slice(j * HEAD_DIM, (j + 1) * HEAD_DIM)
                prob = prob_refs[i][slot, j]
                d_prob = nt(vals[rows], d_own[j][first:])
                d_score = (prob.astype(f32) * (d_prob - inner[j : j + 1, first:])).astype(bf16)
                dv_part = nn(prob, d_own[j][first:])
                dk_part = nn(d_score, q_own[j][first:])
                dv = dv_part if dv is None else dv + dv_part
                dk = dk_part if dk is None else dk + dk_part
                dq_part = nn(keys_t[head, rows], d_score)
                if i == 0:
                    dq_acc[head, :] = dq_part
                else:
                    dq_acc[head, first:] += dq_part
            dproj_ref[n, rows, PAIR : 2 * PAIR] = dk.astype(bf16)
            dproj_ref[n, rows, 2 * PAIR :] = dv.astype(bf16)
        dproj_ref[n, :, :PAIR] = jnp.transpose((dq_acc[...] * HEAD_DIM**-0.5).astype(bf16))
        g_in, g_out = nn(x_nt[...], dproj_ref[n]), nn(dh_t[...], att_ref[s, n])
        if s == 0:
            gw_acc[n, :, : 3 * PAIR] = g_in
            gw_acc[n, :, 3 * PAIR :] = g_out
        else:
            gw_acc[n, :, : 3 * PAIR] += g_in
            gw_acc[n, :, 3 * PAIR :] += g_out
        hooks(n)
        return carry

    lax.fori_loop(0, wall_ref.shape[0], one_pair, 0)


def back_kinds(seqs, pairs, side):
    kinds = {name: "column" for name in ("mixed", "gexp", "eo", "gm")}
    kinds["out"] = "wide"
    for t in range(2):
        first, second = ("x", "y") if t == 0 else ("y", "x")
        kinds[f"sum_a{t}"], kinds[f"sum_b{t}"], kinds[f"sum_z{t}"] = first, second, "narrow"
        kinds[f"full_a{t}"], kinds[f"full_b{t}"] = first, second
        for m in range(side):
            kinds[f"full_twin{t}_{m}"] = "twin"
    for s in range(seqs):
        kinds[f"dh{s}"], kinds[f"gx{s}"] = "all", "narrow"
    for n in range(pairs):
        kinds[f"wall_twin{n}"] = "twin"
    for n in range(pairs):
        kinds[f"wall_row{n}"] = "row"
    kinds["wall_z"], kinds["wall_full"] = "narrow", "wide"
    kinds["small_w"], kinds["small_z"] = "wide", "narrow"
    return kinds


def backward_body(
    sizes,
    block,
    bases,
    xmix_in,
    gmix_in,
    weight_in,
    x_in,
    wall_in,
    qkv_in,
    att_in,
    key_ref,
    gain_one,
    gain_two,
    router_ref,
    *refs,
):
    count = len(refs) - 39
    backward_rest(
        sizes,
        block,
        bases,
        (xmix_in, gmix_in, weight_in, x_in, wall_in, qkv_in, att_in),
        (key_ref, gain_one, gain_two, router_ref),
        refs[:count],
        *refs[count:],
    )


def backward_rest(
    sizes,
    block,
    bases,
    arrays,
    small_arrays,
    prob_ins,
    out_home,
    gx_home,
    full_up,
    full_down,
    wall_out,
    small_out,
    mixed_src,
    gexp_src,
    eo_src,
    gm_src,
    mixed_land,
    gexp_land,
    eo_land,
    gm_land,
    grad_src,
    land_a,
    sum_mid,
    land_b,
    sum_src,
    gh_ref,
    out_ref,
    dh_ref,
    gx_ref,
    gw_src,
    gw_twin,
    gw_half,
    gw_row,
    gw_z_src,
    gw_z,
    gw_last,
    small_ref,
    small_w,
    small_mid,
    small_z,
    send,
    recv,
    local,
    load_sem,
    prob_sem,
):
    xmix_in, gmix_in, weight_in, x_in, wall_in, qkv_in, att_in = arrays
    key_ref, gain_one, gain_two, router_ref = small_arrays
    narrow, wide, twins = sizes
    w, z = lax.axis_index("wide"), lax.axis_index("narrow")
    row, twin = w // twins, lax.rem(w, twins)
    row_count = wide // twins
    seqs, length, features = dh_ref.shape
    seq_total, pos_dev, _ = gh_ref.shape
    tokens = seq_total * pos_dev
    seq_dev, local_len, _ = out_home.shape
    experts = router_ref.shape[0]
    cells = mixed_src.shape[0] // experts
    pairs = gw_src.shape[0]
    side = grad_src.shape[2]
    row_y, row_x = row // side, lax.rem(row, side)
    wall_rows = gw_last.shape[0]
    sems = (send, recv, local)
    owns = iter(range(local.shape[0]))

    def exchange(name, kind, source_at, target_at, own=False, slots=False):
        return Exchange(
            kind, sizes, source_at, target_at, sems, bases[name], next(owns) if own else None, slots
        )

    def column(name, source, target):
        return exchange(
            name,
            "column",
            lambda j: source.at[rows_of(j, 1, cells)],
            lambda j: target.at[rows_of(j, 1, cells)],
            True,
        )

    mixed_x = column("mixed", mixed_src, mixed_land)
    gexp_x = column("gexp", gexp_src, gexp_land)
    eo_x = column("eo", eo_src, eo_land)
    gm_x = column("gm", gm_src, gm_land)
    out_x = exchange(
        "out",
        "wide",
        lambda j: out_ref.at[pl.ds(j * seq_dev, seq_dev)],
        lambda j: out_home.at[:, rows_of(j, 1, pos_dev)],
        True,
    )
    first_kind, second_kind = ("x", "y"), ("y", "x")
    full_ref = (full_up, full_down)

    def line_of(ref, t, j, along):
        return ref.at[t, :, :, j] if along == "x" else ref.at[t, :, j]

    sum_a = [
        exchange(
            f"sum_a{t}",
            first_kind[t],
            lambda j, t=t: line_of(grad_src, t, j, first_kind[t]),
            lambda k, t=t: land_a.at[k, t],
            slots=True,
        )
        for t in range(2)
    ]
    sum_b = [
        exchange(
            f"sum_b{t}",
            second_kind[t],
            lambda j, t=t: sum_mid.at[t, :, j],
            lambda k, t=t: land_b.at[k, t],
            slots=True,
        )
        for t in range(2)
    ]
    sum_z = [
        exchange(
            f"sum_z{t}",
            "narrow",
            lambda j, t=t: sum_src.at[t, j],
            lambda j, t=t: full_ref[t].at[j, twin, row_y, row_x],
            True,
        )
        for t in range(2)
    ]
    full_a = [
        exchange(
            f"full_a{t}",
            first_kind[t],
            lambda j, t=t: full_ref[t].at[:, twin, row_y, row_x],
            lambda j, t=t: (
                full_ref[t].at[:, twin, row_y, j]
                if first_kind[t] == "x"
                else full_ref[t].at[:, twin, j, row_x]
            ),
        )
        for t in range(2)
    ]

    def full_line(j, along, t):
        return full_ref[t].at[:, twin, j] if along == "y" else full_ref[t].at[:, twin, :, j]

    full_b = [
        exchange(
            f"full_b{t}",
            second_kind[t],
            lambda j, t=t: full_line(
                row_y if second_kind[t] == "y" else row_x, second_kind[t], t
            ),
            lambda j, t=t: full_line(j, second_kind[t], t),
        )
        for t in range(2)
    ]
    def twin_line(j, t, m):
        place = lax.rem((row_y if second_kind[t] == "y" else row_x) + m, side)
        return (
            full_ref[t].at[:, j, place] if second_kind[t] == "y" else full_ref[t].at[:, j, :, place]
        )

    full_twin = [
        [
            exchange(
                f"full_twin{t}_{m}",
                "twin",
                lambda j, t=t, m=m: twin_line(twin, t, m),
                lambda j, t=t, m=m: twin_line(j, t, m),
            )
            for m in range(side)
        ]
        for t in range(2)
    ]
    dh_x = [
        exchange(
            f"dh{s}",
            "all",
            lambda j, s=s: gh_ref.at[j * seqs + s],
            lambda j, s=s: dh_ref.at[
                s, rows_of(lax.rem(j, narrow) * wide + j // narrow, 1, pos_dev)
            ],
            True,
        )
        for s in range(seqs)
    ]
    gx_x = [
        exchange(
            f"gx{s}",
            "narrow",
            lambda j, s=s: gx_ref.at[s, rows_of(j, 1, local_len)],
            lambda j, s=s: gx_home.at[j * seqs + s],
            True,
        )
        for s in range(seqs)
    ]

    def wall_twin(n):
        e = exchange(
            "wall_twin0",
            "twin",
            lambda j: gw_src.at[n, :, j],
            lambda k: gw_twin.at[k, n],
            slots=True,
        )
        e.base = bases["wall_twin0"] + n * twins
        return e

    def wall_row(n):
        e = exchange(
            "wall_row0", "row", lambda j: gw_half.at[n, j], lambda k: gw_row.at[k, n], slots=True
        )
        e.base = bases["wall_row0"] + n * row_count
        return e

    wall_z = exchange(
        "wall_z", "narrow", lambda j: gw_z_src.at[j], lambda k: gw_z.at[k], slots=True
    )
    wall_full = exchange(
        "wall_full",
        "wide",
        lambda j: gw_last,
        lambda j: wall_out.at[rows_of(j, 1, wall_rows)],
        True,
    )
    small_wide = exchange("small_w", "wide", lambda j: small_ref, lambda j: small_w.at[j])
    small_narrow = exchange("small_z", "narrow", lambda j: small_mid, lambda j: small_z.at[j])

    greet(sizes)

    def mixture(x_ref, g_ref, normed_ref, weight_ref, low_ref, low_t, logit_ref):
        x_load = pltpu.make_async_copy(xmix_in, x_ref, load_sem.at[0])
        g_load = pltpu.make_async_copy(gmix_in, g_ref, load_sem.at[1])
        x_load.start()
        g_load.start()

        def experts_of(up_down, act_ref, slope_ref, pre_ref):
            w_load = pltpu.make_async_copy(weight_in, up_down, load_sem.at[2])

            def weight_of(t, h):
                return up_down[t, h].reshape(-1, up_down.shape[-1])

            w_load.start()
            x_load.wait()
            mix_forward(
                experts, cells, x_ref, key_ref, gain_two, router_ref, normed_ref, weight_ref, low_ref, logit_ref
            )
            mixed_src[...] = nn(low_ref[...], normed_ref[...]).astype(bf16)
            mixed_x.start()
            g_load.wait()
            gexp_src[...] = nn(low_ref[...], g_ref[...]).astype(bf16)
            gexp_x.start()
            low_t[...] = jnp.transpose(low_ref[...])
            w_load.wait()
            mixed_x.wait_recv()
            rows = mixed_land[...]
            total = None
            for h in range(narrow):
                act, slope = gelu_parts(nn(rows, weight_of(0, h)))
                act_ref[h] = act.astype(bf16)
                slope_ref[h] = slope.astype(bf16)
                part = nn(act_ref[h], weight_of(1, h))
                total = part if total is None else total + part
            eo_src[...] = total.astype(bf16)
            eo_x.start()
            gexp_x.wait_recv()
            total = None
            for h in range(narrow):
                pre = nt(gexp_land[...], weight_of(1, h)) * slope_ref[h].astype(f32)
                pre_ref[h] = pre.astype(bf16)
                part = nt(pre_ref[h], weight_of(0, h))
                total = part if total is None else total + part
            gm_src[...] = total.astype(bf16)
            gm_x.start()
            rows_t = jnp.transpose(rows)
            for h in range(narrow):
                grad_src[0, h] = nn(rows_t, pre_ref[h]).astype(bf16).reshape(grad_src.shape[2:])
            sum_a[0].start()
            for h in range(narrow):
                grad_src[1, h] = (
                    tn(act_ref[h], gexp_land[...]).astype(bf16).reshape(grad_src.shape[2:])
                )
            sum_a[1].start()

        part_shape = (narrow, experts * cells, weight_in.shape[-1])
        pl.run_scoped(
            experts_of,
            pltpu.VMEM(weight_in.shape, bf16),
            pltpu.VMEM(part_shape, bf16),
            pltpu.VMEM(part_shape, bf16),
            pltpu.VMEM(part_shape, bf16),
        )

        def come_back(gw_ref, gl_ref):
            chunk = min(512, tokens)
            seq_chunk = chunk // pos_dev
            eo_x.wait_recv()

            def out_rows(c, carry):
                rows = rows_of(c, 1, chunk)
                got = x_ref[rows, :].astype(f32) + nn(low_t[rows, :], eo_land[...])
                out_ref[pl.ds(c * seq_chunk, seq_chunk)] = got.astype(bf16).reshape(
                    seq_chunk, pos_dev, features
                )
                return carry

            lax.fori_loop(0, tokens // chunk, out_rows, 0)
            gw_ref[...] = nt(eo_land[...], g_ref[...])
            gm_x.wait_recv()
            gw_ref[...] += nt(gm_land[...], normed_ref[...])
            mix_weights_back(experts, cells, weight_ref, gw_ref, gl_ref)
            g_logit = gl_ref[...].astype(bf16)
            small_ref[:experts, :] = nn(g_logit, normed_ref[...])
            small_ref[experts:, :] = jnp.zeros((small_ref.shape[0] - experts, features), f32)

            def back_rows(c, carry):
                rows = rows_of(c, 1, chunk)
                unit, scaling = unit_of(x_ref[rows, :].astype(f32))
                g_l = gl_ref[:, rows].astype(bf16)
                g_normed = nn(low_t[rows, :], gm_land[...]) + tn(g_l, router_ref[...])
                small_ref[experts : experts + 1, :] += jnp.sum(
                    g_normed * unit, axis=0, keepdims=True
                )
                got = g_ref[rows, :].astype(f32) + unit_back(g_normed, unit, scaling, gain_two[...])
                gh_ref[pl.ds(c * seq_chunk, seq_chunk)] = got.astype(bf16).reshape(
                    seq_chunk, pos_dev, features
                )
                return carry

            lax.fori_loop(0, tokens // chunk, back_rows, 0)

        pl.run_scoped(
            come_back,
            pltpu.VMEM((experts * cells, tokens), f32),
            pltpu.VMEM((experts, tokens), f32),
        )

    pl.run_scoped(
        mixture,
        pltpu.VMEM((tokens, features), bf16),
        pltpu.VMEM((tokens, features), bf16),
        pltpu.VMEM((tokens, features), bf16),
        pltpu.VMEM((experts * cells, tokens), f32),
        pltpu.VMEM((experts * cells, tokens), bf16),
        pltpu.VMEM((tokens, experts * cells), bf16),
        pltpu.VMEM((experts, tokens), f32),
    )
    dh_x[0].start()

    def sum_first():
        for t in range(2):
            sum_a[t].wait_recv()
            for h in range(narrow):
                if first_kind[t] == "x":
                    total = grad_src[t, h, :, row_x].astype(f32)
                else:
                    total = grad_src[t, h, row_y].astype(f32)
                for k in range(side - 1):
                    total = total + land_a[k, t, h].astype(f32)
                sum_mid[t, h] = total.astype(bf16)
            sum_b[t].start()

    def sum_second():
        for t in range(2):
            place = row_y if second_kind[t] == "y" else row_x
            sum_b[t].wait_recv()
            for h in range(narrow):
                total = sum_mid[t, h, place].astype(f32)
                for k in range(side - 1):
                    total = total + land_b[k, t, h].astype(f32)
                sum_src[t, h] = total.astype(bf16)

    def start_sum_z():
        for t in range(2):
            sum_z[t].start()

    def spread_first():
        for t in range(2):
            sum_z[t].wait_recv()
            full_a[t].start()

    def spread_second():
        for t in range(2):
            full_a[t].wait_recv()
            full_b[t].start()
            full_twin[t][0].start()

    def spread_third():
        for t in range(2):
            full_b[t].wait_recv()
            for e in full_twin[t][1:]:
                e.start()

    def wall_halves(n):
        wall_twin(n).wait_recv()
        total = gw_src[n, :, twin].astype(f32)
        for k in range(twins - 1):
            total = total + gw_twin[k, n].astype(f32)
        gw_half[n] = total.astype(bf16)
        wall_row(n).start()

    def attention(
        x_ref, wall_ref, qkv_ref, att_ref, x_nt, dh_t, gw_acc, dq_acc, dproj_ref, *prob_refs
    ):
        def load(s, n, slot):
            return [
                pltpu.make_async_copy(source.at[s, n], ref.at[slot], prob_sem.at[i, slot])
                for i, (source, ref) in enumerate(zip(prob_ins, prob_refs))
            ]

        loads = [
            pltpu.make_async_copy(source, target, load_sem.at[3 + i])
            for i, (source, target) in enumerate(
                ((x_in, x_ref), (wall_in, wall_ref), (qkv_in, qkv_ref), (att_in, att_ref))
            )
        ]
        for c in loads:
            c.start()
        sum_first()
        for c in loads:
            c.wait()

        def finished(n):
            part = gw_acc[n].astype(bf16)
            gw_src[n] = part.reshape(gw_src.shape[1:])
            wall_twin(n).start()

            @pl.when(n > 0)
            def _():
                wall_halves(n - 1)

        def hooks_of(s):
            steps = {}
            if s == 0:
                steps[0] = (out_x.start,)
                steps[1] = (sum_second, start_sum_z)
            elif s == 1:
                steps[pairs - 2] = (spread_first,)

            def hooks(n):
                if s == seqs - 1:
                    finished(n)
                for at, actions in steps.items():

                    @pl.when(n == at)
                    def _(actions=actions):
                        for action in actions:
                            action()

            return hooks

        def rows_back(s, k):
            j = lax.rem(z + k, narrow)
            rows = rows_of(j, 1, local_len)
            grad = nt(dproj_ref[0, rows, :], wall_of(wall_ref, 0)[:, : 3 * PAIR])
            for n in range(1, pairs):
                grad = grad + nt(dproj_ref[n, rows, :], wall_of(wall_ref, n)[:, : 3 * PAIR])
            unit, scaling = unit_of(x_ref[s, rows, :].astype(f32))
            small_ref[experts + 1 : experts + 2, :] += jnp.sum(grad * unit, axis=0, keepdims=True)
            got = dh_ref[s, rows, :].astype(f32) + unit_back(grad, unit, scaling, gain_one[...])
            gx_ref[s, rows, :] = got.astype(bf16)

        for s in range(seqs):
            for c in load(s, 0, 0):
                c.start()
            unit, _ = unit_of(x_ref[s].astype(f32))
            x_nt[...] = jnp.transpose((unit * gain_one[...]).astype(bf16))
            dh_x[s].wait_recv()
            if s + 1 < seqs:
                dh_x[s + 1].start()
            dh_t[...] = jnp.transpose(dh_ref[s])
            attend_back_pairs(
                block, s, (prob_refs, load), x_nt, dh_ref, dh_t, wall_ref, qkv_ref, att_ref, dq_acc, dproj_ref, gw_acc, hooks_of(s)
            )

            def to_peer(k, carry, s=s):
                rows_back(s, k)
                gx_x[s].copy_of(k).start()
                return carry

            lax.fori_loop(1, narrow, to_peer, 0)
            rows_back(s, 0)
            gx_x[s].kept().start()
            if s == seqs - 1:
                wall_halves(pairs - 1)

    pl.run_scoped(
        attention,
        pltpu.VMEM(x_in.shape, bf16),
        pltpu.VMEM(wall_in.shape, bf16),
        pltpu.VMEM(qkv_in.shape, bf16),
        pltpu.VMEM(att_in.shape, bf16),
        pltpu.VMEM((features, length), bf16),
        pltpu.VMEM((features, length), bf16),
        pltpu.VMEM((pairs, features, 4 * PAIR), f32),
        pltpu.VMEM((PAIR, length), f32),
        pltpu.VMEM((pairs, length, 3 * PAIR), bf16),
        *(pltpu.VMEM((2,) + ref.shape[2:], bf16) for ref in prob_ins),
    )
    small_wide.start()
    total = gw_half[:, row].astype(f32)
    for n in range(pairs):
        wall_row(n).wait_recv()
    for k in range(row_count - 1):
        total = total + gw_row[k].astype(f32)
    gw_z_src[...] = total.astype(bf16)
    wall_z.start()
    small_wide.wait_recv()
    small_w[w] = small_ref[...]
    total = small_w[0]
    for j in range(1, wide):
        total = total + small_w[j]
    small_mid[...] = total
    small_narrow.start()
    spread_second()
    wall_z.wait_recv()
    total = gw_z_src[z].astype(f32)
    for k in range(narrow - 1):
        total = total + gw_z[k].astype(f32)
    gw_last[...] = total.astype(bf16)
    wall_full.start()
    spread_third()
    small_narrow.wait_recv()
    small_z[z] = small_mid[...]
    total = small_z[0]
    for j in range(1, narrow):
        total = total + small_z[j]
    small_out[...] = total
    for e in (mixed_x, gexp_x, eo_x, gm_x, out_x, *sum_a, *sum_b, *sum_z, *dh_x):
        e.wait_send()
    for n in range(pairs):
        wall_twin(n).wait_send()
        wall_row(n).wait_send()
    for e in (wall_z, small_wide, small_narrow, *full_a, *full_b):
        e.wait_send()
    out_x.wait_recv()
    for e in (*gx_x, wall_full, *full_twin[0], *full_twin[1]):
        e.wait_recv()
        e.wait_send()


def backward(x_mix, g_mix, weights, x_seq, wall, qkv, att, probs, key_row, gain_one, gain_two, router, home, sizes):
    narrow, wide, twins = sizes
    seq_total, pos_dev, features = x_mix.shape
    seqs, length, _ = x_seq.shape
    pairs, experts = narrow, router.shape[0]
    row_count = wide // twins
    tokens = seq_total * pos_dev
    side, part_rows, columns = weights.shape[3:]
    wall_rows = features // wide
    cells = pos_dev * key_row[1]
    bases, used = plan(back_kinds(seqs, pairs, math.isqrt(row_count)), sizes)
    dma = pltpu.SemaphoreType.DMA
    rows = (experts * cells, features)
    vm = pltpu.VMEM
    return pl.pallas_call(
        functools.partial(backward_body, sizes, min(256, length), bases),
        out_shape=[
            jax.ShapeDtypeStruct(home, bf16),
            jax.ShapeDtypeStruct(home, bf16),
            jax.ShapeDtypeStruct((narrow, twins, side, side, part_rows, columns), bf16),
            jax.ShapeDtypeStruct((narrow, twins, side, side, part_rows, columns), bf16),
            jax.ShapeDtypeStruct((features, 4 * PAIR), bf16),
            jax.ShapeDtypeStruct((2 * experts, features), f32),
        ],
        in_specs=[whole(pl.ANY)] * 7 + [whole()] * 4 + [whole(pl.ANY)] * len(probs),
        out_specs=[whole(pl.ANY)] * 5 + [whole()],
        scratch_shapes=[vm(rows, bf16)] * 8
        + [
            vm(weights.shape, bf16),
            vm((side - 1, 2, narrow, side, part_rows, columns), bf16),
            vm((2, narrow, side, part_rows, columns), bf16),
            vm((side - 1, 2, narrow, part_rows, columns), bf16),
            vm((2, narrow, part_rows, columns), bf16),
            vm(x_mix.shape, bf16),
            vm(x_mix.shape, bf16),
            vm(x_seq.shape, bf16),
            vm(x_seq.shape, bf16),
            vm((pairs, row_count, twins, wall_rows, 4 * PAIR), bf16),
            vm((twins - 1, pairs, row_count, wall_rows, 4 * PAIR), bf16),
            vm((pairs, row_count, wall_rows, 4 * PAIR), bf16),
            vm((row_count - 1, pairs, wall_rows, 4 * PAIR), bf16),
            vm((pairs, wall_rows, 4 * PAIR), bf16),
            vm((narrow - 1, wall_rows, 4 * PAIR), bf16),
            vm((wall_rows, 4 * PAIR), bf16),
            vm((2 * experts, features), f32),
            vm((wide, 2 * experts, features), f32),
            vm((2 * experts, features), f32),
            vm((narrow, 2 * experts, features), f32),
            dma((used,)),
            dma((used,)),
            dma((8 + 2 * seqs,)),
            dma((7,)),
            dma((len(probs), 2)),
        ],
        compiler_params=pltpu.CompilerParams(
            collective_id=2, has_side_effects=True, vmem_limit_bytes=VMEM_LIMIT
        ),
    )(
        x_mix.reshape(tokens, features),
        g_mix.reshape(tokens, features),
        weights,
        x_seq,
        wall,
        qkv,
        att,
        key_row[0],
        gain_one,
        gain_two,
        router,
        *probs,
    )


def widen_body(*refs):
    half = len(refs) // 2
    for source, target in zip(refs[:half], refs[half:]):
        target[...] = source[...].astype(f32)


def widen(arrays, steps):
    flat = [a.reshape(steps, -1, a.shape[-1]) for a in arrays]
    specs = [pl.BlockSpec((1,) + a.shape[1:], lambda i: (i, 0, 0)) for a in flat]
    wide = pl.pallas_call(
        widen_body,
        grid=(steps,),
        out_shape=[jax.ShapeDtypeStruct(a.shape, f32) for a in flat],
        in_specs=specs,
        out_specs=specs,
        compiler_params=pltpu.CompilerParams(vmem_limit_bytes=VMEM_LIMIT),
    )(*flat)
    return [b.reshape(a.shape) for a, b in zip(arrays, wide)]


def per_device(
    inputs,
    positions,
    members_index,
    members_mask,
    gain_attn,
    input_projection_weight,
    output_projection_weight,
    gain_mixer,
    weight_router,
    weight_up,
    weight_down,
    cotangent,
):
    narrow, wide = lax.axis_size("narrow"), lax.axis_size("wide")
    w, z = lax.axis_index("wide"), lax.axis_index("narrow")
    seq_dev, local_len, features = inputs.shape
    length = positions.shape[1]
    groups = members_index.shape[1]
    experts = weight_up.shape[0]
    own_seqs = seq_dev // narrow
    pos_dev = local_len // wide
    seq_total = seq_dev * wide
    sizes = (narrow, wide, experts // narrow)

    offset_rows = w * pos_dev
    index_rows = lax.dynamic_slice_in_dim(members_index, offset_rows, pos_dev, 0)
    live = lax.dynamic_slice_in_dim(members_mask, offset_rows, pos_dev, 0) > 0
    named = (
        index_rows[..., None] == jnp.arange(seq_total, dtype=jnp.int32)[None, None, None, :]
    ) & live[..., None]
    group_of = jnp.max(
        jnp.where(named, jnp.arange(groups, dtype=jnp.int32)[None, :, None, None], 0), axis=(1, 2)
    )
    key_row = group_of + groups * jnp.arange(pos_dev, dtype=jnp.int32)[:, None]
    key_row = jnp.transpose(key_row).reshape(1, seq_total * pos_dev)

    gain_one, gain_two = gain_attn.reshape(1, features), gain_mixer.reshape(1, features)
    router = jnp.transpose(weight_router)
    x_mix, g_mix, weights, x_seq, wall, qkv, att, *probs = forward(
        inputs,
        cotangent,
        weight_up,
        weight_down,
        jnp.transpose(input_projection_weight, (1, 0, 2)),
        output_projection_weight,
        positions,
        gain_one,
        sizes,
    )
    outputs, gx, full_up, full_down, g_wall, small = backward(
        x_mix,
        g_mix,
        weights,
        x_seq,
        wall,
        qkv,
        att,
        probs,
        (key_row, groups),
        gain_one,
        gain_two,
        router,
        inputs.shape,
        sizes,
    )
    g_up, g_down, gx = widen(
        [full_up.reshape(weight_up.shape), full_down.reshape(weight_down.shape), gx], 4
    )
    g_wall = g_wall.astype(f32)
    return (
        outputs,
        gx,
        small[experts + 1],
        g_wall[:, : 3 * PAIR].reshape(input_projection_weight.shape),
        jnp.transpose(g_wall[:, 3 * PAIR :]),
        small[experts],
        jnp.transpose(small[:experts]),
        g_up,
        g_down,
    )


def solution(mesh):
    in_specs = (
        P("wide", "narrow", None),
        P("wide", None),
        P("narrow", None, None),
        P("narrow", None, None),
        P(),
        P(None, None, "narrow"),
        P("narrow", None),
        P(),
        P(),
        P(None, None, "narrow"),
        P(None, "narrow", None),
        P("wide", "narrow", None),
    )
    out_specs = (
        P("wide", "narrow", None),
        P("wide", "narrow", None),
        P(),
        P(None, None, "narrow"),
        P("narrow", None),
        P(),
        P(),
        P(None, None, "narrow"),
        P(None, "narrow", None),
    )
    return jax.shard_map(
        per_device, mesh=mesh, in_specs=in_specs, out_specs=out_specs, check_vma=False
    )
```
